32 devices in a mesh: grp: 2 (over y), gx: 4 (over z), gy: 2 (over x), sa: 2 (over core).
Axes of the slice: x: 2, y: 2, z: 4, core: 2. Of those that a mesh axis runs over, the one named last changes fastest.
Arguments:
- initial: float32 [6, 16, 64, 512], P('grp', None, 'gx', ('gy', 'sa')), parts along dimension 0, may hold values from 0 to 1
- logk: float32 [32, 64, 512], P('grp', 'gx', ('gy', 'sa')), parts along dimension 0, may hold values from -1 to 1
- direction: float32 [32, 64, 512], P('grp', 'gx', ('gy', 'sa')), parts along dimension 0, may hold values from -4 to 4
- face_speed: float32 [4, 16, 64, 512], P('grp', None, 'gx', ('gy', 'sa')), parts along dimension 0, may hold values from 0.04 to 0.16
- face_flags: int32 [4, 16, 64, 512], P('grp', None, 'gx', ('gy', 'sa')), parts along dimension 0, may hold values 0 or 1
- retard: float32 [3], replicated, may hold values from 1 to 3
- decay: float32 [3], replicated, may hold values from 0.05 to 0.7
- screen_cells: int32 [768, 32], P('grp'), parts along dimension 0, may hold values from 0 to 524287, as said below
- screen_count: int32 [768], P('grp'), parts along dimension 0, may hold values from 1 to 32, as said below
- well_weight: float32 [6, 384], P('grp'), parts along dimension 0, may hold values from 2000 to 32000
Outputs:
- hessian: float32 [32, 64, 512], P('grp', 'gx', ('gy', 'sa')), parts along dimension 0
The draws below stay inside these ranges and needn't reach their ends.
There are 2 independent parts, one for each index of `grp`. The reference program is written for one: setup_inputs(seed, part) draws one part's arguments, and reference() takes and returns one part's arrays. A program takes and returns all parts, laid end to end along the dimension named above; an argument that names none is the same for every part. Nothing has to cross between parts.
Inputs may be any that keep to these rules, and one draw needn't show every extreme that they name: `screen_cells`: each well's 32 entries are cells in a row along x at one z and one y, flat index z * 64 * 512 + x * 512 + y; only the first screen_count entries of a well are used. `screen_count`: some well uses all 32 entries.
All inputs are finite; a program needn't handle non-finite values. No bound on the sum of `face_flags` on one device may be relied on, other than what follows from the above.
Results may differ from the reference program's by a relative error of at most 0.00002.
Values sent between devices are 32-bit elements; how exact they have to be, the bound alone decides.
No kernel may reach another device: no remote copies, remote signals or barrier semaphores. Data moves between devices by JAX's collectives and lax.ppermute only.
A program may use at most 128 MiB of HBM per device.

```python
import math
import jax
import jax.numpy as jnp
from jax import lax

S = 3
NZ = 16
STEPS = 4
WELLS = 384
SCREEN = 32
NX = 64
NY = 512


def draw_screen_cells(key, part):
    key = jax.random.fold_in(key, 11)
    key_x, key_y, key_z = jax.random.split(key, 3)
    start_x = jax.random.randint(key_x, (WELLS, 1), 0, NX - SCREEN + 1)
    start_y = jax.random.randint(key_y, (WELLS, 1), 0, NY)
    start_z = jax.random.randint(key_z, (WELLS, 1), 0, NZ)
    offsets = jnp.arange(SCREEN, dtype=jnp.int32)[None, :]
    return (start_z * (NX * NY) + (start_x + offsets) * NY + start_y).astype(jnp.int32)


def draw_screen_count(key, part):
    key = jax.random.fold_in(key, 12)
    counts = jax.random.randint(key, (WELLS,), 1, SCREEN + 1)
    return counts.at[0].set(SCREEN).astype(jnp.int32)


def plant(array, rng, least, high):
    dims = array.shape
    place = [jax.random.randint(jax.random.fold_in(rng, axis), (), 0, dims[axis]) for axis in range(len(dims))]
    array = array.at[tuple(place)].set(least)
    longest = dims.index(max(dims))
    place[longest] = (place[longest] + 1) % dims[longest]
    return array.at[tuple(place)].set(high)


def block_scale(own_key, dims, cuts, smallest, high):
    factor_of = 1.0
    for position, shards_of in cuts:
        heights = jax.random.uniform(jax.random.fold_in(jax.random.fold_in(own_key, 6), position), (shards_of,), jnp.float32, smallest / len(cuts), high / len(cuts))
        factor_of = factor_of * jnp.repeat(jnp.exp(heights), dims[position] // shards_of).reshape((-1,) + (1,) * (len(dims) - 1 - position))
    return factor_of


def scatter_about(rng, extent, spread, reach, cuts=(), held_as=jnp.bfloat16):
    factor_of = block_scale(rng, extent, cuts, -0.22, 0.18) if cuts else 1.0
    values = jax.random.normal(rng, extent, jnp.float32) * spread * factor_of
    return jnp.minimum(jnp.maximum(values, -reach), reach).astype(held_as)


def setup_inputs(seed: int = 0, part: int = 0) -> dict:
    splits = jax.random.split(jax.random.key(seed), 11)
    part_splits = jax.random.split(jax.random.fold_in(splits[10], part), 11)
    return {
        "initial": jnp.clip(1.0 * jax.random.uniform(part_splits[0], (S, NZ, NX, NY), jnp.float32) ** block_scale(part_splits[0], (S, NZ, NX, NY), ((2, 4), (3, 4)), -0.2, 0.2), 0.0, 1.0),
        "logk": jnp.clip(jax.random.uniform(part_splits[1], (NZ, NX, NY), jnp.float32, -1.0, 1.0) * block_scale(part_splits[1], (NZ, NX, NY), ((1, 4), (2, 4)), -0.4, 0.0), -1.0, 1.0),
        "direction": scatter_about(part_splits[2], (NZ, NX, NY), 1.0, 4.0, ((1, 4), (2, 4)), jnp.float32),
        "face_speed": jnp.clip(jnp.exp(math.log(0.16) - 1.3862944 * jax.random.uniform(part_splits[3], (2, NZ, NX, NY), jnp.float32) ** block_scale(part_splits[3], (2, NZ, NX, NY), ((2, 4), (3, 4)), -0.2, 0.2)), 0.04, 0.16),
        "face_flags": plant((jax.random.randint(part_splits[4], (2, NZ, NX, NY), 0, 2) < 1).astype(jnp.int32), jax.random.fold_in(part_splits[4], 1), 0, 1),
        "retard": jnp.clip(jax.random.uniform(splits[5], (S,), jnp.float32, 1.0, 3.0), 1.0, 3.0),
        "decay": jnp.clip(jnp.exp(jax.random.uniform(splits[6], (S,), jnp.float32, math.log(0.05), math.log(0.7))), 0.05, 0.7),
        "screen_cells": draw_screen_cells(jax.random.fold_in(jax.random.fold_in(splits[10], part), 71), part),
        "screen_count": draw_screen_count(jax.random.fold_in(jax.random.fold_in(splits[10], part), 71), part),
        "well_weight": jnp.clip(jnp.exp(jax.random.uniform(part_splits[9], (S, WELLS), jnp.float32, math.log(2000.0), math.log(32000.0))), 2000.0, 32000.0),
    }


TIME_STEP = 0.05
VERTICAL_RATE = 0.02

def divergence(flux_rows, flux_cols):
    zero_rows = jnp.zeros(flux_rows.shape[:-2] + (1, flux_rows.shape[-1]), flux_rows.dtype)
    zero_cols = jnp.zeros(flux_cols.shape[:-1] + (1,), flux_cols.dtype)
    along_rows = jnp.concatenate([zero_rows, flux_rows], -2) - jnp.concatenate([flux_rows, zero_rows], -2)
    along_cols = jnp.concatenate([zero_cols, flux_cols], -1) - jnp.concatenate([flux_cols, zero_cols], -1)
    return along_rows + along_cols

def vertical(current):
    jump = current[:, 1:] - current[:, :-1]
    zero_layer = jnp.zeros_like(current[:, :1])
    return VERTICAL_RATE * (jnp.concatenate([jump, zero_layer], 1) - jnp.concatenate([zero_layer, jump], 1))

def transport(current, conductance, speed_rows, speed_cols):
    cond_rows = 0.5 * TIME_STEP * (conductance[:, :-1, :] + conductance[:, 1:, :])
    low_side = current[..., :-1, :]
    high_side = current[..., 1:, :]
    flux_rows = cond_rows * (low_side - high_side) + jnp.maximum(speed_rows[:, :-1, :], 0.0) * low_side + jnp.minimum(speed_rows[:, :-1, :], 0.0) * high_side
    cond_cols = 0.5 * TIME_STEP * (conductance[..., :-1] + conductance[..., 1:])
    low_side = current[..., :-1]
    high_side = current[..., 1:]
    flux_cols = cond_cols * (low_side - high_side) + jnp.maximum(speed_cols[..., :-1], 0.0) * low_side + jnp.minimum(speed_cols[..., :-1], 0.0) * high_side
    return divergence(flux_rows, flux_cols) + vertical(current)

def reference(initial, logk, direction, face_speed, face_flags, retard, decay, screen_cells, screen_count, well_weight):
    signed = jnp.where(face_flags == 1, face_speed, -face_speed)
    decay_factor = jnp.exp(-decay)[:, None, None, None]
    retarding = retard[:, None, None, None]
    active = (jnp.arange(SCREEN)[None, :] < screen_count[:, None]).astype(initial.dtype)
    counts = screen_count.astype(initial.dtype)

    def observe(field):
        current = initial
        conductance = jnp.exp(field)
        for moment in range(STEPS):
            current = decay_factor * (current + transport(current, conductance, signed[0], signed[1]) / retarding)
        values = current.reshape(current.shape[0], -1)[:, screen_cells]
        return lax.optimization_barrier(jnp.sum(values * active, -1)) / counts
    _, tangent = jax.jvp(observe, (logk,), (direction,))
    _, pullback = jax.vjp(observe, logk)
    return pullback(well_weight * tangent)[0]
```

```python
import functools

import jax
import jax.numpy as jnp
from jax import lax
from jax.experimental import pallas as pl
from jax.experimental.pallas import tpu as pltpu
from jax.sharding import PartitionSpec as P

STEPS = 4
HALO = STEPS
RATE = 0.02
HALF_DT = 0.025
LANES = 128
GROUP = 16
RIGHT = 64
Y = ("gy", "sa")
VMEM_LIMIT = 40 * 1024 * 1024


def lane_of(shape):
    return lax.broadcasted_iota(jnp.int32, shape, len(shape) - 1)


def roll(value, shift, axis):
    return pltpu.roll(value, shift % value.shape[axis], axis)


def pack_edges(fields):
    lane = lane_of(fields[0].shape)
    packed = jnp.zeros_like(fields[0])
    for f, field in enumerate(fields):
        packed = jnp.where(lane // GROUP == f, roll(field, 8 + GROUP * f, 1), packed)
    return packed


def y_neighbours(value, strip, s):
    lane = lane_of(value.shape)
    after = jnp.where(lane == LANES - 1, roll(strip, 127 - (RIGHT + GROUP * s + 8), 1), roll(value, 127, 1))
    before = jnp.where(lane == 0, roll(strip, -(GROUP * s + 7), 1), roll(value, 1, 1))
    return after, before


def y_before(value, strip):
    return jnp.where(lane_of(value.shape) == 0, roll(strip, -7, 1), roll(value, 1, 1))


def y_after(value, strip, s):
    lane = lane_of(value.shape)
    return jnp.where(lane == LANES - 1, roll(strip, 127 - (RIGHT + GROUP * s + 8), 1), roll(value, 127, 1))


def z_pair(value):
    layers = value.shape[0]
    depth = lax.broadcasted_iota(jnp.int32, value.shape, 0)
    above = jnp.where(depth == layers - 1, value, roll(value, layers - 1, 0))
    below = jnp.where(depth == 0, value, roll(value, 1, 0))
    return above + below


def strip_retard(retard_ref, shape):
    place = lane_of(shape) % RIGHT // GROUP
    return jnp.where(place == 0, retard_ref[0], jnp.where(place == 1, retard_ref[1], retard_ref[2]))


def pack_kernel(initial_ref, logk_ref, direction_ref, speed_ref, flags_ref, f7_ref, e_ref, xa_ref, xb_ref, *, layers, width, species):
    plane = layers * width
    even = lax.rem(lax.axis_index("gx"), 2) == 0
    top, bottom = width - HALO, 0

    def row(x, carry):
        def take(ref, index):
            return ref[pl.ds(index * plane + x, layers, stride=width), :]

        fields = [take(initial_ref, s) for s in range(species)]
        conductance = jnp.exp(take(logk_ref, 0))
        fields += [conductance, conductance * take(direction_ref, 0)]
        for axis in range(2):
            speed = take(speed_ref, axis)
            fields.append(jnp.where(take(flags_ref, axis) == 1, speed, -speed))
        for f, field in enumerate(fields):
            f7_ref[x, f] = field
        e_ref[x] = pack_edges(fields)
        return carry

    lax.fori_loop(0, width, row, 0)
    count = species + 4
    start_a = jnp.where(even, top, bottom)
    start_b = jnp.where(even, bottom, top)
    for r in range(HALO):
        xa_ref[r, 0:count] = f7_ref[start_a + r]
        xb_ref[r, 0:count] = f7_ref[start_b + r]


def pack(initial, logk, direction, face_speed, face_flags):
    species, layers, width, _ = initial.shape
    flat = lambda a: a.reshape(-1, LANES)
    f32 = jnp.float32
    return pl.pallas_call(
        functools.partial(pack_kernel, layers=layers, width=width, species=species),
        out_shape=(
            jax.ShapeDtypeStruct((width, species + 4, layers, LANES), f32),
            jax.ShapeDtypeStruct((width, layers, LANES), f32),
            jax.ShapeDtypeStruct((HALO, species + 5, layers, LANES), f32),
            jax.ShapeDtypeStruct((HALO, species + 5, layers, LANES), f32),
        ),
        in_specs=[pl.BlockSpec(memory_space=pltpu.VMEM)] * 5,
        out_specs=[pl.BlockSpec(memory_space=pltpu.VMEM)] * 4,
        name="pack",
    )(flat(initial), flat(logk), flat(direction), flat(face_speed), flat(face_flags))


def strips_kernel(ea_ref, eb_ref, xa_in, xb_in, xa_ref, xb_ref, buf_a, buf_b, sem_a, sem_b, *, width, count):
    even_x = lax.rem(lax.axis_index("gx"), 2) == 0
    even_y = lax.rem(lax.axis_index(Y), 2) == 0
    start_a = jnp.where(even_x, width - HALO, 0)
    start_b = jnp.where(even_x, 0, width - HALO)
    for r in range(HALO):
        for start, buf in ((start_a, buf_a), (start_b, buf_b)):
            one, two = ea_ref[start + r], eb_ref[start + r]
            from_left = lane_of(one.shape) % GROUP < 8
            buf[r] = jnp.where(from_left == even_y, two, one)
    copies = [
        pltpu.make_async_copy(buf_a, xa_ref.at[:, count], sem_a),
        pltpu.make_async_copy(buf_b, xb_ref.at[:, count], sem_b),
    ]
    for copy in copies:
        copy.start()
    for copy in copies:
        copy.wait()


def add_strips(ea, eb, xa, xb):
    width, layers, _ = ea.shape
    buffer = pltpu.VMEM((HALO, layers, LANES), jnp.float32)
    return pl.pallas_call(
        functools.partial(strips_kernel, width=width, count=xa.shape[1] - 1),
        out_shape=(jax.ShapeDtypeStruct(xa.shape, xa.dtype), jax.ShapeDtypeStruct(xb.shape, xb.dtype)),
        in_specs=[pl.BlockSpec(memory_space=pltpu.VMEM)] * 2 + [pl.BlockSpec(memory_space=pl.ANY)] * 2,
        out_specs=[pl.BlockSpec(memory_space=pl.ANY)] * 2,
        input_output_aliases={2: 0, 3: 1},
        scratch_shapes=[buffer, buffer, pltpu.SemaphoreType.DMA, pltpu.SemaphoreType.DMA],
        name="corner_strips",
    )(ea, eb, xa, xb)


def well_rows(meta_ref):
    return [meta_ref[i : i + 1, :] for i in range(4)]


def forward_kernel(
    retard_ref, f7_ref, e_ref, ea_ref, eb_ref, xa_ref, xb_ref, meta_ref,
    partial_ref, px_ref, qx_ref, py_ref, qym_ref, d_ref, c_ref, jy_ref,
    k_ref, kd_ref, ux_ref, uy_ref, qy_ref, pym_ref, bx_ref, by_ref, bym_ref, t_ref, wide_ref,
    *, layers, width, species,
):
    f32 = jnp.float32
    rows = width + 2 * HALO
    shape = (layers, LANES)
    lane = lane_of(shape)
    gx, gy = lax.axis_index("gx"), lax.axis_index(Y)
    even_x, even_y = lax.rem(gx, 2) == 0, lax.rem(gy, 2) == 0
    total_x = width * lax.axis_size("gx")
    first_y, last_y = gy == 0, gy == lax.axis_size(Y) - 1
    column = lane % GROUP
    near = column < 8
    left = lane < RIGHT
    count = species + 4

    def place(r, fields, own_edges, outer_edges):
        left_strip = jnp.where(near, outer_edges, own_edges)
        right_strip = jnp.where(near, own_edges, outer_edges)
        for s in range(species):
            c_ref[0, r, s] = fields[s]
        c_ref[0, r, species] = jnp.where(left, left_strip, roll(right_strip, RIGHT, 1))
        for f, ref in enumerate((k_ref, kd_ref, ux_ref, uy_ref), species):
            ref[r, 0] = fields[f]
            index = GROUP * f + column
            ref[r, 1] = jnp.where(
                left,
                jnp.take_along_axis(left_strip, index, 1, mode="promise_in_bounds"),
                jnp.take_along_axis(right_strip, index, 1, mode="promise_in_bounds"),
            )

    def own_row(x, carry):
        one, two = ea_ref[x], eb_ref[x]
        outer = jnp.where(near == even_y, two, one)
        place(x + HALO, [f7_ref[x, f] for f in range(count)], e_ref[x], outer)
        return carry

    lax.fori_loop(0, width, own_row, 0)

    def halo_row(r, carry):
        for low in (True, False):
            from_a = even_x != low
            both = [jnp.where(from_a, xa_ref[r, f], xb_ref[r, f]) for f in range(count + 1)]
            place(r if low else r + HALO + width, both[:count], pack_edges(both[:count]), both[count])
        return carry

    lax.fori_loop(0, HALO, halo_row, 0)

    strip_mask = jnp.where(
        left, jnp.where(first_y & near, 0.0, 1.0), jnp.where(last_y & (column >= 7), 0.0, 1.0)
    ).astype(f32)
    main_mask = jnp.where(last_y & (lane == LANES - 1), 0.0, 1.0).astype(f32)

    def y_faces(r, carry):
        k4, kd4, u4 = k_ref[r, 1], kd_ref[r, 1], uy_ref[r, 1]
        half4 = HALF_DT * (k4 + roll(k4, 127, 1))
        p4 = (half4 + jnp.maximum(u4, 0.0)) * strip_mask
        q4 = (half4 - jnp.minimum(u4, 0.0)) * strip_mask
        b4 = HALF_DT * (kd4 + roll(kd4, 127, 1)) * strip_mask
        k, kd, u = k_ref[r, 0], kd_ref[r, 0], uy_ref[r, 0]
        half = HALF_DT * (k + y_after(k, k4, 0))
        p = (half + jnp.maximum(u, 0.0)) * main_mask
        q = (half - jnp.minimum(u, 0.0)) * main_mask
        b = HALF_DT * (kd + y_after(kd, kd4, 0)) * main_mask
        py_ref[r, 0], py_ref[r, 1] = p, p4
        qy_ref[r, 0], qy_ref[r, 1] = q, q4
        by_ref[r, 0], by_ref[r, 1] = b, b4
        qm, qm4 = y_before(q, q4), roll(q4, 1, 1)
        pym_ref[r, 0], pym_ref[r, 1] = y_before(p, p4), roll(p4, 1, 1)
        qym_ref[r, 0], qym_ref[r, 1] = qm, qm4
        bym_ref[r, 0], bym_ref[r, 1] = y_before(b, b4), roll(b4, 1, 1)
        d_ref[r, 0], d_ref[r, 1] = p + qm + 2 * RATE, p4 + qm4 + 2 * RATE
        return carry

    lax.fori_loop(0, rows, y_faces, 0)

    def x_faces(r, carry):
        x = gx * width + r - HALO
        mask = jnp.where((x >= 0) & (x + 1 < total_x), 1.0, 0.0).astype(f32)
        for i in range(2):
            u = ux_ref[r, i]
            half = HALF_DT * (k_ref[r, i] + k_ref[r + 1, i])
            p = (half + jnp.maximum(u, 0.0)) * mask
            q = (half - jnp.minimum(u, 0.0)) * mask
            px_ref[r, i] = p
            qx_ref[r, i] = q
            bx_ref[r, i] = HALF_DT * (kd_ref[r, i] + kd_ref[r + 1, i]) * mask
            d_ref[r, i] = d_ref[r, i] + p
            d_ref[r + 1, i] = d_ref[r + 1, i] + q
        return carry

    lax.fori_loop(0, rows - 1, x_faces, 0)

    strip_rate = strip_retard(retard_ref, shape)
    for m in range(STEPS):
        now, later = m % 2, (m + 1) % 2

        def step_row(r, carry, m=m, now=now, later=later):
            for s in (species,) + tuple(range(species)):
                i = 1 if s == species else 0
                rate = strip_rate if i else retard_ref[s]
                kept = rate - d_ref[r, i]
                upper, lower = qx_ref[r, i], px_ref[r - 1, i]
                after, before = qy_ref[r, i], pym_ref[r, i]

                def around(ref, slot):
                    value, strip = ref[slot, r, s], ref[slot, r, species]
                    if i:
                        return value, roll(value, 127, 1), roll(value, 1, 1)
                    return (value,) + y_neighbours(value, strip, s)

                def moved(ref, slot, value, yp, ym):
                    return (
                        kept * value
                        + upper * ref[slot, r + 1, s]
                        + lower * ref[slot, r - 1, s]
                        + after * yp
                        + before * ym
                        + RATE * z_pair(value)
                    )

                c, yp, ym = around(c_ref, m)
                jump = yp - c
                source = (
                    bx_ref[r, i] * (c_ref[m, r + 1, s] - c)
                    - bx_ref[r - 1, i] * (c - c_ref[m, r - 1, s])
                    + by_ref[r, i] * jump
                    - bym_ref[r, i] * (c - ym)
                )
                jy_ref[m, r, s] = jump
                if m + 1 < STEPS:
                    c_ref[m + 1, r, s] = moved(c_ref, m, c, yp, ym)
                if m > 0:
                    t, tp, tm = around(t_ref, now)
                    source = source + moved(t_ref, now, t, tp, tm)
                t_ref[later, r, s] = source
            return carry

        lax.fori_loop(m + 1, rows - 1 - m, step_row, 0)

    final = STEPS % 2
    depth, first, last, where_y = well_rows(meta_ref)
    wells = meta_ref.shape[1]
    own = lax.broadcasted_iota(jnp.int32, (LANES, wells), 0)
    own_hot = jnp.where(own == where_y, 1.0, 0.0).astype(jnp.bfloat16)
    strip_place = own % RIGHT // GROUP
    strip_col = own % GROUP + jnp.where(own < RIGHT, -8, 120)
    outside = (strip_col < 0) | (strip_col >= LANES)
    strip_hit = outside & (strip_col == where_y)
    for x in range(width):
        wide_ref[x, 0] = t_ref[final, x + HALO, species]
    layer = lax.broadcasted_iota(jnp.int32, (layers, wells), 0)
    in_layer = layer == depth
    for s in range(species):
        hot = jnp.concatenate(
            [own_hot, jnp.where(strip_hit & (strip_place == s), 1.0, 0.0).astype(jnp.bfloat16)], axis=0
        )
        total = jnp.zeros((layers, wells), f32)
        for part in range(2):
            half = width // 2
            main = t_ref[final, HALO + part * half : HALO + (part + 1) * half, s].reshape(half * layers, LANES)
            side = t_ref[final, HALO + part * half : HALO + (part + 1) * half, species].reshape(half * layers, LANES)
            both = jnp.concatenate([main, side], axis=1)
            picked = jnp.zeros((half * layers, wells), f32)
            for piece in range(3):
                coarse = both.astype(jnp.bfloat16)
                picked = picked + jnp.dot(coarse, hot, preferred_element_type=f32)
                both = both - coarse.astype(f32)
            picked = picked.reshape(half, layers, wells)
            for x in range(half):
                at = x + part * half
                inside = (first <= at) & (last >= at)
                total = total + jnp.where(inside & in_layer, picked[x], 0.0)
        partial_ref[s : s + 1, :] = jnp.sum(total, axis=0, keepdims=True)


def forward(retard, f7, e, ea, eb, xa, xb, meta):
    width, count, layers, _ = f7.shape
    species = count - 4
    rows = width + 2 * HALO
    f32 = jnp.float32
    coef = (rows, 2, layers, LANES)
    state = (rows, species + 1, layers, LANES)
    vmem = pl.BlockSpec(memory_space=pltpu.VMEM)
    return pl.pallas_call(
        functools.partial(forward_kernel, layers=layers, width=width, species=species),
        out_shape=(jax.ShapeDtypeStruct((species, meta.shape[1]), f32),)
        + (jax.ShapeDtypeStruct(coef, f32),) * 5
        + (jax.ShapeDtypeStruct((STEPS,) + state, f32),) * 2,
        in_specs=[pl.BlockSpec(memory_space=pltpu.SMEM)] + [vmem] * 7,
        out_specs=[vmem] * 8,
        scratch_shapes=[pltpu.VMEM(coef, f32)] * 9
        + [pltpu.VMEM((2,) + state, f32), pltpu.VMEM((width, 1, layers, LANES), f32)],
        compiler_params=pltpu.CompilerParams(vmem_limit_bytes=VMEM_LIMIT),
        name="forward_steps",
    )(retard, f7, e, ea, eb, xa, xb, meta)


def adjoint_kernel(
    retard_ref, decay_ref, weight_ref, meta_ref, px_ref, qx_ref, py_ref, qym_ref, d_ref, c_ref, jy_ref, f7_ref,
    partial_ref, *rest, layers, width, species, parts,
):
    others, out_ref, lam_ref, hx_ref, hy_ref, mask_ref = rest[:parts], *rest[parts:]
    f32, bf16 = jnp.float32, jnp.bfloat16
    rows = width + 2 * HALO
    shape = (layers, LANES)
    lane = lane_of(shape)
    gx, gy = lax.axis_index("gx"), lax.axis_index(Y)
    total_x = width * lax.axis_size("gx")
    depth, first, last, where_y = well_rows(meta_ref)
    wells = meta_ref.shape[1]

    layer = lax.broadcasted_iota(jnp.int32, (layers, wells), 0)
    in_layer = layer == depth
    for r in range(rows):
        x = r - HALO
        inside = (first <= x) & (last >= x) & in_layer
        mask_ref[r * layers : (r + 1) * layers, :] = jnp.where(inside, 1.0, 0.0).astype(bf16)

    counts = meta_ref[4:5, :].astype(f32)
    own = lax.broadcasted_iota(jnp.int32, (LANES, wells), 0)
    strip_place = own % RIGHT // GROUP
    strip_col = own % GROUP + jnp.where(own < RIGHT, -8, 120)
    strip_hit = strip_col == where_y
    own_hit = own == where_y
    targets = [own_hit] * species
    residuals = []
    for s in range(species):
        total = partial_ref[s : s + 1, :]
        for other in others:
            total = total + other[s : s + 1, :]
        rate = jnp.full((1, wells), retard_ref[s], f32)
        factor = jnp.exp(jnp.full((1, wells), -decay_ref[s], f32)) / rate
        factor = factor * factor
        factor = factor * factor
        residual = weight_ref[s : s + 1, :] * (total * factor) / counts
        residuals.append(residual / counts * factor)
    lam = jnp.zeros((rows * layers, (species + 1) * LANES), f32)
    for piece in range(3):
        coarse = [r.astype(bf16).astype(f32) for r in residuals]
        residuals = [r - q for r, q in zip(residuals, coarse)]
        blocks = [jnp.where(own_hit, q, 0.0).astype(bf16) for q in coarse]
        side = jnp.zeros((LANES, wells), f32)
        for s in range(species):
            side = jnp.where(strip_hit & (strip_place == s), coarse[s], side)
        spread = jnp.concatenate(blocks + [side.astype(bf16)], axis=0)
        lam = lam + lax.dot_general(
            mask_ref[...], spread, (((1,), (1,)), ((), ())), preferred_element_type=f32
        )
    for s in range(species + 1):
        lam_ref[0, :, s] = lam[:, s * LANES : (s + 1) * LANES].reshape(rows, layers, LANES)

    strip_rate = strip_retard(retard_ref, shape)
    for m in reversed(range(STEPS)):
        now, later = (STEPS - 1 - m) % 2, (STEPS - m) % 2
        low, high = STEPS - m, rows - (STEPS - m)

        def retreat_row(r, carry, m=m, now=now, later=later):
            for s in range(species + 1):
                i = 1 if s == species else 0
                value = lam_ref[now, r, s]
                if i:
                    yp, ym = roll(value, 127, 1), roll(value, 1, 1)
                else:
                    yp, ym = y_neighbours(value, lam_ref[now, r, species], s)
                rate = strip_rate if i else retard_ref[s]
                lam_ref[later, r, s] = (
                    (rate - d_ref[r, i]) * value
                    + px_ref[r, i] * lam_ref[now, r + 1, s]
                    + qx_ref[r - 1, i] * lam_ref[now, r - 1, s]
                    + py_ref[r, i] * yp
                    + qym_ref[r, i] * ym
                    + RATE * z_pair(value)
                )
            return carry

        def sense_row(r, carry, m=m, now=now):
            along_x = jnp.zeros(shape, f32)
            along_y = jnp.zeros(shape, f32)
            for s in range(species):
                value = lam_ref[now, r, s]
                along_x += (c_ref[m, r + 1, s] - c_ref[m, r, s]) * (lam_ref[now, r + 1, s] - value)
                along_y += jy_ref[m, r, s] * (y_after(value, lam_ref[now, r, species], s) - value)
            strip = lam_ref[now, r, species]
            side = jy_ref[m, r, species] * (roll(strip, 127, 1) - strip)
            if m + 1 < STEPS:
                along_x += hx_ref[r]
                along_y += hy_ref[r, 0]
                side += hy_ref[r, 1]
            hx_ref[r] = along_x
            hy_ref[r, 0] = along_y
            hy_ref[r, 1] = side
            return carry

        lax.fori_loop(HALO - 1, HALO + width, sense_row, 0)
        if m > 0:
            lax.fori_loop(low, high, retreat_row, 0)

    main_mask = jnp.where((gy == lax.axis_size(Y) - 1) & (lane == LANES - 1), 0.0, 1.0).astype(f32)
    side_mask = jnp.where((gy == 0) & (lane == 0), 0.0, 1.0).astype(f32)

    def finish(x, carry):
        r = x + HALO
        at = gx * width + x
        lower = jnp.where(at > 0, 1.0, 0.0).astype(f32)
        upper = jnp.where(at + 1 < total_x, 1.0, 0.0).astype(f32)
        along_y, strip = hy_ref[r, 0] * main_mask, hy_ref[r, 1]
        side = roll(strip, -7, 1)
        for s in range(1, species):
            side = side + roll(strip, -(GROUP * s + 7), 1)
        before = jnp.where(lane == 0, side * side_mask, roll(along_y, 1, 1))
        total = hx_ref[r] * upper + hx_ref[r - 1] * lower + along_y + before
        out_ref[pl.ds(x, layers, stride=width), :] = -HALF_DT * f7_ref[x, species] * total
        return carry

    lax.fori_loop(0, width, finish, 0)


def adjoint(retard, decay, weight, meta, coefs, c, jy, f7, partials):
    width, count, layers, _ = f7.shape
    species = count - 4
    rows = width + 2 * HALO
    f32 = jnp.float32
    vmem = pl.BlockSpec(memory_space=pltpu.VMEM)
    smem = pl.BlockSpec(memory_space=pltpu.SMEM)
    parts = len(partials) - 1
    return pl.pallas_call(
        functools.partial(adjoint_kernel, layers=layers, width=width, species=species, parts=parts),
        out_shape=jax.ShapeDtypeStruct((layers * width, LANES), f32),
        in_specs=[smem] * 2 + [vmem] * (2 + len(coefs) + 3 + len(partials)),
        out_specs=vmem,
        scratch_shapes=[
            pltpu.VMEM((2, rows, species + 1, layers, LANES), f32),
            pltpu.VMEM((rows, layers, LANES), f32),
            pltpu.VMEM((rows, 2, layers, LANES), f32),
            pltpu.VMEM((rows * layers, meta.shape[1]), jnp.bfloat16),
        ],
        compiler_params=pltpu.CompilerParams(vmem_limit_bytes=VMEM_LIMIT),
        name="adjoint_steps",
    )(retard, decay, weight, meta, *coefs, c, jy, f7, *partials)


def swaps(first, second, axis):
    count = lax.axis_size(axis)
    even = [p for i in range(0, count - 1, 2) for p in ((i, i + 1), (i + 1, i))]
    odd = [p for i in range(1, count - 1, 2) for p in ((i, i + 1), (i + 1, i))]
    return lax.ppermute(first, axis, even), lax.ppermute(second, axis, odd)


def from_others(value, axis, reach):
    count = lax.axis_size(axis)
    if count in (2, 4):
        return [lax.ppermute(value, axis, [(i, i ^ d) for i in range(count)]) for d in range(1, count)]
    return [
        lax.ppermute(value, axis, [(i, i + d) for i in range(count) if 0 <= i + d < count])
        for distance in range(1, min(reach, count - 1) + 1)
        for d in (distance, -distance)
    ]


def well_table(screen_cells, screen_count, row_start, col_start, total_x, total_y):
    start, second = screen_cells[:, 0], screen_cells[:, 1]
    plane = total_x * total_y
    depth = start // plane
    x = start % plane // total_y
    y = start % total_y
    end = x + (screen_count - 1) * ((second - start) // total_y)
    first, last = jnp.minimum(x, end) - row_start, jnp.maximum(x, end) - row_start
    zero = jnp.zeros_like(depth)
    return jnp.stack([depth, first, last, y - col_start, screen_count, zero, zero, zero])


def shards(
    initial, logk, direction, face_speed, face_flags, retard, decay, screen_cells, screen_count, well_weight
):
    species, layers, width, columns = initial.shape
    total_x = width * lax.axis_size("gx")
    total_y = columns * lax.axis_size(Y)
    meta = well_table(
        screen_cells, screen_count, lax.axis_index("gx") * width, lax.axis_index(Y) * columns, total_x, total_y
    )
    f7, e, xa, xb = pack(initial, logk, direction, face_speed, face_flags)
    ea, eb = swaps(e, e, Y)
    xa, xb = add_strips(ea, eb, xa, xb)
    xa, xb = swaps(xa, xb, "gx")
    partial, px, qx, py, qym, d, c, jy = forward(retard, f7, e, ea, eb, xa, xb, meta)
    reach = -(-(screen_cells.shape[1] - 1 + HALO) // width)
    partials = [partial] + from_others(partial, "gx", reach)
    hessian = adjoint(retard, decay, well_weight, meta, (px, qx, py, qym, d), c, jy, f7, partials)
    return hessian.reshape(layers, width, columns)


def solution(mesh):
    in_specs = (
        P("grp", None, "gx", Y),
        P("grp", "gx", Y),
        P("grp", "gx", Y),
        P("grp", None, "gx", Y),
        P("grp", None, "gx", Y),
        P(),
        P(),
        P("grp", None),
        P("grp"),
        P("grp", None),
    )
    return jax.shard_map(shards, mesh=mesh, in_specs=in_specs, out_specs=P("grp", "gx", Y), check_vma=False)
```

```python
import functools

import jax
import jax.numpy as jnp
from jax import lax
from jax.experimental import pallas as pl
from jax.experimental.pallas import tpu as pltpu
from jax.sharding import PartitionSpec as P

STEPS = 4
HALO = STEPS
RATE = 0.02
HALF_DT = 0.025
LANES = 128
GROUP = 16
RIGHT = 64
Y = ("gy", "sa")
MIB = 1024 * 1024


def lane_of(shape):
    return lax.broadcasted_iota(jnp.int32, shape, len(shape) - 1)


def roll(value, shift, axis):
    return pltpu.roll(value, shift % value.shape[axis], axis)


def pack_edges(fields):
    lane = lane_of(fields[0].shape)
    packed = jnp.zeros_like(fields[0])
    for f, field in enumerate(fields):
        packed = jnp.where(lane // GROUP == f, roll(field, 8 + GROUP * f, 1), packed)
    return packed


def y_neighbours(value, strip, s):
    lane = lane_of(value.shape)
    after = jnp.where(lane == LANES - 1, roll(strip, 127 - (RIGHT + GROUP * s + 8), 1), roll(value, 127, 1))
    before = jnp.where(lane == 0, roll(strip, -(GROUP * s + 7), 1), roll(value, 1, 1))
    return after, before


def y_before(value, strip):
    return jnp.where(lane_of(value.shape) == 0, roll(strip, -7, 1), roll(value, 1, 1))


def y_after(value, strip, s):
    lane = lane_of(value.shape)
    return jnp.where(lane == LANES - 1, roll(strip, 127 - (RIGHT + GROUP * s + 8), 1), roll(value, 127, 1))


def z_pair(value):
    layers = value.shape[0]
    depth = lax.broadcasted_iota(jnp.int32, value.shape, 0)
    above = jnp.where(depth == layers - 1, value, roll(value, layers - 1, 0))
    below = jnp.where(depth == 0, value, roll(value, 1, 0))
    return above + below


def strip_retard(retard_ref, shape):
    place = lane_of(shape) % RIGHT // GROUP
    return jnp.where(place == 0, retard_ref[0], jnp.where(place == 1, retard_ref[1], retard_ref[2]))


def pack_kernel(initial_ref, logk_ref, direction_ref, speed_ref, flags_ref, f7_ref, e_ref, xa_ref, xb_ref, *, layers, width, species):
    plane = layers * width
    even = lax.rem(lax.axis_index("gx"), 2) == 0
    top, bottom = width - HALO, 0

    def row(x, carry):
        def take(ref, index):
            return ref[pl.ds(index * plane + x, layers, stride=width), :]

        fields = [take(initial_ref, s) for s in range(species)]
        conductance = jnp.exp(take(logk_ref, 0))
        fields += [conductance, conductance * take(direction_ref, 0)]
        for axis in range(2):
            speed = take(speed_ref, axis)
            fields.append(jnp.where(take(flags_ref, axis) == 1, speed, -speed))
        for f, field in enumerate(fields):
            f7_ref[x, f] = field
        e_ref[x] = pack_edges(fields)
        return carry

    lax.fori_loop(0, width, row, 0, unroll=True)
    count = species + 4
    start_a = jnp.where(even, top, bottom)
    start_b = jnp.where(even, bottom, top)
    for r in range(HALO):
        xa_ref[r, 0:count] = f7_ref[start_a + r]
        xb_ref[r, 0:count] = f7_ref[start_b + r]


def pack(initial, logk, direction, face_speed, face_flags):
    species, layers, width, _ = initial.shape
    flat = lambda a: a.reshape(-1, LANES)
    f32 = jnp.float32
    return pl.pallas_call(
        functools.partial(pack_kernel, layers=layers, width=width, species=species),
        out_shape=(
            jax.ShapeDtypeStruct((width, species + 4, layers, LANES), f32),
            jax.ShapeDtypeStruct((width, layers, LANES), f32),
            jax.ShapeDtypeStruct((HALO, species + 5, layers, LANES), f32),
            jax.ShapeDtypeStruct((HALO, species + 5, layers, LANES), f32),
        ),
        in_specs=[pl.BlockSpec(memory_space=pltpu.VMEM)] * 5,
        out_specs=[pl.BlockSpec(memory_space=pltpu.VMEM)] * 4,
        compiler_params=pltpu.CompilerParams(vmem_limit_bytes=4 * MIB),
        name="pack",
    )(flat(initial), flat(logk), flat(direction), flat(face_speed), flat(face_flags))


def strips_kernel(ea_ref, eb_ref, xa_in, xb_in, xa_ref, xb_ref, buf_a, buf_b, sem_a, sem_b, *, width, count):
    even_x = lax.rem(lax.axis_index("gx"), 2) == 0
    even_y = lax.rem(lax.axis_index(Y), 2) == 0
    start_a = jnp.where(even_x, width - HALO, 0)
    start_b = jnp.where(even_x, 0, width - HALO)
    for r in range(HALO):
        for start, buf in ((start_a, buf_a), (start_b, buf_b)):
            one, two = ea_ref[start + r], eb_ref[start + r]
            from_left = lane_of(one.shape) % GROUP < 8
            buf[r] = jnp.where(from_left == even_y, two, one)
    copies = [
        pltpu.make_async_copy(buf_a, xa_ref.at[:, count], sem_a),
        pltpu.make_async_copy(buf_b, xb_ref.at[:, count], sem_b),
    ]
    for copy in copies:
        copy.start()
    for copy in copies:
        copy.wait()


def add_strips(ea, eb, xa, xb):
    width, layers, _ = ea.shape
    buffer = pltpu.VMEM((HALO, layers, LANES), jnp.float32)
    return pl.pallas_call(
        functools.partial(strips_kernel, width=width, count=xa.shape[1] - 1),
        out_shape=(jax.ShapeDtypeStruct(xa.shape, xa.dtype), jax.ShapeDtypeStruct(xb.shape, xb.dtype)),
        in_specs=[pl.BlockSpec(memory_space=pltpu.VMEM)] * 2 + [pl.BlockSpec(memory_space=pl.ANY)] * 2,
        out_specs=[pl.BlockSpec(memory_space=pl.ANY)] * 2,
        input_output_aliases={2: 0, 3: 1},
        scratch_shapes=[buffer, buffer, pltpu.SemaphoreType.DMA, pltpu.SemaphoreType.DMA],
        compiler_params=pltpu.CompilerParams(vmem_limit_bytes=2 * MIB),
        name="corner_strips",
    )(ea, eb, xa, xb)


def well_rows(meta_ref):
    return [meta_ref[i : i + 1, :] for i in range(4)]


def forward_kernel(
    retard_ref, f7_ref, e_ref, ea_ref, eb_ref, xa_ref, xb_ref, meta_ref,
    partial_ref, px_ref, qx_ref, py_ref, qym_ref, d_ref, c_ref, jy_ref,
    k_ref, kd_ref, ux_ref, uy_ref, qy_ref, pym_ref, bx_ref, by_ref, bym_ref, t_ref,
    *, layers, width, species,
):
    f32 = jnp.float32
    rows = width + 2 * HALO
    shape = (layers, LANES)
    lane = lane_of(shape)
    gx, gy = lax.axis_index("gx"), lax.axis_index(Y)
    even_x, even_y = lax.rem(gx, 2) == 0, lax.rem(gy, 2) == 0
    total_x = width * lax.axis_size("gx")
    first_y, last_y = gy == 0, gy == lax.axis_size(Y) - 1
    column = lane % GROUP
    near = column < 8
    left = lane < RIGHT
    count = species + 4

    def place(r, fields, own_edges, outer_edges):
        left_strip = jnp.where(near, outer_edges, own_edges)
        right_strip = jnp.where(near, own_edges, outer_edges)
        for s in range(species):
            c_ref[0, r, s] = fields[s]
        c_ref[0, r, species] = jnp.where(left, left_strip, roll(right_strip, RIGHT, 1))
        for f, ref in enumerate((k_ref, kd_ref, ux_ref, uy_ref), species):
            ref[r, 0] = fields[f]
            index = GROUP * f + column
            ref[r, 1] = jnp.where(
                left,
                jnp.take_along_axis(left_strip, index, 1, mode="promise_in_bounds"),
                jnp.take_along_axis(right_strip, index, 1, mode="promise_in_bounds"),
            )

    def own_row(x, carry):
        one, two = ea_ref[x], eb_ref[x]
        outer = jnp.where(near == even_y, two, one)
        place(x + HALO, [f7_ref[x, f] for f in range(count)], e_ref[x], outer)
        return carry

    lax.fori_loop(0, width, own_row, 0, unroll=True)

    def halo_row(r, carry):
        for low in (True, False):
            from_a = even_x != low
            both = [jnp.where(from_a, xa_ref[r, f], xb_ref[r, f]) for f in range(count + 1)]
            place(r if low else r + HALO + width, both[:count], pack_edges(both[:count]), both[count])
        return carry

    lax.fori_loop(0, HALO, halo_row, 0, unroll=True)

    strip_mask = jnp.where(
        left, jnp.where(first_y & near, 0.0, 1.0), jnp.where(last_y & (column >= 7), 0.0, 1.0)
    ).astype(f32)
    main_mask = jnp.where(last_y & (lane == LANES - 1), 0.0, 1.0).astype(f32)

    def y_faces(r, carry):
        k4, kd4, u4 = k_ref[r, 1], kd_ref[r, 1], uy_ref[r, 1]
        half4 = HALF_DT * (k4 + roll(k4, 127, 1))
        p4 = (half4 + jnp.maximum(u4, 0.0)) * strip_mask
        q4 = (half4 - jnp.minimum(u4, 0.0)) * strip_mask
        b4 = HALF_DT * (kd4 + roll(kd4, 127, 1)) * strip_mask
        k, kd, u = k_ref[r, 0], kd_ref[r, 0], uy_ref[r, 0]
        half = HALF_DT * (k + y_after(k, k4, 0))
        p = (half + jnp.maximum(u, 0.0)) * main_mask
        q = (half - jnp.minimum(u, 0.0)) * main_mask
        b = HALF_DT * (kd + y_after(kd, kd4, 0)) * main_mask
        py_ref[r, 0], py_ref[r, 1] = p, p4
        qy_ref[r, 0], qy_ref[r, 1] = q, q4
        by_ref[r, 0], by_ref[r, 1] = b, b4
        qm, qm4 = y_before(q, q4), roll(q4, 1, 1)
        pym_ref[r, 0], pym_ref[r, 1] = y_before(p, p4), roll(p4, 1, 1)
        qym_ref[r, 0], qym_ref[r, 1] = qm, qm4
        bym_ref[r, 0], bym_ref[r, 1] = y_before(b, b4), roll(b4, 1, 1)
        d_ref[r, 0], d_ref[r, 1] = p + qm + 2 * RATE, p4 + qm4 + 2 * RATE
        return carry

    lax.fori_loop(0, rows, y_faces, 0, unroll=True)

    def x_faces(r, carry):
        x = gx * width + r - HALO
        mask = jnp.where((x >= 0) & (x + 1 < total_x), 1.0, 0.0).astype(f32)
        for i in range(2):
            u = ux_ref[r, i]
            half = HALF_DT * (k_ref[r, i] + k_ref[r + 1, i])
            p = (half + jnp.maximum(u, 0.0)) * mask
            q = (half - jnp.minimum(u, 0.0)) * mask
            px_ref[r, i] = p
            qx_ref[r, i] = q
            bx_ref[r, i] = HALF_DT * (kd_ref[r, i] + kd_ref[r + 1, i]) * mask
            d_ref[r, i] = d_ref[r, i] + p
            d_ref[r + 1, i] = d_ref[r + 1, i] + q
        return carry

    lax.fori_loop(0, rows - 1, x_faces, 0, unroll=True)

    strip_rate = strip_retard(retard_ref, shape)
    for m in range(STEPS):
        now, later = m % 2, (m + 1) % 2

        def step_row(r, carry, m=m, now=now, later=later):
            for s in (species,) + tuple(range(species)):
                i = 1 if s == species else 0
                rate = strip_rate if i else retard_ref[s]
                kept = rate - d_ref[r, i]
                upper, lower = qx_ref[r, i], px_ref[r - 1, i]
                after, before = qy_ref[r, i], pym_ref[r, i]

                def around(ref, slot):
                    value, strip = ref[slot, r, s], ref[slot, r, species]
                    if i:
                        return value, roll(value, 127, 1), roll(value, 1, 1)
                    return (value,) + y_neighbours(value, strip, s)

                def moved(ref, slot, value, yp, ym):
                    return (
                        kept * value
                        + upper * ref[slot, r + 1, s]
                        + lower * ref[slot, r - 1, s]
                        + after * yp
                        + before * ym
                        + RATE * z_pair(value)
                    )

                c, yp, ym = around(c_ref, m)
                jump = yp - c
                source = (
                    bx_ref[r, i] * (c_ref[m, r + 1, s] - c)
                    - bx_ref[r - 1, i] * (c - c_ref[m, r - 1, s])
                    + by_ref[r, i] * jump
                    - bym_ref[r, i] * (c - ym)
                )
                jy_ref[m, r, s] = jump
                if m + 1 < STEPS:
                    c_ref[m + 1, r, s] = moved(c_ref, m, c, yp, ym)
                if m > 0:
                    t, tp, tm = around(t_ref, now)
                    source = source + moved(t_ref, now, t, tp, tm)
                t_ref[later, r, s] = source
            return carry

        lax.fori_loop(m + 1, rows - 1 - m, step_row, 0, unroll=True)

    final = STEPS % 2
    depth, first, last, where_y = well_rows(meta_ref)
    wells = meta_ref.shape[1]
    own = lax.broadcasted_iota(jnp.int32, (LANES, wells), 0)
    own_hot = jnp.where(own == where_y, 1.0, 0.0).astype(jnp.bfloat16)
    strip_place = own % RIGHT // GROUP
    strip_col = own % GROUP + jnp.where(own < RIGHT, -8, 120)
    outside = (strip_col < 0) | (strip_col >= LANES)
    strip_hit = outside & (strip_col == where_y)
    layer = lax.broadcasted_iota(jnp.int32, (layers, wells), 0)
    in_layer = layer == depth
    for s in range(species):
        hot = jnp.concatenate(
            [own_hot, jnp.where(strip_hit & (strip_place == s), 1.0, 0.0).astype(jnp.bfloat16)], axis=0
        )
        total = jnp.zeros((layers, wells), f32)
        for part in range(2):
            half = width // 2
            main = t_ref[final, HALO + part * half : HALO + (part + 1) * half, s].reshape(half * layers, LANES)
            side = t_ref[final, HALO + part * half : HALO + (part + 1) * half, species].reshape(half * layers, LANES)
            both = jnp.concatenate([main, side], axis=1)
            picked = jnp.zeros((half * layers, wells), f32)
            for piece in range(3):
                coarse = both.astype(jnp.bfloat16)
                picked = picked + jnp.dot(coarse, hot, preferred_element_type=f32)
                both = both - coarse.astype(f32)
            picked = picked.reshape(half, layers, wells)
            for x in range(half):
                at = x + part * half
                inside = (first <= at) & (last >= at)
                total = total + jnp.where(inside & in_layer, picked[x], 0.0)
        partial_ref[s : s + 1, :] = jnp.sum(total, axis=0, keepdims=True)


def forward(retard, f7, e, ea, eb, xa, xb, meta):
    width, count, layers, _ = f7.shape
    species = count - 4
    rows = width + 2 * HALO
    f32 = jnp.float32
    coef = (rows, 2, layers, LANES)
    state = (rows, species + 1, layers, LANES)
    vmem = pl.BlockSpec(memory_space=pltpu.VMEM)
    return pl.pallas_call(
        functools.partial(forward_kernel, layers=layers, width=width, species=species),
        out_shape=(jax.ShapeDtypeStruct((species, meta.shape[1]), f32),)
        + (jax.ShapeDtypeStruct(coef, f32),) * 5
        + (jax.ShapeDtypeStruct((STEPS,) + state, f32),) * 2,
        in_specs=[pl.BlockSpec(memory_space=pltpu.SMEM)] + [vmem] * 7,
        out_specs=[vmem] * 8,
        scratch_shapes=[pltpu.VMEM(coef, f32)] * 9
        + [pltpu.VMEM((2,) + state, f32)],
        compiler_params=pltpu.CompilerParams(vmem_limit_bytes=24 * MIB),
        name="forward_steps",
    )(retard, f7, e, ea, eb, xa, xb, meta)


def adjoint_kernel(
    retard_ref, decay_ref, weight_ref, meta_ref, px_ref, qx_ref, py_ref, qym_ref, d_ref, c_ref, jy_ref, f7_ref,
    partial_ref, *rest, layers, width, species, parts,
):
    others, out_ref, lam_ref, hx_ref, hy_ref, mask_ref = rest[:parts], *rest[parts:]
    f32, bf16 = jnp.float32, jnp.bfloat16
    rows = width + 2 * HALO
    shape = (layers, LANES)
    lane = lane_of(shape)
    gx, gy = lax.axis_index("gx"), lax.axis_index(Y)
    total_x = width * lax.axis_size("gx")
    depth, first, last, where_y = well_rows(meta_ref)
    wells = meta_ref.shape[1]

    layer = lax.broadcasted_iota(jnp.int32, (layers, wells), 0)
    in_layer = layer == depth
    for r in range(rows):
        x = r - HALO
        inside = (first <= x) & (last >= x) & in_layer
        mask_ref[r * layers : (r + 1) * layers, :] = jnp.where(inside, 1.0, 0.0).astype(bf16)

    counts = meta_ref[4:5, :].astype(f32)
    own = lax.broadcasted_iota(jnp.int32, (LANES, wells), 0)
    strip_place = own % RIGHT // GROUP
    strip_col = own % GROUP + jnp.where(own < RIGHT, -8, 120)
    strip_hit = strip_col == where_y
    own_hit = own == where_y
    targets = [own_hit] * species
    residuals = []
    for s in range(species):
        total = partial_ref[s : s + 1, :]
        for other in others:
            total = total + other[s : s + 1, :]
        rate = jnp.full((1, wells), retard_ref[s], f32)
        factor = jnp.exp(jnp.full((1, wells), -decay_ref[s], f32)) / rate
        factor = factor * factor
        factor = factor * factor
        residual = weight_ref[s : s + 1, :] * (total * factor) / counts
        residuals.append(residual / counts * factor)
    lam = jnp.zeros((rows * layers, (species + 1) * LANES), f32)
    for piece in range(3):
        coarse = [r.astype(bf16).astype(f32) for r in residuals]
        residuals = [r - q for r, q in zip(residuals, coarse)]
        blocks = [jnp.where(own_hit, q, 0.0).astype(bf16) for q in coarse]
        side = jnp.zeros((LANES, wells), f32)
        for s in range(species):
            side = jnp.where(strip_hit & (strip_place == s), coarse[s], side)
        spread = jnp.concatenate(blocks + [side.astype(bf16)], axis=0)
        lam = lam + lax.dot_general(
            mask_ref[...], spread, (((1,), (1,)), ((), ())), preferred_element_type=f32
        )
    for s in range(species + 1):
        lam_ref[0, :, s] = lam[:, s * LANES : (s + 1) * LANES].reshape(rows, layers, LANES)

    strip_rate = strip_retard(retard_ref, shape)
    for m in reversed(range(STEPS)):
        now, later = (STEPS - 1 - m) % 2, (STEPS - m) % 2
        low, high = STEPS - m, rows - (STEPS - m)

        def retreat_row(r, carry, m=m, now=now, later=later):
            for s in range(species + 1):
                i = 1 if s == species else 0
                value = lam_ref[now, r, s]
                if i:
                    yp, ym = roll(value, 127, 1), roll(value, 1, 1)
                else:
                    yp, ym = y_neighbours(value, lam_ref[now, r, species], s)
                rate = strip_rate if i else retard_ref[s]
                lam_ref[later, r, s] = (
                    (rate - d_ref[r, i]) * value
                    + px_ref[r, i] * lam_ref[now, r + 1, s]
                    + qx_ref[r - 1, i] * lam_ref[now, r - 1, s]
                    + py_ref[r, i] * yp
                    + qym_ref[r, i] * ym
                    + RATE * z_pair(value)
                )
            return carry

        def sense_row(r, carry, m=m, now=now):
            along_x = jnp.zeros(shape, f32)
            along_y = jnp.zeros(shape, f32)
            for s in range(species):
                value = lam_ref[now, r, s]
                along_x += (c_ref[m, r + 1, s] - c_ref[m, r, s]) * (lam_ref[now, r + 1, s] - value)
                along_y += jy_ref[m, r, s] * (y_after(value, lam_ref[now, r, species], s) - value)
            strip = lam_ref[now, r, species]
            side = jy_ref[m, r, species] * (roll(strip, 127, 1) - strip)
            if m + 1 < STEPS:
                along_x += hx_ref[r]
                along_y += hy_ref[r, 0]
                side += hy_ref[r, 1]
            hx_ref[r] = along_x
            hy_ref[r, 0] = along_y
            hy_ref[r, 1] = side
            return carry

        lax.fori_loop(HALO - 1, HALO + width, sense_row, 0, unroll=True)
        if m > 0:
            lax.fori_loop(low, high, retreat_row, 0, unroll=True)

    main_mask = jnp.where((gy == lax.axis_size(Y) - 1) & (lane == LANES - 1), 0.0, 1.0).astype(f32)
    side_mask = jnp.where((gy == 0) & (lane == 0), 0.0, 1.0).astype(f32)

    def finish(x, carry):
        r = x + HALO
        at = gx * width + x
        lower = jnp.where(at > 0, 1.0, 0.0).astype(f32)
        upper = jnp.where(at + 1 < total_x, 1.0, 0.0).astype(f32)
        along_y, strip = hy_ref[r, 0] * main_mask, hy_ref[r, 1]
        side = roll(strip, -7, 1)
        for s in range(1, species):
            side = side + roll(strip, -(GROUP * s + 7), 1)
        before = jnp.where(lane == 0, side * side_mask, roll(along_y, 1, 1))
        total = hx_ref[r] * upper + hx_ref[r - 1] * lower + along_y + before
        out_ref[pl.ds(x, layers, stride=width), :] = -HALF_DT * f7_ref[x, species] * total
        return carry

    lax.fori_loop(0, width, finish, 0)


def adjoint(retard, decay, weight, meta, coefs, c, jy, f7, partials):
    width, count, layers, _ = f7.shape
    species = count - 4
    rows = width + 2 * HALO
    f32 = jnp.float32
    vmem = pl.BlockSpec(memory_space=pltpu.VMEM)
    smem = pl.BlockSpec(memory_space=pltpu.SMEM)
    parts = len(partials) - 1
    return pl.pallas_call(
        functools.partial(adjoint_kernel, layers=layers, width=width, species=species, parts=parts),
        out_shape=jax.ShapeDtypeStruct((layers * width, LANES), f32),
        in_specs=[smem] * 2 + [vmem] * (2 + len(coefs) + 3 + len(partials)),
        out_specs=vmem,
        scratch_shapes=[
            pltpu.VMEM((2, rows, species + 1, layers, LANES), f32),
            pltpu.VMEM((rows, layers, LANES), f32),
            pltpu.VMEM((rows, 2, layers, LANES), f32),
            pltpu.VMEM((rows * layers, meta.shape[1]), jnp.bfloat16),
        ],
        compiler_params=pltpu.CompilerParams(vmem_limit_bytes=16 * MIB),
        name="adjoint_steps",
    )(retard, decay, weight, meta, *coefs, c, jy, f7, *partials)


def swaps(first, second, axis):
    count = lax.axis_size(axis)
    even = [p for i in range(0, count - 1, 2) for p in ((i, i + 1), (i + 1, i))]
    odd = [p for i in range(1, count - 1, 2) for p in ((i, i + 1), (i + 1, i))]
    return lax.ppermute(first, axis, even), lax.ppermute(second, axis, odd)


def from_others(value, axis, reach):
    count = lax.axis_size(axis)
    if count in (2, 4):
        return [lax.ppermute(value, axis, [(i, i ^ d) for i in range(count)]) for d in range(1, count)]
    return [
        lax.ppermute(value, axis, [(i, i + d) for i in range(count) if 0 <= i + d < count])
        for distance in range(1, min(reach, count - 1) + 1)
        for d in (distance, -distance)
    ]


def well_table(screen_cells, screen_count, row_start, col_start, total_x, total_y):
    start, second = screen_cells[:, 0], screen_cells[:, 1]
    plane = total_x * total_y
    depth = start // plane
    x = start % plane // total_y
    y = start % total_y
    end = x + (screen_count - 1) * ((second - start) // total_y)
    first, last = jnp.minimum(x, end) - row_start, jnp.maximum(x, end) - row_start
    zero = jnp.zeros_like(depth)
    return jnp.stack([depth, first, last, y - col_start, screen_count, zero, zero, zero])


def shards(
    initial, logk, direction, face_speed, face_flags, retard, decay, screen_cells, screen_count, well_weight
):
    species, layers, width, columns = initial.shape
    total_x = width * lax.axis_size("gx")
    total_y = columns * lax.axis_size(Y)
    meta = well_table(
        screen_cells, screen_count, lax.axis_index("gx") * width, lax.axis_index(Y) * columns, total_x, total_y
    )
    f7, e, xa, xb = pack(initial, logk, direction, face_speed, face_flags)
    ea, eb = swaps(e, e, Y)
    xa, xb = add_strips(ea, eb, xa, xb)
    xa, xb = swaps(xa, xb, "gx")
    partial, px, qx, py, qym, d, c, jy = forward(retard, f7, e, ea, eb, xa, xb, meta)
    reach = -(-(screen_cells.shape[1] - 1 + HALO) // width)
    partials = [partial] + from_others(partial, "gx", reach)
    hessian = adjoint(retard, decay, well_weight, meta, (px, qx, py, qym, d), c, jy, f7, partials)
    return hessian.reshape(layers, width, columns)


def solution(mesh):
    in_specs = (
        P("grp", None, "gx", Y),
        P("grp", "gx", Y),
        P("grp", "gx", Y),
        P("grp", None, "gx", Y),
        P("grp", None, "gx", Y),
        P(),
        P(),
        P("grp", None),
        P("grp"),
        P("grp", None),
    )
    return jax.shard_map(shards, mesh=mesh, in_specs=in_specs, out_specs=P("grp", "gx", Y), check_vma=False)
```

```python
import functools

import jax
import jax.numpy as jnp
from jax import lax
from jax.experimental import pallas as pl
from jax.experimental.pallas import tpu as pltpu
from jax.sharding import PartitionSpec as P

STEPS = 4
HALO = STEPS
RATE = 0.02
HALF_DT = 0.025
LANES = 128
TILE = 8
GROUP = 16
RIGHT = 64
Y = ("gy", "sa")
MIB = 1024 * 1024
PX, QX, BX, PY, QYM, QY, PYM, BY, BYM, D, KIND, KDIR = range(12)
KINDS = 12
VMEM = pl.BlockSpec(memory_space=pltpu.VMEM)
HBM = pl.BlockSpec(memory_space=pltpu.HBM)


def lane_of(shape):
    return lax.broadcasted_iota(jnp.int32, shape, len(shape) - 1)


def roll(value, shift, axis):
    return pltpu.roll(value, shift % value.shape[axis], axis)


def pack_edges(fields):
    lane = lane_of(fields[0].shape)
    packed = jnp.zeros_like(fields[0])
    for f, field in enumerate(fields):
        packed = jnp.where(lane // GROUP == f, roll(field, 8 + GROUP * f, 1), packed)
    return packed


def y_after(value, strip, s):
    edge = roll(strip, LANES - 1 - (RIGHT + GROUP * s + 8), 1)
    return jnp.where(lane_of(value.shape) == LANES - 1, edge, roll(value, LANES - 1, 1))


def y_before(value, strip, s):
    edge = roll(strip, -(GROUP * s + 7), 1)
    return jnp.where(lane_of(value.shape) == 0, edge, roll(value, 1, 1))


def z_pair(value):
    tiles = [value[i : i + TILE] for i in range(0, value.shape[0], TILE)]
    row = lax.broadcasted_iota(jnp.int32, tiles[0].shape, 0)
    ups = [roll(t, TILE - 1, 0) for t in tiles]
    downs = [roll(t, 1, 0) for t in tiles]
    pairs = []
    for i, tile in enumerate(tiles):
        above = jnp.where(row == TILE - 1, ups[i + 1] if i + 1 < len(tiles) else tile, ups[i])
        below = jnp.where(row == 0, downs[i - 1] if i else tile, downs[i])
        pairs.append(above + below)
    return jnp.concatenate(pairs, axis=0)


def state_row(m, width):
    low, high = HALO + m, HALO + width - 1 - m

    def find(r):
        if low <= r <= high:
            return 0, r - HALO
        return (1, r - m) if r < low else (1, HALO + r - high - 1)

    return find


def coef_row(kind, width):
    low, high = HALO, HALO + width - 1
    if kind in (PX, QX, BX, D):
        high -= 1
    if kind == D:
        low += 1

    def find(r):
        if low <= r <= high:
            return 0, r - HALO
        return (1, r) if r <= HALO else (1, HALO + 1 + r - (HALO + width - 1))

    return find


def read_state(refs, m, width, r, s):
    which, index = state_row(m, width)(r)
    return refs[which][m, index, s]


def read_coef(refs, kind, width, r, i):
    which, index = coef_row(kind, width)(r)
    return refs[which][index, kind, i]


def pack_kernel(*refs, layers, width, species):
    sources, (f7_ref, e_ref, xa_ref, xb_ref), buffers, sem = refs[:5], refs[5:9], refs[9:14], refs[14]
    copies = [pltpu.make_async_copy(a, b, sem.at[i]) for i, (a, b) in enumerate(zip(sources, buffers))]
    for copy in copies:
        copy.start()
    for copy in copies:
        copy.wait()
    initial_ref, logk_ref, direction_ref, speed_ref, flags_ref = buffers
    plane = layers * width
    even = lax.rem(lax.axis_index("gx"), 2) == 0
    top, bottom = width - HALO, 0
    for x in range(width):

        def take(ref, index):
            return ref[pl.ds(index * plane + x, layers, stride=width), :]

        fields = [take(initial_ref, s) for s in range(species)]
        conductance = jnp.exp(take(logk_ref, 0))
        fields += [conductance, conductance * take(direction_ref, 0)]
        for axis in range(2):
            speed = take(speed_ref, axis)
            fields.append(jnp.where(take(flags_ref, axis) == 1, speed, -speed))
        for f, field in enumerate(fields):
            f7_ref[x, f] = field
        e_ref[x] = pack_edges(fields)
    count = species + 4
    start_a = jnp.where(even, top, bottom)
    start_b = jnp.where(even, bottom, top)
    for r in range(HALO):
        xa_ref[r, 0:count] = f7_ref[start_a + r]
        xb_ref[r, 0:count] = f7_ref[start_b + r]


def pack(initial, logk, direction, face_speed, face_flags):
    species, layers, width, _ = initial.shape
    f32 = jnp.float32
    sources = [a.reshape(-1, LANES) for a in (initial, logk, direction, face_speed, face_flags)]
    return pl.pallas_call(
        functools.partial(pack_kernel, layers=layers, width=width, species=species),
        out_shape=(
            jax.ShapeDtypeStruct((width, species + 4, layers, LANES), f32),
            jax.ShapeDtypeStruct((width, layers, LANES), f32),
            jax.ShapeDtypeStruct((HALO, species + 5, layers, LANES), f32),
            jax.ShapeDtypeStruct((HALO, species + 5, layers, LANES), f32),
        ),
        in_specs=[HBM] * 5,
        out_specs=[VMEM] * 4,
        scratch_shapes=[pltpu.VMEM(a.shape, a.dtype) for a in sources] + [pltpu.SemaphoreType.DMA((5,))],
        compiler_params=pltpu.CompilerParams(vmem_limit_bytes=5 * MIB),
        name="pack",
    )(*sources)


def strips_kernel(ea_ref, eb_ref, xa_in, xb_in, xa_ref, xb_ref, buf_a, buf_b, sem_a, sem_b, *, width, count):
    even_x = lax.rem(lax.axis_index("gx"), 2) == 0
    even_y = lax.rem(lax.axis_index(Y), 2) == 0
    start_a = jnp.where(even_x, width - HALO, 0)
    start_b = jnp.where(even_x, 0, width - HALO)
    for r in range(HALO):
        for start, buf in ((start_a, buf_a), (start_b, buf_b)):
            one, two = ea_ref[start + r], eb_ref[start + r]
            from_left = lane_of(one.shape) % GROUP < 8
            buf[r] = jnp.where(from_left == even_y, two, one)
    copies = [
        pltpu.make_async_copy(buf_a, xa_ref.at[:, count], sem_a),
        pltpu.make_async_copy(buf_b, xb_ref.at[:, count], sem_b),
    ]
    for copy in copies:
        copy.start()
    for copy in copies:
        copy.wait()


def add_strips(ea, eb, xa, xb):
    width, layers, _ = ea.shape
    buffer = pltpu.VMEM((HALO, layers, LANES), jnp.float32)
    return pl.pallas_call(
        functools.partial(strips_kernel, width=width, count=xa.shape[1] - 1),
        out_shape=(jax.ShapeDtypeStruct(xa.shape, xa.dtype), jax.ShapeDtypeStruct(xb.shape, xb.dtype)),
        in_specs=[pl.BlockSpec(memory_space=pltpu.VMEM)] * 2 + [pl.BlockSpec(memory_space=pl.ANY)] * 2,
        out_specs=[pl.BlockSpec(memory_space=pl.ANY)] * 2,
        input_output_aliases={2: 0, 3: 1},
        scratch_shapes=[buffer, buffer, pltpu.SemaphoreType.DMA, pltpu.SemaphoreType.DMA],
        compiler_params=pltpu.CompilerParams(vmem_limit_bytes=2 * MIB),
        name="corner_strips",
    )(ea, eb, xa, xb)


def place(fields, own_edges, outer_edges, left, near, column, species):
    left_strip = jnp.where(near, outer_edges, own_edges)
    right_strip = jnp.where(near, own_edges, outer_edges)
    states = list(fields[:species]) + [jnp.where(left, left_strip, roll(right_strip, RIGHT, 1))]
    others = []
    for f in range(species, species + 4):
        index = GROUP * f + column
        strip = jnp.where(
            left,
            jnp.take_along_axis(left_strip, index, 1, mode="promise_in_bounds"),
            jnp.take_along_axis(right_strip, index, 1, mode="promise_in_bounds"),
        )
        others.append((fields[f], strip))
    return states, others


def y_coefs(k, kd, u, main_mask, strip_mask):
    half4 = HALF_DT * (k[1] + roll(k[1], 127, 1))
    p4 = (half4 + jnp.maximum(u[1], 0.0)) * strip_mask
    q4 = (half4 - jnp.minimum(u[1], 0.0)) * strip_mask
    b4 = HALF_DT * (kd[1] + roll(kd[1], 127, 1)) * strip_mask
    half = HALF_DT * (k[0] + y_after(k[0], k[1], 0))
    p = (half + jnp.maximum(u[0], 0.0)) * main_mask
    q = (half - jnp.minimum(u[0], 0.0)) * main_mask
    b = HALF_DT * (kd[0] + y_after(kd[0], kd[1], 0)) * main_mask
    return {
        PY: (p, p4),
        QY: (q, q4),
        BY: (b, b4),
        PYM: (y_before(p, p4, 0), roll(p4, 1, 1)),
        QYM: (y_before(q, q4, 0), roll(q4, 1, 1)),
        BYM: (y_before(b, b4, 0), roll(b4, 1, 1)),
    }


def x_coefs(k, k_next, kd, kd_next, u, mask):
    half = HALF_DT * (k + k_next)
    p = half + jnp.maximum(u, 0.0)
    q = half - jnp.minimum(u, 0.0)
    b = HALF_DT * (kd + kd_next)
    return (p, q, b) if mask is None else (p * mask, q * mask, b * mask)


def masks(layers):
    shape = (layers, LANES)
    lane = lane_of(shape)
    column = lane % GROUP
    near, left = column < 8, lane < RIGHT
    gy = lax.axis_index(Y)
    first_y, last_y = gy == 0, gy == lax.axis_size(Y) - 1
    strip_mask = jnp.where(
        left, jnp.where(first_y & near, 0.0, 1.0), jnp.where(last_y & (column >= 7), 0.0, 1.0)
    ).astype(jnp.float32)
    main_mask = jnp.where(last_y & (lane == LANES - 1), 0.0, 1.0).astype(jnp.float32)
    return column, near, left, main_mask, strip_mask


def step_row(r, m, rates, coef, state, tangent, put_c, put_t, put_jy):
    species = len(rates) - 1
    strips = state(r, species)
    strips_t = tangent(r, species) if m > 0 else None
    for s in (species,) + tuple(range(species)):
        i = 1 if s == species else 0
        kept = rates[s] - coef(D, r, i)
        upper, lower = coef(QX, r, i), coef(PX, r - 1, i)
        after, before = coef(QY, r, i), coef(PYM, r, i)

        def around(value, strip):
            if i:
                return roll(value, LANES - 1, 1), roll(value, 1, 1)
            return y_after(value, strip, s), y_before(value, strip, s)

        def moved(value, up, down, yp, ym):
            return kept * value + upper * up + lower * down + after * yp + before * ym + RATE * z_pair(value)

        c = strips if i else state(r, s)
        up, down = state(r + 1, s), state(r - 1, s)
        yp, ym = around(c, strips)
        jump = yp - c
        source = (
            coef(BX, r, i) * (up - c)
            - coef(BX, r - 1, i) * (c - down)
            + coef(BY, r, i) * jump
            - coef(BYM, r, i) * (c - ym)
        )
        put_jy(s, jump)
        if m + 1 < STEPS:
            put_c(s, moved(c, up, down, yp, ym))
        if m > 0:
            t = strips_t if i else tangent(r, s)
            tp, tm = around(t, strips_t)
            source = source + moved(t, tangent(r + 1, s), tangent(r - 1, s), tp, tm)
        put_t(s, source)


def well_rows(meta_ref):
    return [meta_ref[i : i + 1, :] for i in range(4)]


def strip_columns(wells):
    own = lax.broadcasted_iota(jnp.int32, (LANES, wells), 0)
    return own, own % RIGHT // GROUP, own % GROUP + jnp.where(own < RIGHT, -8, 120)


def cone_kernel(
    rate_ref, f7_ref, e_ref, ea_ref, eb_ref, meta_ref,
    coef_ref, c_ref, t_ref, jy_ref, mask_ref, hot_ref, *, layers, width, species,
):
    f32, bf16 = jnp.float32, jnp.bfloat16
    column, near, left, main_mask, strip_mask = masks(layers)
    even_y = lax.rem(lax.axis_index(Y), 2) == 0
    count = species + 4
    kept = []
    for x in range(width):
        outer = jnp.where(near == even_y, eb_ref[x], ea_ref[x])
        states, (k, kd, ux, uy) = place(
            [f7_ref[x, f] for f in range(count)], e_ref[x], outer, left, near, column, species
        )
        for s in range(species + 1):
            c_ref[0, x, s] = states[s]
        found = y_coefs(k, kd, uy, main_mask, strip_mask)
        for kind, pair in found.items():
            coef_ref[x, kind, 0], coef_ref[x, kind, 1] = pair
        for i in range(2):
            coef_ref[x, KIND, i], coef_ref[x, KDIR, i] = k[i], kd[i]
            diagonal = found[PY][i] + found[QYM][i] + 2 * RATE
            if x:
                p, q, b = x_coefs(kept[0][i], k[i], kept[1][i], kd[i], kept[2][i], None)
                coef_ref[x - 1, PX, i], coef_ref[x - 1, QX, i], coef_ref[x - 1, BX, i] = p, q, b
                coef_ref[x - 1, D, i] = coef_ref[x - 1, D, i] + p
                diagonal = diagonal + q
            coef_ref[x, D, i] = diagonal
            if x == width - 1:
                coef_ref[x, PX, i] = ux[i]
        kept = (k, kd, ux)

    rates = [rate_ref[s : s + 1, :] for s in range(species + 1)]
    for m in range(STEPS):
        for r in range(HALO + 1 + m, HALO + width - 1 - m):
            x = r - HALO

            def put(ref, slot):
                def store(s, value):
                    ref[slot, x, s] = value

                return store

            step_row(
                r, m, rates,
                lambda kind, r, i: coef_ref[r - HALO, kind, i],
                lambda r, s: c_ref[m, r - HALO, s],
                lambda r, s: t_ref[m - 1, r - HALO, s],
                put(c_ref, m + 1), put(t_ref, m), put(jy_ref, m),
            )

    depth, first, last, where_y = well_rows(meta_ref)
    wells = meta_ref.shape[1]
    in_layer = lax.broadcasted_iota(jnp.int32, (layers, wells), 0) == depth
    for r in range(width + 2 * HALO):
        inside = (first <= r - HALO) & (last >= r - HALO) & in_layer
        mask_ref[r * layers : (r + 1) * layers, :] = jnp.where(inside, 1.0, 0.0).astype(bf16)
    own, strip_species, strip_column = strip_columns(wells)
    hit = ((strip_column < 0) | (strip_column >= LANES)) & (strip_column == where_y)
    for s in range(species):
        hot_ref[s, 0:LANES] = jnp.where(own == where_y, 1.0, 0.0).astype(bf16)
        hot_ref[s, LANES : 2 * LANES] = jnp.where(hit & (strip_species == s), 1.0, 0.0).astype(bf16)


def cone(rates, f7, e, ea, eb, meta):
    width, count, layers, _ = f7.shape
    species, wells = count - 4, meta.shape[1]
    f32 = jnp.float32
    state = jax.ShapeDtypeStruct((STEPS, width, species + 1, layers, LANES), f32)
    return pl.pallas_call(
        functools.partial(cone_kernel, layers=layers, width=width, species=species),
        out_shape=(
            jax.ShapeDtypeStruct((width, KINDS, 2, layers, LANES), f32),
            state,
            state,
            state,
            jax.ShapeDtypeStruct(((width + 2 * HALO) * layers, wells), jnp.bfloat16),
            jax.ShapeDtypeStruct((species, 2 * LANES, wells), jnp.bfloat16),
        ),
        in_specs=[VMEM] * 6,
        out_specs=[VMEM] * 6,
        compiler_params=pltpu.CompilerParams(vmem_limit_bytes=4 * MIB),
        cost_estimate=pl.CostEstimate(flops=10**7, bytes_accessed=10**7, transcendentals=0),
        name="cone_steps",
    )(rates, f7, e, ea, eb, meta)


def rim_kernel(
    rate_ref, xa_ref, xb_ref, coef_in, c_in, t_in, mask_ref, hot_ref,
    partial_ref, coef_out, c_out, jy_out, t_out, *, layers, width, species,
):
    f32, bf16 = jnp.float32, jnp.bfloat16
    column, near, left, main_mask, strip_mask = masks(layers)
    gx = lax.axis_index("gx")
    even_x = lax.rem(gx, 2) == 0
    count = species + 4
    rows = width + 2 * HALO
    coefs = (coef_in, coef_out)

    def put_coef(kind, r, i, value):
        which, index = coef_row(kind, width)(r)
        coefs[which][index, kind, i] = value

    speeds = {}
    for r in list(range(HALO)) + list(range(HALO + width, rows)):
        from_a = even_x if r > HALO else jnp.logical_not(even_x)
        both = [jnp.where(from_a, xa_ref[r % (HALO + width), f], xb_ref[r % (HALO + width), f]) for f in range(count + 1)]
        states, (k, kd, ux, uy) = place(
            both[:count], pack_edges(both[:count]), both[count], left, near, column, species
        )
        index = state_row(0, width)(r)[1]
        for s in range(species + 1):
            c_out[0, index, s] = states[s]
        for kind, pair in y_coefs(k, kd, uy, main_mask, strip_mask).items():
            for i in range(2):
                put_coef(kind, r, i, pair[i])
        for i in range(2):
            put_coef(KIND, r, i, k[i])
            put_coef(KDIR, r, i, kd[i])
        speeds[r] = ux
    last = HALO + width - 1
    speeds[last] = [coef_in[width - 1, PX, i] for i in range(2)]
    inside_low = jnp.where(gx > 0, 1.0, 0.0).astype(f32)
    inside_high = jnp.where(gx < lax.axis_size("gx") - 1, 1.0, 0.0).astype(f32)
    get = lambda kind, r, i: read_coef(coefs, kind, width, r, i)
    for r in list(range(HALO)) + list(range(last, rows - 1)):
        for i in range(2):
            p, q, b = x_coefs(
                get(KIND, r, i), get(KIND, r + 1, i), get(KDIR, r, i), get(KDIR, r + 1, i), speeds[r][i],
                inside_low if r < HALO else inside_high,
            )
            put_coef(PX, r, i, p)
            put_coef(QX, r, i, q)
            put_coef(BX, r, i, b)
    for r in list(range(1, HALO + 1)) + list(range(last, rows - 1)):
        for i in range(2):
            if r == HALO:
                value = coef_in[0, D, i] + get(QX, r - 1, i)
            elif r == last:
                value = coef_in[width - 1, D, i] + get(PX, r, i)
            else:
                value = get(PY, r, i) + get(QYM, r, i) + 2 * RATE + get(PX, r, i) + get(QX, r - 1, i)
            put_coef(D, r, i, value)

    rates = [rate_ref[s : s + 1, :] for s in range(species + 1)]
    for m in range(STEPS):
        for r in list(range(1 + m, HALO + 1 + m)) + list(range(last - m, rows - 1 - m)):
            index = state_row(m + 1, width)(r)[1]

            def put(ref, slot):
                def store(s, value):
                    ref[slot, index, s] = value

                return store

            step_row(
                r, m, rates, get,
                lambda r, s: read_state((c_in, c_out), m, width, r, s),
                lambda r, s: tangent_row(t_in, t_out, m, width, r)[s],
                put(c_out, m + 1), put(t_out, m), put(jy_out, m),
            )

    wells = mask_ref.shape[1]
    for s in range(species):
        total = jnp.zeros((layers, wells), f32)
        for half in range(2):
            span = range(HALO + half * width // 2, HALO + (half + 1) * width // 2)
            both = jnp.concatenate(
                [
                    jnp.concatenate([tangent_row(t_in, t_out, STEPS, width, r)[p] for r in span], axis=0)
                    for p in (s, species)
                ],
                axis=1,
            )
            picked = jnp.zeros((len(span) * layers, wells), f32)
            for piece in range(3):
                coarse = both.astype(bf16)
                picked = picked + jnp.dot(coarse, hot_ref[s], preferred_element_type=f32)
                both = both - coarse.astype(f32)
            picked = picked * mask_ref[span[0] * layers : (span[-1] + 1) * layers, :].astype(f32)
            for x in range(len(span)):
                total = total + picked[x * layers : (x + 1) * layers]
        partial_ref[s : s + 1, :] = jnp.sum(total, axis=0, keepdims=True)


def tangent_row(t_in, t_out, m, width, r):
    which, index = state_row(m, width)(r)
    return (t_in, t_out)[which].at[m - 1, index]


def rim(rates, xa, xb, coef, c, t, mask, hot):
    _, width, planes, layers, _ = c.shape
    species, wells = planes - 1, mask.shape[1]
    f32 = jnp.float32
    state = (STEPS, 2 * HALO, planes, layers, LANES)
    return pl.pallas_call(
        functools.partial(rim_kernel, layers=layers, width=width, species=species),
        out_shape=(
            jax.ShapeDtypeStruct((species, wells), f32),
            jax.ShapeDtypeStruct((2 * HALO + 2, KINDS, 2, layers, LANES), f32),
            jax.ShapeDtypeStruct(state, f32),
            jax.ShapeDtypeStruct(state, f32),
        ),
        in_specs=[VMEM] * 8,
        out_specs=[VMEM] * 4,
        scratch_shapes=[pltpu.VMEM(state, f32)],
        compiler_params=pltpu.CompilerParams(vmem_limit_bytes=8 * MIB),
        name="rim_steps",
    )(rates, xa, xb, coef, c, t, mask, hot)


def adjoint_kernel(
    rate_ref, weight_ref, meta_ref, coef_in, coef_out, c_in, c_out, jy_in, jy_out, mask_ref, partial_ref, *rest,
    layers, width, species, parts,
):
    others, out_ref, lam_ref = rest[:parts], *rest[parts:]
    f32, bf16 = jnp.float32, jnp.bfloat16
    rows = width + 2 * HALO
    shape = (layers, LANES)
    lane = lane_of(shape)
    gx, gy = lax.axis_index("gx"), lax.axis_index(Y)
    where_y = meta_ref[3:4, :]
    counts = meta_ref[4:5, :].astype(f32)
    wells = meta_ref.shape[1]
    coefs, states = (coef_in, coef_out), (c_in, c_out)
    coef = lambda kind, r, i: read_coef(coefs, kind, width, r, i)

    own, strip_species, strip_column = strip_columns(wells)
    strip_hit, own_hit = strip_column == where_y, own == where_y
    residuals = []
    for s in range(species):
        total = partial_ref[s : s + 1, :]
        for other in others:
            total = total + other[s : s + 1, :]
        factor = rate_ref[species + 1 + s, 0:1][:, None]
        residual = weight_ref[s : s + 1, :] * (total * factor) / counts
        residuals.append(residual / counts * factor)
    lam = jnp.zeros((rows * layers, (species + 1) * LANES), f32)
    for piece in range(3):
        coarse = [r.astype(bf16).astype(f32) for r in residuals]
        residuals = [r - q for r, q in zip(residuals, coarse)]
        blocks = [jnp.where(own_hit, q, 0.0).astype(bf16) for q in coarse]
        side = jnp.zeros((LANES, wells), f32)
        for s in range(species):
            side = jnp.where(strip_hit & (strip_species == s), coarse[s], side)
        spread = jnp.concatenate(blocks + [side.astype(bf16)], axis=0)
        lam = lam + lax.dot_general(mask_ref[...], spread, (((1,), (1,)), ((), ())), preferred_element_type=f32)
    for s in range(species + 1):
        lam_ref[0, :, s] = lam[:, s * LANES : (s + 1) * LANES].reshape(rows, layers, LANES)

    rates = [rate_ref[s : s + 1, :] for s in range(species + 1)]
    first_row, last_row = HALO - 1, HALO + width - 1
    sums_x, sums_y, sums_side = {}, {}, {}
    for m in reversed(range(STEPS)):
        now = STEPS - 1 - m
        low, high = STEPS - m, rows - 1 - (STEPS - m)
        for r in range(min(low, first_row), max(high, last_row) + 1):
            sense, retreat = first_row <= r <= last_row, m > 0 and low <= r <= high
            strip = lam_ref[now, r, species]
            along_x = along_y = side = None
            for s in range(species + 1):
                i = 1 if s == species else 0
                value = strip if i else lam_ref[now, r, s]
                up = lam_ref[now, r + 1, s]
                yp = roll(value, LANES - 1, 1) if i else y_after(value, strip, s)
                if sense:
                    if not i:
                        jump = read_state(states, m, width, r + 1, s) - read_state(states, m, width, r, s)
                        term = jump * (up - value)
                        along_x = term if along_x is None else along_x + term
                    if r >= HALO:
                        which, index = state_row(m + 1, width)(r)
                        term = (jy_in, jy_out)[which][m, index, s] * (yp - value)
                        if i:
                            side = term
                        else:
                            along_y = term if along_y is None else along_y + term
                if retreat:
                    ym = roll(value, 1, 1) if i else y_before(value, strip, s)
                    lam_ref[now + 1, r, s] = (
                        (rates[s] - coef(D, r, i)) * value
                        + coef(PX, r, i) * up
                        + coef(QX, r - 1, i) * lam_ref[now, r - 1, s]
                        + coef(PY, r, i) * yp
                        + coef(QYM, r, i) * ym
                        + RATE * z_pair(value)
                    )
            if sense:
                for store, term in ((sums_x, along_x), (sums_y, along_y), (sums_side, side)):
                    if term is not None:
                        store[r] = store[r] + term if r in store else term

    main_mask = jnp.where((gy == lax.axis_size(Y) - 1) & (lane == LANES - 1), 0.0, 1.0).astype(f32)
    side_mask = jnp.where((gy == 0) & (lane == 0), 0.0, 1.0).astype(f32)
    for x in range(width):
        r = x + HALO
        upper, lower = sums_x[r], sums_x[r - 1]
        if x == 0:
            lower = lower * jnp.where(gx > 0, 1.0, 0.0).astype(f32)
        if x == width - 1:
            upper = upper * jnp.where(gx < lax.axis_size("gx") - 1, 1.0, 0.0).astype(f32)
        along_y, strip = sums_y[r] * main_mask, sums_side[r]
        side = roll(strip, -7, 1)
        for s in range(1, species):
            side = side + roll(strip, -(GROUP * s + 7), 1)
        before = jnp.where(lane == 0, side * side_mask, roll(along_y, 1, 1))
        out_ref[pl.ds(x, layers, stride=width), :] = -HALF_DT * coef(KIND, r, 0) * (upper + lower + along_y + before)


def adjoint(rates, weight, meta, coef_in, coef_out, c_in, c_out, jy_in, jy_out, mask, partials):
    _, width, planes, layers, _ = c_in.shape
    species = planes - 1
    parts = len(partials) - 1
    return pl.pallas_call(
        functools.partial(adjoint_kernel, layers=layers, width=width, species=species, parts=parts),
        out_shape=jax.ShapeDtypeStruct((layers * width, LANES), jnp.float32),
        in_specs=[VMEM] * (10 + len(partials)),
        out_specs=VMEM,
        scratch_shapes=[pltpu.VMEM((STEPS, width + 2 * HALO, planes, layers, LANES), jnp.float32)],
        compiler_params=pltpu.CompilerParams(vmem_limit_bytes=12 * MIB),
        name="adjoint_steps",
    )(rates, weight, meta, coef_in, coef_out, c_in, c_out, jy_in, jy_out, mask, *partials)


def swaps(first, second, axis):
    count = lax.axis_size(axis)
    even = [p for i in range(0, count - 1, 2) for p in ((i, i + 1), (i + 1, i))]
    odd = [p for i in range(1, count - 1, 2) for p in ((i, i + 1), (i + 1, i))]
    return lax.ppermute(first, axis, even), lax.ppermute(second, axis, odd)


def from_others(value, axis, reach):
    count = lax.axis_size(axis)
    if count in (2, 4):
        return [lax.ppermute(value, axis, [(i, i ^ d) for i in range(count)]) for d in range(1, count)]
    return [
        lax.ppermute(value, axis, [(i, i + d) for i in range(count) if 0 <= i + d < count])
        for distance in range(1, min(reach, count - 1) + 1)
        for d in (distance, -distance)
    ]


def well_table(screen_cells, screen_count, row_start, col_start, total_x, total_y):
    start, second = screen_cells[:, 0], screen_cells[:, 1]
    plane = total_x * total_y
    depth = start // plane
    x = start % plane // total_y
    y = start % total_y
    end = x + (screen_count - 1) * ((second - start) // total_y)
    first, last = jnp.minimum(x, end) - row_start, jnp.maximum(x, end) - row_start
    zero = jnp.zeros_like(depth)
    return jnp.stack([depth, first, last, y - col_start, screen_count, zero, zero, zero])


def rate_table(retard, decay):
    species = retard.shape[0]
    factor = (jnp.exp(-decay) / retard) ** STEPS
    place = jnp.minimum(jnp.arange(LANES) % RIGHT // GROUP, species - 1)
    strips = jnp.where(place == 0, retard[0], jnp.where(place == 1, retard[1], retard[2]))
    rows = [jnp.broadcast_to(retard[:, None], (species, LANES)), strips[None]]
    rows.append(jnp.broadcast_to(factor[:, None], (species, LANES)))
    rows.append(jnp.zeros((1, LANES), jnp.float32))
    return jnp.concatenate(rows, axis=0)


def shards(
    initial, logk, direction, face_speed, face_flags, retard, decay, screen_cells, screen_count, well_weight
):
    species, layers, width, columns = initial.shape
    total_x = width * lax.axis_size("gx")
    total_y = columns * lax.axis_size(Y)
    meta = well_table(
        screen_cells, screen_count, lax.axis_index("gx") * width, lax.axis_index(Y) * columns, total_x, total_y
    )
    rates = rate_table(retard, decay)
    f7, e, xa, xb = pack(initial, logk, direction, face_speed, face_flags)
    ea, eb = swaps(e, e, Y)
    xa, xb = add_strips(ea, eb, xa, xb)
    xa, xb = swaps(xa, xb, "gx")
    coef_in, c_in, t_in, jy_in, mask, hot = cone(rates, f7, e, ea, eb, meta)
    partial, coef_out, c_out, jy_out = rim(rates, xa, xb, coef_in, c_in, t_in, mask, hot)
    reach = -(-(screen_cells.shape[1] - 1 + HALO) // width)
    partials = [partial] + from_others(partial, "gx", reach)
    hessian = adjoint(
        rates, well_weight, meta, coef_in, coef_out, c_in, c_out, jy_in, jy_out, mask, partials
    )
    return hessian.reshape(layers, width, columns)


def solution(mesh):
    in_specs = (
        P("grp", None, "gx", Y),
        P("grp", "gx", Y),
        P("grp", "gx", Y),
        P("grp", None, "gx", Y),
        P("grp", None, "gx", Y),
        P(),
        P(),
        P("grp", None),
        P("grp"),
        P("grp", None),
    )
    return jax.shard_map(shards, mesh=mesh, in_specs=in_specs, out_specs=P("grp", "gx", Y), check_vma=False)
```

```python
import functools

import jax
import jax.numpy as jnp
from jax import lax
from jax.experimental import pallas as pl
from jax.experimental.pallas import tpu as pltpu
from jax.sharding import PartitionSpec as P

STEPS = 4
HALO = STEPS
RATE = 0.02
HALF_DT = 0.025
LANES = 128
TILE = 8
GROUP = 16
RIGHT = 64
Y = ("gy", "sa")
MIB = 1024 * 1024
PX, QX, BX, PY, QYM, QY, PYM, BY, BYM, D, KIND, KDIR = range(12)
KINDS = 12
VMEM = pl.BlockSpec(memory_space=pltpu.VMEM)
HBM = pl.BlockSpec(memory_space=pltpu.HBM)


def in_hbm(*arrays):
    return [pltpu.with_memory_space_constraint(a, pltpu.HBM) for a in arrays]


def lane_of(shape):
    return lax.broadcasted_iota(jnp.int32, shape, len(shape) - 1)


def roll(value, shift, axis):
    return pltpu.roll(value, shift % value.shape[axis], axis)


def pack_edges(fields):
    lane = lane_of(fields[0].shape)
    packed = jnp.zeros_like(fields[0])
    for f, field in enumerate(fields):
        packed = jnp.where(lane // GROUP == f, roll(field, 8 + GROUP * f, 1), packed)
    return packed


def y_after(value, strip, s):
    edge = roll(strip, LANES - 1 - (RIGHT + GROUP * s + 8), 1)
    return jnp.where(lane_of(value.shape) == LANES - 1, edge, roll(value, LANES - 1, 1))


def y_before(value, strip, s):
    edge = roll(strip, -(GROUP * s + 7), 1)
    return jnp.where(lane_of(value.shape) == 0, edge, roll(value, 1, 1))


def z_pair(value):
    tiles = [value[i : i + TILE] for i in range(0, value.shape[0], TILE)]
    row = lax.broadcasted_iota(jnp.int32, tiles[0].shape, 0)
    ups = [roll(t, TILE - 1, 0) for t in tiles]
    downs = [roll(t, 1, 0) for t in tiles]
    pairs = []
    for i, tile in enumerate(tiles):
        above = jnp.where(row == TILE - 1, ups[i + 1] if i + 1 < len(tiles) else tile, ups[i])
        below = jnp.where(row == 0, downs[i - 1] if i else tile, downs[i])
        pairs.append(above + below)
    return jnp.concatenate(pairs, axis=0)


def state_row(m, width):
    low, high = HALO + m, HALO + width - 1 - m

    def find(r):
        if low <= r <= high:
            return 0, r - HALO
        return (1, r - m) if r < low else (1, HALO + r - high - 1)

    return find


def coef_row(kind, width):
    low, high = HALO, HALO + width - 1
    if kind in (PX, QX, BX, D):
        high -= 1
    if kind == D:
        low += 1

    def find(r):
        if low <= r <= high:
            return 0, r - HALO
        return (1, r) if r <= HALO else (1, HALO + 1 + r - (HALO + width - 1))

    return find


def read_state(refs, m, width, r, s):
    which, index = state_row(m, width)(r)
    return refs[which][m, index, s]


def read_coef(refs, kind, width, r, i):
    which, index = coef_row(kind, width)(r)
    return refs[which][index, kind, i]


def pack_kernel(*refs, layers, width, species):
    sources, (f7_ref, e_ref, xa_ref, xb_ref), buffers, sem = refs[:5], refs[5:9], refs[9:14], refs[14]
    copies = [pltpu.make_async_copy(a, b, sem.at[i]) for i, (a, b) in enumerate(zip(sources, buffers))]
    for copy in copies:
        copy.start()
    for copy in copies:
        copy.wait()
    initial_ref, logk_ref, direction_ref, speed_ref, flags_ref = buffers
    plane = layers * width
    even = lax.rem(lax.axis_index("gx"), 2) == 0
    top, bottom = width - HALO, 0
    for x in range(width):

        def take(ref, index):
            return ref[pl.ds(index * plane + x, layers, stride=width), :]

        fields = [take(initial_ref, s) for s in range(species)]
        conductance = jnp.exp(take(logk_ref, 0))
        fields += [conductance, conductance * take(direction_ref, 0)]
        for axis in range(2):
            speed = take(speed_ref, axis)
            fields.append(jnp.where(take(flags_ref, axis) == 1, speed, -speed))
        for f, field in enumerate(fields):
            f7_ref[x, f] = field
        e_ref[x] = pack_edges(fields)
    count = species + 4
    start_a = jnp.where(even, top, bottom)
    start_b = jnp.where(even, bottom, top)
    for r in range(HALO):
        xa_ref[r, 0:count] = f7_ref[start_a + r]
        xb_ref[r, 0:count] = f7_ref[start_b + r]


def pack(initial, logk, direction, face_speed, face_flags):
    species, layers, width, _ = initial.shape
    f32 = jnp.float32
    sources = [a.reshape(-1, LANES) for a in (initial, logk, direction, face_speed, face_flags)]
    return pl.pallas_call(
        functools.partial(pack_kernel, layers=layers, width=width, species=species),
        out_shape=(
            jax.ShapeDtypeStruct((width, species + 4, layers, LANES), f32),
            jax.ShapeDtypeStruct((width, layers, LANES), f32),
            jax.ShapeDtypeStruct((HALO, species + 5, layers, LANES), f32),
            jax.ShapeDtypeStruct((HALO, species + 5, layers, LANES), f32),
        ),
        in_specs=[HBM] * 5,
        out_specs=[VMEM] * 4,
        scratch_shapes=[pltpu.VMEM(a.shape, a.dtype) for a in sources] + [pltpu.SemaphoreType.DMA((5,))],
        compiler_params=pltpu.CompilerParams(vmem_limit_bytes=5 * MIB),
        name="pack",
    )(*in_hbm(*sources))


def strips_kernel(ea_ref, eb_ref, xa_in, xb_in, xa_ref, xb_ref, buf_a, buf_b, sem_a, sem_b, *, width, count):
    even_x = lax.rem(lax.axis_index("gx"), 2) == 0
    even_y = lax.rem(lax.axis_index(Y), 2) == 0
    start_a = jnp.where(even_x, width - HALO, 0)
    start_b = jnp.where(even_x, 0, width - HALO)
    for r in range(HALO):
        for start, buf in ((start_a, buf_a), (start_b, buf_b)):
            one, two = ea_ref[start + r], eb_ref[start + r]
            from_left = lane_of(one.shape) % GROUP < 8
            buf[r] = jnp.where(from_left == even_y, two, one)
    copies = [
        pltpu.make_async_copy(buf_a, xa_ref.at[:, count], sem_a),
        pltpu.make_async_copy(buf_b, xb_ref.at[:, count], sem_b),
    ]
    for copy in copies:
        copy.start()
    for copy in copies:
        copy.wait()


def add_strips(ea, eb, xa, xb):
    width, layers, _ = ea.shape
    buffer = pltpu.VMEM((HALO, layers, LANES), jnp.float32)
    return pl.pallas_call(
        functools.partial(strips_kernel, width=width, count=xa.shape[1] - 1),
        out_shape=(jax.ShapeDtypeStruct(xa.shape, xa.dtype), jax.ShapeDtypeStruct(xb.shape, xb.dtype)),
        in_specs=[pl.BlockSpec(memory_space=pltpu.VMEM)] * 2 + [pl.BlockSpec(memory_space=pl.ANY)] * 2,
        out_specs=[pl.BlockSpec(memory_space=pl.ANY)] * 2,
        input_output_aliases={2: 0, 3: 1},
        scratch_shapes=[buffer, buffer, pltpu.SemaphoreType.DMA, pltpu.SemaphoreType.DMA],
        compiler_params=pltpu.CompilerParams(vmem_limit_bytes=2 * MIB),
        name="corner_strips",
    )(ea, eb, xa, xb)


def place(fields, own_edges, outer_edges, left, near, column, species):
    left_strip = jnp.where(near, outer_edges, own_edges)
    right_strip = jnp.where(near, own_edges, outer_edges)
    states = list(fields[:species]) + [jnp.where(left, left_strip, roll(right_strip, RIGHT, 1))]
    others = []
    for f in range(species, species + 4):
        index = GROUP * f + column
        strip = jnp.where(
            left,
            jnp.take_along_axis(left_strip, index, 1, mode="promise_in_bounds"),
            jnp.take_along_axis(right_strip, index, 1, mode="promise_in_bounds"),
        )
        others.append((fields[f], strip))
    return states, others


def y_coefs(k, kd, u, main_mask, strip_mask):
    half4 = HALF_DT * (k[1] + roll(k[1], 127, 1))
    p4 = (half4 + jnp.maximum(u[1], 0.0)) * strip_mask
    q4 = (half4 - jnp.minimum(u[1], 0.0)) * strip_mask
    b4 = HALF_DT * (kd[1] + roll(kd[1], 127, 1)) * strip_mask
    half = HALF_DT * (k[0] + y_after(k[0], k[1], 0))
    p = (half + jnp.maximum(u[0], 0.0)) * main_mask
    q = (half - jnp.minimum(u[0], 0.0)) * main_mask
    b = HALF_DT * (kd[0] + y_after(kd[0], kd[1], 0)) * main_mask
    return {
        PY: (p, p4),
        QY: (q, q4),
        BY: (b, b4),
        PYM: (y_before(p, p4, 0), roll(p4, 1, 1)),
        QYM: (y_before(q, q4, 0), roll(q4, 1, 1)),
        BYM: (y_before(b, b4, 0), roll(b4, 1, 1)),
    }


def x_coefs(k, k_next, kd, kd_next, u, mask):
    half = HALF_DT * (k + k_next)
    p = half + jnp.maximum(u, 0.0)
    q = half - jnp.minimum(u, 0.0)
    b = HALF_DT * (kd + kd_next)
    return (p, q, b) if mask is None else (p * mask, q * mask, b * mask)


def masks(layers):
    shape = (layers, LANES)
    lane = lane_of(shape)
    column = lane % GROUP
    near, left = column < 8, lane < RIGHT
    gy = lax.axis_index(Y)
    first_y, last_y = gy == 0, gy == lax.axis_size(Y) - 1
    strip_mask = jnp.where(
        left, jnp.where(first_y & near, 0.0, 1.0), jnp.where(last_y & (column >= 7), 0.0, 1.0)
    ).astype(jnp.float32)
    main_mask = jnp.where(last_y & (lane == LANES - 1), 0.0, 1.0).astype(jnp.float32)
    return column, near, left, main_mask, strip_mask


def step_row(r, m, rates, coef, state, tangent, put_c, put_t, put_jy):
    species = len(rates) - 1
    strips = state(r, species)
    strips_t = tangent(r, species) if m > 0 else None
    for s in (species,) + tuple(range(species)):
        i = 1 if s == species else 0
        kept = rates[s] - coef(D, r, i)
        upper, lower = coef(QX, r, i), coef(PX, r - 1, i)
        after, before = coef(QY, r, i), coef(PYM, r, i)

        def around(value, strip):
            if i:
                return roll(value, LANES - 1, 1), roll(value, 1, 1)
            return y_after(value, strip, s), y_before(value, strip, s)

        def moved(value, up, down, yp, ym):
            return kept * value + upper * up + lower * down + after * yp + before * ym + RATE * z_pair(value)

        c = strips if i else state(r, s)
        up, down = state(r + 1, s), state(r - 1, s)
        yp, ym = around(c, strips)
        jump = yp - c
        source = (
            coef(BX, r, i) * (up - c)
            - coef(BX, r - 1, i) * (c - down)
            + coef(BY, r, i) * jump
            - coef(BYM, r, i) * (c - ym)
        )
        put_jy(s, jump)
        if m + 1 < STEPS:
            put_c(s, moved(c, up, down, yp, ym))
        if m > 0:
            t = strips_t if i else tangent(r, s)
            tp, tm = around(t, strips_t)
            source = source + moved(t, tangent(r + 1, s), tangent(r - 1, s), tp, tm)
        put_t(s, source)


def strip_columns(wells):
    own = lax.broadcasted_iota(jnp.int32, (LANES, wells), 0)
    return own, own % RIGHT // GROUP, own % GROUP + jnp.where(own < RIGHT, -8, 120)


def divide(value, by):
    return lax.shift_right_logical(value, by.bit_length() - 1) if by & (by - 1) == 0 else lax.div(value, by)


def well_table(cells, counts, width):
    total_x, total_y = width * lax.axis_size("gx"), LANES * lax.axis_size(Y)
    start, second = cells[0:1], cells[1:2]
    depth = divide(start, total_x * total_y)
    rest = start - depth * (total_x * total_y)
    x = divide(rest, total_y)
    y = rest - x * total_y
    end = x + jnp.where(second > start, counts - 1, 1 - counts)
    row_start, col_start = lax.axis_index("gx") * width, lax.axis_index(Y) * LANES
    return [depth, jnp.minimum(x, end) - row_start, jnp.maximum(x, end) - row_start, y - col_start, counts]


def cone_kernel(
    retard_hbm, decay_hbm, cells_hbm, count_hbm, f7_ref, e_ref, ea_ref, eb_ref,
    coef_ref, c_ref, t_ref, jy_ref, mask_ref, hot_ref, rate_ref, meta_ref,
    retard_ref, decay_ref, cells_ref, count_ref, sem, *, layers, width, species,
):
    f32, bf16 = jnp.float32, jnp.bfloat16
    copies = [
        pltpu.make_async_copy(a, b, sem.at[i])
        for i, (a, b) in enumerate(
            ((retard_hbm, retard_ref), (decay_hbm, decay_ref), (cells_hbm, cells_ref), (count_hbm, count_ref))
        )
    ]
    for copy in copies:
        copy.start()
    column, near, left, main_mask, strip_mask = masks(layers)
    even_y = lax.rem(lax.axis_index(Y), 2) == 0
    count = species + 4
    kept = []
    for x in range(width):
        outer = jnp.where(near == even_y, eb_ref[x], ea_ref[x])
        states, (k, kd, ux, uy) = place(
            [f7_ref[x, f] for f in range(count)], e_ref[x], outer, left, near, column, species
        )
        for s in range(species + 1):
            c_ref[0, x, s] = states[s]
        found = y_coefs(k, kd, uy, main_mask, strip_mask)
        for kind, pair in found.items():
            coef_ref[x, kind, 0], coef_ref[x, kind, 1] = pair
        for i in range(2):
            coef_ref[x, KIND, i], coef_ref[x, KDIR, i] = k[i], kd[i]
            diagonal = found[PY][i] + found[QYM][i] + 2 * RATE
            if x:
                p, q, b = x_coefs(kept[0][i], k[i], kept[1][i], kd[i], kept[2][i], None)
                coef_ref[x - 1, PX, i], coef_ref[x - 1, QX, i], coef_ref[x - 1, BX, i] = p, q, b
                coef_ref[x - 1, D, i] = coef_ref[x - 1, D, i] + p
                diagonal = diagonal + q
            coef_ref[x, D, i] = diagonal
            if x == width - 1:
                coef_ref[x, PX, i] = ux[i]
        kept = (k, kd, ux)

    for copy in copies:
        copy.wait()
    lane = lane_of((1, LANES))
    strips = jnp.full((1, LANES), retard_ref[species - 1], f32)
    for s in range(species):
        rate = jnp.full((1, LANES), retard_ref[s], f32)
        strips = jnp.where(lane % RIGHT // GROUP == s, rate, strips)
        factor = jnp.exp(jnp.full((1, LANES), -decay_ref[s], f32)) / rate
        rate_ref[s : s + 1, :] = rate
        rate_ref[species + 1 + s : species + 2 + s, :] = factor**STEPS
    rate_ref[species : species + 1, :] = strips

    rates = [rate_ref[s : s + 1, :] for s in range(species + 1)]
    for m in range(STEPS):
        for r in range(HALO + 1 + m, HALO + width - 1 - m):
            x = r - HALO

            def put(ref, slot):
                def store(s, value):
                    ref[slot, x, s] = value

                return store

            step_row(
                r, m, rates,
                lambda kind, r, i: coef_ref[r - HALO, kind, i],
                lambda r, s: c_ref[m, r - HALO, s],
                lambda r, s: t_ref[m - 1, r - HALO, s],
                put(c_ref, m + 1), put(t_ref, m), put(jy_ref, m),
            )

    wells = meta_ref.shape[1]
    cells = cells_ref[...]
    cells = jnp.concatenate([cells, jnp.zeros((wells, LANES - cells.shape[1]), jnp.int32)], axis=1)
    table = well_table(cells.T, count_ref[...].reshape(1, wells), width)
    for i, row in enumerate(table):
        meta_ref[i : i + 1, :] = row
    depth, first, last, where_y = table[:4]
    in_layer = lax.broadcasted_iota(jnp.int32, (layers, wells), 0) == depth
    for r in range(width + 2 * HALO):
        inside = (first <= r - HALO) & (last >= r - HALO) & in_layer
        mask_ref[r * layers : (r + 1) * layers, :] = jnp.where(inside, 1.0, 0.0).astype(bf16)
    own, strip_species, strip_column = strip_columns(wells)
    hit = ((strip_column < 0) | (strip_column >= LANES)) & (strip_column == where_y)
    for s in range(species):
        hot_ref[s, 0:LANES] = jnp.where(own == where_y, 1.0, 0.0).astype(bf16)
        hot_ref[s, LANES : 2 * LANES] = jnp.where(hit & (strip_species == s), 1.0, 0.0).astype(bf16)


def cone(retard, decay, cells, counts, f7, e, ea, eb):
    width, count, layers, _ = f7.shape
    species, wells = count - 4, counts.shape[0]
    f32, i32 = jnp.float32, jnp.int32
    state = jax.ShapeDtypeStruct((STEPS, width, species + 1, layers, LANES), f32)
    return pl.pallas_call(
        functools.partial(cone_kernel, layers=layers, width=width, species=species),
        out_shape=(
            jax.ShapeDtypeStruct((width, KINDS, 2, layers, LANES), f32),
            state,
            state,
            state,
            jax.ShapeDtypeStruct(((width + 2 * HALO) * layers, wells), jnp.bfloat16),
            jax.ShapeDtypeStruct((species, 2 * LANES, wells), jnp.bfloat16),
            jax.ShapeDtypeStruct((2 * species + 2, LANES), f32),
            jax.ShapeDtypeStruct((TILE, wells), i32),
        ),
        in_specs=[HBM] * 4 + [VMEM] * 4,
        out_specs=[VMEM] * 8,
        scratch_shapes=[
            pltpu.SMEM(retard.shape, f32),
            pltpu.SMEM(decay.shape, f32),
            pltpu.VMEM(cells.shape, i32),
            pltpu.VMEM(counts.shape, i32),
            pltpu.SemaphoreType.DMA((4,)),
        ],
        compiler_params=pltpu.CompilerParams(vmem_limit_bytes=4 * MIB),
        cost_estimate=pl.CostEstimate(flops=10**7, bytes_accessed=10**7, transcendentals=0),
        name="cone_steps",
    )(*in_hbm(retard, decay, cells, counts), f7, e, ea, eb)


def rim_kernel(
    rate_ref, xa_ref, xb_ref, coef_in, c_in, t_in, mask_ref, hot_ref,
    partial_ref, coef_out, c_out, jy_out, t_out, *, layers, width, species,
):
    f32, bf16 = jnp.float32, jnp.bfloat16
    column, near, left, main_mask, strip_mask = masks(layers)
    gx = lax.axis_index("gx")
    even_x = lax.rem(gx, 2) == 0
    count = species + 4
    rows = width + 2 * HALO
    coefs = (coef_in, coef_out)

    def put_coef(kind, r, i, value):
        which, index = coef_row(kind, width)(r)
        coefs[which][index, kind, i] = value

    speeds = {}
    for r in list(range(HALO)) + list(range(HALO + width, rows)):
        from_a = even_x if r > HALO else jnp.logical_not(even_x)
        both = [jnp.where(from_a, xa_ref[r % (HALO + width), f], xb_ref[r % (HALO + width), f]) for f in range(count + 1)]
        states, (k, kd, ux, uy) = place(
            both[:count], pack_edges(both[:count]), both[count], left, near, column, species
        )
        index = state_row(0, width)(r)[1]
        for s in range(species + 1):
            c_out[0, index, s] = states[s]
        for kind, pair in y_coefs(k, kd, uy, main_mask, strip_mask).items():
            for i in range(2):
                put_coef(kind, r, i, pair[i])
        for i in range(2):
            put_coef(KIND, r, i, k[i])
            put_coef(KDIR, r, i, kd[i])
        speeds[r] = ux
    last = HALO + width - 1
    speeds[last] = [coef_in[width - 1, PX, i] for i in range(2)]
    inside_low = jnp.where(gx > 0, 1.0, 0.0).astype(f32)
    inside_high = jnp.where(gx < lax.axis_size("gx") - 1, 1.0, 0.0).astype(f32)
    get = lambda kind, r, i: read_coef(coefs, kind, width, r, i)
    for r in list(range(HALO)) + list(range(last, rows - 1)):
        for i in range(2):
            p, q, b = x_coefs(
                get(KIND, r, i), get(KIND, r + 1, i), get(KDIR, r, i), get(KDIR, r + 1, i), speeds[r][i],
                inside_low if r < HALO else inside_high,
            )
            put_coef(PX, r, i, p)
            put_coef(QX, r, i, q)
            put_coef(BX, r, i, b)
    for r in list(range(1, HALO + 1)) + list(range(last, rows - 1)):
        for i in range(2):
            if r == HALO:
                value = coef_in[0, D, i] + get(QX, r - 1, i)
            elif r == last:
                value = coef_in[width - 1, D, i] + get(PX, r, i)
            else:
                value = get(PY, r, i) + get(QYM, r, i) + 2 * RATE + get(PX, r, i) + get(QX, r - 1, i)
            put_coef(D, r, i, value)

    rates = [rate_ref[s : s + 1, :] for s in range(species + 1)]
    for m in range(STEPS):
        for r in list(range(1 + m, HALO + 1 + m)) + list(range(last - m, rows - 1 - m)):
            index = state_row(m + 1, width)(r)[1]

            def put(ref, slot):
                def store(s, value):
                    ref[slot, index, s] = value

                return store

            step_row(
                r, m, rates, get,
                lambda r, s: read_state((c_in, c_out), m, width, r, s),
                lambda r, s: tangent_row(t_in, t_out, m, width, r)[s],
                put(c_out, m + 1), put(t_out, m), put(jy_out, m),
            )

    wells = mask_ref.shape[1]
    for s in range(species):
        total = jnp.zeros((layers, wells), f32)
        for half in range(2):
            span = range(HALO + half * width // 2, HALO + (half + 1) * width // 2)
            both = jnp.concatenate(
                [
                    jnp.concatenate([tangent_row(t_in, t_out, STEPS, width, r)[p] for r in span], axis=0)
                    for p in (s, species)
                ],
                axis=1,
            )
            picked = jnp.zeros((len(span) * layers, wells), f32)
            for piece in range(3):
                coarse = both.astype(bf16)
                picked = picked + jnp.dot(coarse, hot_ref[s], preferred_element_type=f32)
                both = both - coarse.astype(f32)
            picked = picked * mask_ref[span[0] * layers : (span[-1] + 1) * layers, :].astype(f32)
            for x in range(len(span)):
                total = total + picked[x * layers : (x + 1) * layers]
        partial_ref[s : s + 1, :] = jnp.sum(total, axis=0, keepdims=True)


def tangent_row(t_in, t_out, m, width, r):
    which, index = state_row(m, width)(r)
    return (t_in, t_out)[which].at[m - 1, index]


def rim(rates, xa, xb, coef, c, t, mask, hot):
    _, width, planes, layers, _ = c.shape
    species, wells = planes - 1, mask.shape[1]
    f32 = jnp.float32
    state = (STEPS, 2 * HALO, planes, layers, LANES)
    return pl.pallas_call(
        functools.partial(rim_kernel, layers=layers, width=width, species=species),
        out_shape=(
            jax.ShapeDtypeStruct((species, wells), f32),
            jax.ShapeDtypeStruct((2 * HALO + 2, KINDS, 2, layers, LANES), f32),
            jax.ShapeDtypeStruct(state, f32),
            jax.ShapeDtypeStruct(state, f32),
        ),
        in_specs=[VMEM] * 8,
        out_specs=[VMEM] * 4,
        scratch_shapes=[pltpu.VMEM(state, f32)],
        compiler_params=pltpu.CompilerParams(vmem_limit_bytes=8 * MIB),
        name="rim_steps",
    )(rates, xa, xb, coef, c, t, mask, hot)


def adjoint_kernel(
    rate_ref, weight_ref, meta_ref, coef_in, coef_out, c_in, c_out, jy_in, jy_out, mask_ref, partial_ref, *rest,
    layers, width, species, parts,
):
    others, out_ref, lam_ref = rest[:parts], *rest[parts:]
    f32, bf16 = jnp.float32, jnp.bfloat16
    rows = width + 2 * HALO
    shape = (layers, LANES)
    lane = lane_of(shape)
    gx, gy = lax.axis_index("gx"), lax.axis_index(Y)
    where_y = meta_ref[3:4, :]
    counts = meta_ref[4:5, :].astype(f32)
    wells = meta_ref.shape[1]
    coefs, states = (coef_in, coef_out), (c_in, c_out)
    coef = lambda kind, r, i: read_coef(coefs, kind, width, r, i)

    own, strip_species, strip_column = strip_columns(wells)
    strip_hit, own_hit = strip_column == where_y, own == where_y
    residuals = []
    for s in range(species):
        total = partial_ref[s : s + 1, :]
        for other in others:
            total = total + other[s : s + 1, :]
        factor = rate_ref[species + 1 + s, 0:1][:, None]
        residual = weight_ref[s : s + 1, :] * (total * factor) / counts
        residuals.append(residual / counts * factor)
    lam = jnp.zeros((rows * layers, (species + 1) * LANES), f32)
    for piece in range(3):
        coarse = [r.astype(bf16).astype(f32) for r in residuals]
        residuals = [r - q for r, q in zip(residuals, coarse)]
        blocks = [jnp.where(own_hit, q, 0.0).astype(bf16) for q in coarse]
        side = jnp.zeros((LANES, wells), f32)
        for s in range(species):
            side = jnp.where(strip_hit & (strip_species == s), coarse[s], side)
        spread = jnp.concatenate(blocks + [side.astype(bf16)], axis=0)
        lam = lam + lax.dot_general(mask_ref[...], spread, (((1,), (1,)), ((), ())), preferred_element_type=f32)
    for s in range(species + 1):
        lam_ref[0, :, s] = lam[:, s * LANES : (s + 1) * LANES].reshape(rows, layers, LANES)

    rates = [rate_ref[s : s + 1, :] for s in range(species + 1)]
    first_row, last_row = HALO - 1, HALO + width - 1
    sums_x, sums_y, sums_side = {}, {}, {}
    for m in reversed(range(STEPS)):
        now = STEPS - 1 - m
        low, high = STEPS - m, rows - 1 - (STEPS - m)
        for r in range(min(low, first_row), max(high, last_row) + 1):
            sense, retreat = first_row <= r <= last_row, m > 0 and low <= r <= high
            strip = lam_ref[now, r, species]
            along_x = along_y = side = None
            for s in range(species + 1):
                i = 1 if s == species else 0
                value = strip if i else lam_ref[now, r, s]
                up = lam_ref[now, r + 1, s]
                yp = roll(value, LANES - 1, 1) if i else y_after(value, strip, s)
                if sense:
                    if not i:
                        jump = read_state(states, m, width, r + 1, s) - read_state(states, m, width, r, s)
                        term = jump * (up - value)
                        along_x = term if along_x is None else along_x + term
                    if r >= HALO:
                        which, index = state_row(m + 1, width)(r)
                        term = (jy_in, jy_out)[which][m, index, s] * (yp - value)
                        if i:
                            side = term
                        else:
                            along_y = term if along_y is None else along_y + term
                if retreat:
                    ym = roll(value, 1, 1) if i else y_before(value, strip, s)
                    lam_ref[now + 1, r, s] = (
                        (rates[s] - coef(D, r, i)) * value
                        + coef(PX, r, i) * up
                        + coef(QX, r - 1, i) * lam_ref[now, r - 1, s]
                        + coef(PY, r, i) * yp
                        + coef(QYM, r, i) * ym
                        + RATE * z_pair(value)
                    )
            if sense:
                for store, term in ((sums_x, along_x), (sums_y, along_y), (sums_side, side)):
                    if term is not None:
                        store[r] = store[r] + term if r in store else term

    main_mask = jnp.where((gy == lax.axis_size(Y) - 1) & (lane == LANES - 1), 0.0, 1.0).astype(f32)
    side_mask = jnp.where((gy == 0) & (lane == 0), 0.0, 1.0).astype(f32)
    for x in range(width):
        r = x + HALO
        upper, lower = sums_x[r], sums_x[r - 1]
        if x == 0:
            lower = lower * jnp.where(gx > 0, 1.0, 0.0).astype(f32)
        if x == width - 1:
            upper = upper * jnp.where(gx < lax.axis_size("gx") - 1, 1.0, 0.0).astype(f32)
        along_y, strip = sums_y[r] * main_mask, sums_side[r]
        side = roll(strip, -7, 1)
        for s in range(1, species):
            side = side + roll(strip, -(GROUP * s + 7), 1)
        before = jnp.where(lane == 0, side * side_mask, roll(along_y, 1, 1))
        out_ref[pl.ds(x, layers, stride=width), :] = -HALF_DT * coef(KIND, r, 0) * (upper + lower + along_y + before)


def adjoint(rates, weight, meta, coef_in, coef_out, c_in, c_out, jy_in, jy_out, mask, partials):
    _, width, planes, layers, _ = c_in.shape
    species = planes - 1
    parts = len(partials) - 1
    return pl.pallas_call(
        functools.partial(adjoint_kernel, layers=layers, width=width, species=species, parts=parts),
        out_shape=jax.ShapeDtypeStruct((layers * width, LANES), jnp.float32),
        in_specs=[VMEM] * (10 + len(partials)),
        out_specs=VMEM,
        scratch_shapes=[pltpu.VMEM((STEPS, width + 2 * HALO, planes, layers, LANES), jnp.float32)],
        compiler_params=pltpu.CompilerParams(vmem_limit_bytes=12 * MIB),
        name="adjoint_steps",
    )(rates, weight, meta, coef_in, coef_out, c_in, c_out, jy_in, jy_out, mask, *partials)


def swaps(first, second, axis):
    count = lax.axis_size(axis)
    even = [p for i in range(0, count - 1, 2) for p in ((i, i + 1), (i + 1, i))]
    odd = [p for i in range(1, count - 1, 2) for p in ((i, i + 1), (i + 1, i))]
    return lax.ppermute(first, axis, even), lax.ppermute(second, axis, odd)


def from_others(value, axis, reach):
    count = lax.axis_size(axis)
    if count in (2, 4):
        return [lax.ppermute(value, axis, [(i, i ^ d) for i in range(count)]) for d in range(1, count)]
    return [
        lax.ppermute(value, axis, [(i, i + d) for i in range(count) if 0 <= i + d < count])
        for distance in range(1, min(reach, count - 1) + 1)
        for d in (distance, -distance)
    ]


def shards(
    initial, logk, direction, face_speed, face_flags, retard, decay, screen_cells, screen_count, well_weight
):
    species, layers, width, columns = initial.shape
    f7, e, xa, xb = pack(initial, logk, direction, face_speed, face_flags)
    ea, eb = swaps(e, e, Y)
    xa, xb = add_strips(ea, eb, xa, xb)
    xa, xb = swaps(xa, xb, "gx")
    coef_in, c_in, t_in, jy_in, mask, hot, rates, meta = cone(
        retard, decay, screen_cells, screen_count, f7, e, ea, eb
    )
    partial, coef_out, c_out, jy_out = rim(rates, xa, xb, coef_in, c_in, t_in, mask, hot)
    reach = -(-(screen_cells.shape[1] - 1 + HALO) // width)
    partials = [partial] + from_others(partial, "gx", reach)
    hessian = adjoint(
        rates, well_weight, meta, coef_in, coef_out, c_in, c_out, jy_in, jy_out, mask, partials
    )
    return hessian.reshape(layers, width, columns)


def solution(mesh):
    in_specs = (
        P("grp", None, "gx", Y),
        P("grp", "gx", Y),
        P("grp", "gx", Y),
        P("grp", None, "gx", Y),
        P("grp", None, "gx", Y),
        P(),
        P(),
        P("grp", None),
        P("grp"),
        P("grp", None),
    )
    return jax.shard_map(shards, mesh=mesh, in_specs=in_specs, out_specs=P("grp", "gx", Y), check_vma=False)
```

```python
import functools

import jax
import jax.numpy as jnp
from jax import lax
from jax.experimental import pallas as pl
from jax.experimental.pallas import tpu as pltpu
from jax.sharding import PartitionSpec as P

STEPS = 4
HALO = STEPS
RATE = 0.02
HALF_DT = 0.025
LANES = 128
TILE = 8
GROUP = 16
RIGHT = 64
Y = ("gy", "sa")
MIB = 1024 * 1024
PX, QX, BX, PY, QYM, QY, PYM, BY, BYM, D, K, KDIR = range(12)
KINDS = 12
VMEM = pl.BlockSpec(memory_space=pltpu.VMEM)
HBM = pl.BlockSpec(memory_space=pltpu.HBM)
F32, BF16, I32 = jnp.float32, jnp.bfloat16, jnp.int32


def in_hbm(*arrays):
    return [pltpu.with_memory_space_constraint(a, pltpu.HBM) for a in arrays]


def lane_of(shape):
    return lax.broadcasted_iota(I32, shape, len(shape) - 1)


def roll(value, shift, axis):
    return pltpu.roll(value, shift % value.shape[axis], axis)


def y_next(value):
    return roll(value, LANES - 1, 1)


def y_previous(value):
    return roll(value, 1, 1)


def pack_edges(fields):
    lane = lane_of(fields[0].shape)
    packed = jnp.zeros_like(fields[0])
    for f, field in enumerate(fields):
        packed = jnp.where(lane // GROUP == f, roll(field, 8 + GROUP * f, 1), packed)
    return packed


def z_pair(value):
    tiles = [value[i : i + TILE] for i in range(0, value.shape[0], TILE)]
    row = lax.broadcasted_iota(I32, tiles[0].shape, 0)
    ups = [roll(t, TILE - 1, 0) for t in tiles]
    downs = [roll(t, 1, 0) for t in tiles]
    pairs = []
    for i, tile in enumerate(tiles):
        above = jnp.where(row == TILE - 1, ups[i + 1] if i + 1 < len(tiles) else tile, ups[i])
        below = jnp.where(row == 0, downs[i - 1] if i else tile, downs[i])
        pairs.append(above + below)
    return jnp.concatenate(pairs, axis=0)


def state_row(m, width):
    low, high = HALO + m, HALO + width - 1 - m

    def find(r):
        if low <= r <= high:
            return 0, r - HALO
        return (1, r - m) if r < low else (1, HALO + r - high - 1)

    return find


def coef_row(kind, width):
    low, high = HALO, HALO + width - 1
    if kind in (PX, QX, BX, D):
        high -= 1
    if kind == D:
        low += 1

    def find(r):
        if low <= r <= high:
            return 0, r - HALO
        return (1, r) if r <= HALO else (1, HALO + 1 + r - (HALO + width - 1))

    return find


def read_state(refs, m, width, r, s):
    which, index = state_row(m, width)(r)
    return refs[which][m, index, s]


def read_coef(refs, kind, width, r):
    which, index = coef_row(kind, width)(r)
    return refs[which][index, kind]


def row_fields(raw, x, layers, width, species):
    initial_ref, logk_ref, direction_ref, speed_ref, flags_ref = raw
    plane = layers * width

    def take(ref, index):
        return ref[pl.ds(index * plane + x, layers, stride=width), :]

    fields = [take(initial_ref, s) for s in range(species)]
    conductance = jnp.exp(take(logk_ref, 0))
    fields += [conductance, conductance * take(direction_ref, 0)]
    for axis in range(2):
        speed = take(speed_ref, axis)
        fields.append(jnp.where(take(flags_ref, axis) == 1, speed, -speed))
    return fields


def y_coefs(k, kd, u, mask=None):
    half = HALF_DT * (k + y_next(k))
    p = half + jnp.maximum(u, 0.0)
    q = half - jnp.minimum(u, 0.0)
    b = HALF_DT * (kd + y_next(kd))
    if mask is not None:
        p, q, b = p * mask, q * mask, b * mask
    return {PY: p, QY: q, BY: b, PYM: y_previous(p), QYM: y_previous(q), BYM: y_previous(b), K: k, KDIR: kd}


def x_coefs(k, k_next, kd, kd_next, u, mask=None):
    half = HALF_DT * (k + k_next)
    p = half + jnp.maximum(u, 0.0)
    q = half - jnp.minimum(u, 0.0)
    b = HALF_DT * (kd + kd_next)
    return (p, q, b) if mask is None else (p * mask, q * mask, b * mask)


def step_cell(r, m, s, rate, coef, state, tangent, put_c, put_t, put_jy):
    kept = rate - coef(D, r)
    upper, lower = coef(QX, r), coef(PX, r - 1)
    after, before = coef(QY, r), coef(PYM, r)

    def moved(value, up, down, yp, ym):
        return kept * value + upper * up + lower * down + after * yp + before * ym + RATE * z_pair(value)

    c, up, down = state(r, s), state(r + 1, s), state(r - 1, s)
    yp, ym = y_next(c), y_previous(c)
    jump = yp - c
    source = (
        coef(BX, r) * (up - c) - coef(BX, r - 1) * (c - down) + coef(BY, r) * jump - coef(BYM, r) * (c - ym)
    )
    put_jy(s, jump)
    if m + 1 < STEPS:
        put_c(s, moved(c, up, down, yp, ym))
    if m > 0:
        t = tangent(r, s)
        source = source + moved(t, tangent(r + 1, s), tangent(r - 1, s), y_next(t), y_previous(t))
    put_t(s, source)


def put_at(ref, m, index):
    def store(s, value):
        ref[m, index, s] = value

    return store


def picked_sums(wide, hot, masks, layers):
    picked = jnp.zeros((wide.shape[0], hot.shape[1]), F32)
    for piece in range(3):
        coarse = wide.astype(BF16)
        picked = picked + jnp.dot(coarse, hot, preferred_element_type=F32)
        wide = wide - coarse.astype(F32)
    wells = masks.shape[1]
    totals = []
    for s in range(hot.shape[1] // wells):
        total = jnp.zeros((layers, wells), F32)
        for i in range(0, wide.shape[0], layers):
            total = total + picked[i : i + layers, s * wells : (s + 1) * wells] * masks[i : i + layers].astype(F32)
        totals.append(jnp.sum(total, axis=0, keepdims=True))
    return totals


def send_kernel(*refs, layers, width, species):
    sources, raw, (xa_ref, xb_ref, sem) = refs[:5], refs[5:10], refs[10:]
    copies = [pltpu.make_async_copy(a, b, sem.at[i]) for i, (a, b) in enumerate(zip(sources, raw))]
    for copy in copies:
        copy.start()
    for copy in copies:
        copy.wait()
    even = lax.rem(lax.axis_index("gx"), 2) == 0
    for r in range(HALO):
        bottom = row_fields(raw, r, layers, width, species)
        top = row_fields(raw, width - HALO + r, layers, width, species)
        for f in range(species + 4):
            xa_ref[r, f] = jnp.where(even, top[f], bottom[f])
            xb_ref[r, f] = jnp.where(even, bottom[f], top[f])


def send_rows(initial, logk, direction, face_speed, face_flags):
    species, layers, width, _ = initial.shape
    sources = [a.reshape(-1, LANES) for a in (initial, logk, direction, face_speed, face_flags)]
    rows = jax.ShapeDtypeStruct((HALO, species + 4, layers, LANES), F32)
    *raw, xa, xb = pl.pallas_call(
        functools.partial(send_kernel, layers=layers, width=width, species=species),
        out_shape=tuple(jax.ShapeDtypeStruct(a.shape, a.dtype) for a in sources) + (rows, rows),
        in_specs=[HBM] * 5,
        out_specs=[VMEM] * 7,
        scratch_shapes=[pltpu.SemaphoreType.DMA((5,))],
        compiler_params=pltpu.CompilerParams(vmem_limit_bytes=3 * MIB),
        name="send_rows",
    )(*in_hbm(*sources))
    return raw, xa, xb


def divide(value, by):
    return lax.shift_right_logical(value, by.bit_length() - 1) if by & (by - 1) == 0 else lax.div(value, by)


def well_table(cells, counts, width):
    total_x, total_y = width * lax.axis_size("gx"), LANES * lax.axis_size(Y)
    start, second = cells[0:1], cells[1:2]
    depth = divide(start, total_x * total_y)
    rest = start - depth * (total_x * total_y)
    x = divide(rest, total_y)
    y = rest - x * total_y
    end = x + jnp.where(second > start, counts - 1, 1 - counts)
    row_start, col_start = lax.axis_index("gx") * width, lax.axis_index(Y) * LANES
    return [depth, jnp.minimum(x, end) - row_start, jnp.maximum(x, end) - row_start, y - col_start, counts]


def strip_columns(wells):
    own = lax.broadcasted_iota(I32, (LANES, wells), 0)
    return own, own % RIGHT // GROUP, own % GROUP + jnp.where(own < RIGHT, -8, 120)


def cone_kernel(
    retard_hbm, decay_hbm, cells_hbm, count_hbm, initial_ref, logk_ref, direction_ref, speed_ref, flags_ref,
    coef_ref, c_ref, t_ref, jy_ref, e_ref, mask_ref, hot_ref, side_hot_ref, rate_ref, meta_ref,
    retard_ref, decay_ref, cells_ref, count_ref, sem, *, layers, width, species,
):
    copies = [
        pltpu.make_async_copy(a, b, sem.at[i])
        for i, (a, b) in enumerate(
            ((retard_hbm, retard_ref), (decay_hbm, decay_ref), (cells_hbm, cells_ref), (count_hbm, count_ref))
        )
    ]
    for copy in copies:
        copy.start()
    raw = initial_ref, logk_ref, direction_ref, speed_ref, flags_ref
    kept = None
    for x in range(width):
        fields = row_fields(raw, x, layers, width, species)
        k, kd, ux, uy = fields[species:]
        e_ref[x] = pack_edges(fields)
        for s in range(species):
            c_ref[0, x, s] = fields[s]
        found = y_coefs(k, kd, uy)
        for kind, value in found.items():
            coef_ref[x, kind] = value
        diagonal = found[PY] + found[QYM] + 2 * RATE
        if x:
            p, q, b = x_coefs(kept[0], k, kept[1], kd, kept[2])
            coef_ref[x - 1, PX], coef_ref[x - 1, QX], coef_ref[x - 1, BX] = p, q, b
            coef_ref[x - 1, D] = kept[3] + p
            diagonal = diagonal + q
        kept = (k, kd, ux, diagonal)
    coef_ref[width - 1, D] = kept[3]
    coef_ref[width - 1, PX] = kept[2]

    for copy in copies:
        copy.wait()
    lane = lane_of((1, LANES))
    strips = jnp.full((1, LANES), retard_ref[species - 1], F32)
    rates = []
    for s in range(species):
        rate = jnp.full((1, LANES), retard_ref[s], F32)
        strips = jnp.where(lane % RIGHT // GROUP == s, rate, strips)
        factor = jnp.exp(jnp.full((1, LANES), -decay_ref[s], F32)) / rate
        rate_ref[s : s + 1, :] = rate
        rate_ref[species + 1 + s : species + 2 + s, :] = factor**STEPS
        rates.append(rate)
    rate_ref[species : species + 1, :] = strips

    for m in range(STEPS):
        for r in range(HALO + 1 + m, HALO + width - 1 - m):
            x = r - HALO
            for s in range(species):
                step_cell(
                    r, m, s, rates[s],
                    lambda kind, r: coef_ref[r - HALO, kind],
                    lambda r, s: c_ref[m, r - HALO, s],
                    lambda r, s: t_ref[m - 1, r - HALO, s],
                    put_at(c_ref, m + 1, x), put_at(t_ref, m, x), put_at(jy_ref, m, x),
                )

    wells = meta_ref.shape[1]
    table = well_table(cells_ref, count_ref[...].reshape(1, wells), width)
    for i, row in enumerate(table):
        meta_ref[i : i + 1, :] = row
    depth, first, last, where_y = table[:4]
    in_layer = lax.broadcasted_iota(I32, (layers, wells), 0) == depth
    for r in range(width + 2 * HALO):
        inside = (first <= r - HALO) & (last >= r - HALO) & in_layer
        mask_ref[r * layers : (r + 1) * layers, :] = jnp.where(inside, 1.0, 0.0).astype(BF16)
    own, strip_species, strip_column = strip_columns(wells)
    hit = (own == where_y) & (own >= STEPS) & (own < LANES - STEPS)
    hot_ref[...] = jnp.where(hit, 1.0, 0.0).astype(BF16)
    reach = (strip_column < STEPS) & (strip_column >= -HALO)
    reach = reach | ((strip_column >= LANES - STEPS) & (strip_column < LANES + HALO))
    hit = reach & (strip_column == where_y)
    for s in range(species):
        side_hot_ref[:, s * wells : (s + 1) * wells] = jnp.where(hit & (strip_species == s), 1.0, 0.0).astype(BF16)


def cone(retard, decay, cells, counts, raw, layers, width, species):
    wells = counts.shape[0]
    state = jax.ShapeDtypeStruct((STEPS, width, species, layers, LANES), F32)
    return pl.pallas_call(
        functools.partial(cone_kernel, layers=layers, width=width, species=species),
        out_shape=(
            jax.ShapeDtypeStruct((width, KINDS, layers, LANES), F32),
            state,
            state,
            state,
            jax.ShapeDtypeStruct((width, layers, LANES), F32),
            jax.ShapeDtypeStruct(((width + 2 * HALO) * layers, wells), BF16),
            jax.ShapeDtypeStruct((LANES, wells), BF16),
            jax.ShapeDtypeStruct((LANES, species * wells), BF16),
            jax.ShapeDtypeStruct((2 * species + 2, LANES), F32),
            jax.ShapeDtypeStruct((TILE, wells), I32),
        ),
        in_specs=[HBM] * 4 + [VMEM] * 5,
        out_specs=[VMEM] * 10,
        scratch_shapes=[
            pltpu.SMEM(retard.shape, F32),
            pltpu.SMEM(decay.shape, F32),
            pltpu.VMEM(cells.shape, I32),
            pltpu.VMEM(counts.shape, I32),
            pltpu.SemaphoreType.DMA((4,)),
        ],
        compiler_params=pltpu.CompilerParams(vmem_limit_bytes=4 * MIB),
        cost_estimate=pl.CostEstimate(flops=10**7, bytes_accessed=10**7, transcendentals=0),
        name="cone_steps",
    )(*in_hbm(retard, decay, cells, counts), *raw)


def neighbour_row(r, a_ref, b_ref, width):
    even = lax.rem(lax.axis_index("gx"), 2) == 0
    from_a = even if r >= HALO else jnp.logical_not(even)
    index = r % (HALO + width)
    return [jnp.where(from_a, a_ref[index, f], b_ref[index, f]) for f in range(a_ref.shape[1])]


def edges_kernel(e_ref, xa_ref, xb_ref, out_ref, *, width):
    out_ref[HALO : HALO + width] = e_ref[...]
    for r in list(range(HALO)) + list(range(HALO + width, 2 * HALO + width)):
        out_ref[r] = pack_edges(neighbour_row(r, xa_ref, xb_ref, width))


def all_edges(e, xa, xb):
    width, layers, _ = e.shape
    return pl.pallas_call(
        functools.partial(edges_kernel, width=width),
        out_shape=jax.ShapeDtypeStruct((width + 2 * HALO, layers, LANES), F32),
        in_specs=[VMEM] * 3,
        out_specs=VMEM,
        compiler_params=pltpu.CompilerParams(vmem_limit_bytes=1 * MIB),
        name="edge_columns",
    )(e, xa, xb)


def rim_kernel(
    rate_ref, xa_ref, xb_ref, coef_in, c_in, t_in, mask_ref, hot_ref,
    partial_ref, coef_out, c_out, jy_out, t_out, *, layers, width, species,
):
    gx = lax.axis_index("gx")
    rows = width + 2 * HALO
    coefs = (coef_in, coef_out)
    last = HALO + width - 1
    get = lambda kind, r: read_coef(coefs, kind, width, r)

    def put_coef(kind, r, value):
        which, index = coef_row(kind, width)(r)
        coefs[which][index, kind] = value

    speeds = {last: coef_in[width - 1, PX]}
    for r in list(range(HALO)) + list(range(HALO + width, rows)):
        fields = neighbour_row(r, xa_ref, xb_ref, width)
        k, kd, speeds[r], uy = fields[species:]
        index = state_row(0, width)(r)[1]
        for s in range(species):
            c_out[0, index, s] = fields[s]
        for kind, value in y_coefs(k, kd, uy).items():
            put_coef(kind, r, value)
    inside_low = jnp.where(gx > 0, 1.0, 0.0).astype(F32)
    inside_high = jnp.where(gx < lax.axis_size("gx") - 1, 1.0, 0.0).astype(F32)
    for r in list(range(HALO)) + list(range(last, rows - 1)):
        mask = inside_low if r < HALO else inside_high
        values = x_coefs(get(K, r), get(K, r + 1), get(KDIR, r), get(KDIR, r + 1), speeds[r], mask)
        for kind, value in zip((PX, QX, BX), values):
            put_coef(kind, r, value)
    for r in list(range(1, HALO + 1)) + list(range(last, rows - 1)):
        if r == HALO:
            value = coef_in[0, D] + get(QX, r - 1)
        elif r == last:
            value = coef_in[width - 1, D] + get(PX, r)
        else:
            value = get(PY, r) + get(QYM, r) + 2 * RATE + get(PX, r) + get(QX, r - 1)
        put_coef(D, r, value)

    for m in range(STEPS):
        for r in list(range(1 + m, HALO + 1 + m)) + list(range(last - m, rows - 1 - m)):
            index = state_row(m + 1, width)(r)[1]
            for s in range(species):
                step_cell(
                    r, m, s, rate_ref[s : s + 1, :], get,
                    lambda r, s: read_state((c_in, c_out), m, width, r, s),
                    lambda r, s: tangent_row(t_in, t_out, m, width, r)[s],
                    put_at(c_out, m + 1, index), put_at(t_out, m, index), put_at(jy_out, m, index),
                )

    masks = mask_ref[HALO * layers : (HALO + width) * layers, :]
    for s in range(species):
        block = [tangent_row(t_in, t_out, STEPS, width, r)[s] for r in range(HALO, HALO + width)]
        partial_ref[s : s + 1, :] = picked_sums(jnp.concatenate(block, axis=0), hot_ref[...], masks, layers)[0]


def tangent_row(t_in, t_out, m, width, r):
    which, index = state_row(m, width)(r)
    return (t_in, t_out)[which].at[m - 1, index]


def rim(rates, xa, xb, coef, c, t, mask, hot):
    _, width, species, layers, _ = c.shape
    wells = mask.shape[1]
    state = (STEPS, 2 * HALO, species, layers, LANES)
    return pl.pallas_call(
        functools.partial(rim_kernel, layers=layers, width=width, species=species),
        out_shape=(
            jax.ShapeDtypeStruct((species, wells), F32),
            jax.ShapeDtypeStruct((2 * HALO + 2, KINDS, layers, LANES), F32),
            jax.ShapeDtypeStruct(state, F32),
            jax.ShapeDtypeStruct(state, F32),
        ),
        in_specs=[VMEM] * 8,
        out_specs=[VMEM] * 4,
        scratch_shapes=[pltpu.VMEM(state, F32)],
        compiler_params=pltpu.CompilerParams(vmem_limit_bytes=6 * MIB),
        cost_estimate=pl.CostEstimate(flops=10**7, bytes_accessed=10**7, transcendentals=0),
        name="rim_steps",
    )(rates, xa, xb, coef, c, t, mask, hot)


def strips_kernel(
    rate_ref, e_ref, ea_ref, eb_ref, partial_in, mask_ref, hot_ref,
    partial_ref, coef_ref, c_ref, jy_ref, t_ref, *, layers, width, species,
):
    shape = (layers, LANES)
    rows = width + 2 * HALO
    lane = lane_of(shape)
    column = lane % GROUP
    near, left = column < 8, lane < RIGHT
    gx, gy = lax.axis_index("gx"), lax.axis_index(Y)
    even_y = lax.rem(gy, 2) == 0
    first_y, last_y = gy == 0, gy == lax.axis_size(Y) - 1
    mask = jnp.where(
        left, jnp.where(first_y & near, 0.0, 1.0), jnp.where(last_y & (column >= 7), 0.0, 1.0)
    ).astype(F32)
    inside_low = jnp.where(gx > 0, 1.0, 0.0).astype(F32)
    inside_high = jnp.where(gx < lax.axis_size("gx") - 1, 1.0, 0.0).astype(F32)
    kept = None
    for r in range(rows):
        own = e_ref[r]
        outer = jnp.where(near == even_y, eb_ref[r], ea_ref[r])
        left_strip = jnp.where(near, outer, own)
        right_strip = jnp.where(near, own, outer)
        c_ref[0, r] = jnp.where(left, left_strip, roll(right_strip, RIGHT, 1))
        k, kd, ux, uy = [
            jnp.where(
                left,
                jnp.take_along_axis(left_strip, GROUP * f + column, 1, mode="promise_in_bounds"),
                jnp.take_along_axis(right_strip, GROUP * f + column, 1, mode="promise_in_bounds"),
            )
            for f in range(species, species + 4)
        ]
        found = y_coefs(k, kd, uy, mask)
        for kind, value in found.items():
            coef_ref[r, kind] = value
        diagonal = found[PY] + found[QYM] + 2 * RATE
        if r:
            inside = inside_low if r <= HALO else inside_high if r >= HALO + width else None
            p, q, b = x_coefs(kept[0], k, kept[1], kd, kept[2], inside)
            coef_ref[r - 1, PX], coef_ref[r - 1, QX], coef_ref[r - 1, BX] = p, q, b
            coef_ref[r - 1, D] = kept[3] + p
            diagonal = diagonal + q
        kept = (k, kd, ux, diagonal)

    rate = rate_ref[species : species + 1, :]
    for m in range(STEPS):
        for r in range(1 + m, rows - 1 - m):

            def put(ref, slot):
                def store(s, value):
                    ref[slot, r] = value

                return store

            step_cell(
                r, m, 0, rate,
                lambda kind, r: coef_ref[r, kind],
                lambda r, s: c_ref[m, r],
                lambda r, s: t_ref[m - 1, r],
                put(c_ref, m + 1), put(t_ref, m), put(jy_ref, m),
            )

    masks = mask_ref[HALO * layers : (HALO + width) * layers, :]
    block = jnp.concatenate([t_ref[STEPS - 1, r] for r in range(HALO, HALO + width)], axis=0)
    for s, total in enumerate(picked_sums(block, hot_ref[...], masks, layers)):
        partial_ref[s : s + 1, :] = partial_in[s : s + 1, :] + total


def side_steps(rates, e, ea, eb, partial, mask, hot):
    rows, layers, _ = e.shape
    species, wells = partial.shape
    state = (STEPS, rows, layers, LANES)
    return pl.pallas_call(
        functools.partial(strips_kernel, layers=layers, width=rows - 2 * HALO, species=species),
        out_shape=(
            jax.ShapeDtypeStruct((species, wells), F32),
            jax.ShapeDtypeStruct((rows, KINDS, layers, LANES), F32),
            jax.ShapeDtypeStruct(state, F32),
            jax.ShapeDtypeStruct(state, F32),
        ),
        in_specs=[VMEM] * 7,
        out_specs=[VMEM] * 4,
        scratch_shapes=[pltpu.VMEM(state, F32)],
        compiler_params=pltpu.CompilerParams(vmem_limit_bytes=6 * MIB),
        name="strip_steps",
    )(rates, e, ea, eb, partial, mask, hot)


def adjoint_kernel(
    rate_ref, weight_ref, meta_ref, mask_ref, coef_in, coef_out, c_in, c_out, jy_in, jy_out,
    coef_side, c_side, jy_side, partial_ref, *rest, layers, width, species, parts,
):
    others, out_ref, lam_ref = rest[:parts], *rest[parts:]
    rows = width + 2 * HALO
    shape = (layers, LANES)
    lane = lane_of(shape)
    gx, gy = lax.axis_index("gx"), lax.axis_index(Y)
    where_y = meta_ref[3:4, :]
    counts = meta_ref[4:5, :].astype(F32)
    wells = meta_ref.shape[1]

    own, strip_species, strip_column = strip_columns(wells)
    strip_hit, own_hit = strip_column == where_y, own == where_y
    residuals = []
    for s in range(species):
        total = partial_ref[s : s + 1, :]
        for other in others:
            total = total + other[s : s + 1, :]
        factor = rate_ref[species + 1 + s, 0:1][:, None]
        residual = weight_ref[s : s + 1, :] * (total * factor) / counts
        residuals.append(residual / counts * factor)
    lam = jnp.zeros((rows * layers, (species + 1) * LANES), F32)
    for piece in range(3):
        coarse = [r.astype(BF16).astype(F32) for r in residuals]
        residuals = [r - q for r, q in zip(residuals, coarse)]
        blocks = [jnp.where(own_hit, q, 0.0).astype(BF16) for q in coarse]
        side = jnp.zeros((LANES, wells), F32)
        for s in range(species):
            side = jnp.where(strip_hit & (strip_species == s), coarse[s], side)
        spread = jnp.concatenate(blocks + [side.astype(BF16)], axis=0)
        lam = lam + lax.dot_general(mask_ref[...], spread, (((1,), (1,)), ((), ())), preferred_element_type=F32)
    for s in range(species + 1):
        lam_ref[0, :, s] = lam[:, s * LANES : (s + 1) * LANES].reshape(rows, layers, LANES)

    def main_coef(kind, r):
        return read_coef((coef_in, coef_out), kind, width, r)

    def side_coef(kind, r):
        return coef_side[r, kind]

    first_row, last_row = HALO - 1, HALO + width - 1
    sums = {}

    def add(key, term):
        sums[key] = sums[key] + term if key in sums else term

    for m in reversed(range(STEPS)):
        now = STEPS - 1 - m
        low, high = STEPS - m, rows - 1 - (STEPS - m)
        for r in range(min(low, first_row), max(high, last_row) + 1):
            sense, retreat = first_row <= r <= last_row, m > 0 and low <= r <= high
            for s in range(species + 1):
                is_side = s == species
                coef = side_coef if is_side else main_coef
                value, up = lam_ref[now, r, s], lam_ref[now, r + 1, s]
                after = y_next(value)
                if sense:
                    if is_side:
                        jump = c_side[m, r + 1] - c_side[m, r]
                    else:
                        states = (c_in, c_out)
                        jump = read_state(states, m, width, r + 1, s) - read_state(states, m, width, r, s)
                    add(("x", is_side, r), jump * (up - value))
                    if r >= HALO:
                        if is_side:
                            jump = jy_side[m, r]
                        else:
                            which, index = state_row(m + 1, width)(r)
                            jump = (jy_in, jy_out)[which][m, index, s]
                        add(("y", is_side, r), jump * (after - value))
                if retreat:
                    lam_ref[now + 1, r, s] = (
                        (rate_ref[s : s + 1, :] - coef(D, r)) * value
                        + coef(PX, r) * up
                        + coef(QX, r - 1) * lam_ref[now, r - 1, s]
                        + coef(PY, r) * after
                        + coef(QYM, r) * y_previous(value)
                        + RATE * z_pair(value)
                    )

    column, left = lane % GROUP, lane < RIGHT
    first_y, last_y = gy == 0, gy == lax.axis_size(Y) - 1
    side_mask = jnp.where(
        left, jnp.where(first_y & (column < 8), 0.0, 1.0), jnp.where(last_y & (column >= 7), 0.0, 1.0)
    ).astype(F32)
    inside_low = jnp.where(gx > 0, 1.0, 0.0).astype(F32)
    inside_high = jnp.where(gx < lax.axis_size("gx") - 1, 1.0, 0.0).astype(F32)
    for x in range(width):
        r = x + HALO
        totals = []
        for is_side in (False, True):
            upper, lower = sums["x", is_side, r], sums["x", is_side, r - 1]
            if x == 0:
                lower = lower * inside_low
            if x == width - 1:
                upper = upper * inside_high
            along_y = sums["y", is_side, r]
            if is_side:
                along_y = along_y * side_mask
            totals.append(upper + lower + along_y + y_previous(along_y))
        total, side = totals
        all_species = side
        for s in range(1, species):
            all_species = all_species + roll(side, -GROUP * s, 1)
        total = jnp.where(lane < STEPS, roll(all_species, -8, 1), total)
        total = jnp.where(lane >= LANES - STEPS, roll(all_species, 120 - RIGHT, 1), total)
        out_ref[pl.ds(x, layers, stride=width), :] = -HALF_DT * main_coef(K, r) * total


def adjoint(rates, weight, meta, mask, inner, outer, side, partials):
    (coef_in, c_in, jy_in), (coef_out, c_out, jy_out) = inner, outer
    _, width, species, layers, _ = c_in.shape
    parts = len(partials) - 1
    operands = (rates, weight, meta, mask, coef_in, coef_out, c_in, c_out, jy_in, jy_out, *side, *partials)
    return pl.pallas_call(
        functools.partial(adjoint_kernel, layers=layers, width=width, species=species, parts=parts),
        out_shape=jax.ShapeDtypeStruct((layers * width, LANES), F32),
        in_specs=[VMEM] * len(operands),
        out_specs=VMEM,
        scratch_shapes=[pltpu.VMEM((STEPS, width + 2 * HALO, species + 1, layers, LANES), F32)],
        compiler_params=pltpu.CompilerParams(vmem_limit_bytes=12 * MIB),
        name="adjoint_steps",
    )(*operands)


def swaps(first, second, axis):
    count = lax.axis_size(axis)
    even = [p for i in range(0, count - 1, 2) for p in ((i, i + 1), (i + 1, i))]
    odd = [p for i in range(1, count - 1, 2) for p in ((i, i + 1), (i + 1, i))]
    return lax.ppermute(first, axis, even), lax.ppermute(second, axis, odd)


def from_others(value, axis, reach):
    count = lax.axis_size(axis)
    if count in (2, 4):
        return [lax.ppermute(value, axis, [(i, i ^ d) for i in range(count)]) for d in range(1, count)]
    return [
        lax.ppermute(value, axis, [(i, i + d) for i in range(count) if 0 <= i + d < count])
        for distance in range(1, min(reach, count - 1) + 1)
        for d in (distance, -distance)
    ]


def shards(
    initial, logk, direction, face_speed, face_flags, retard, decay, screen_cells, screen_count, well_weight
):
    species, layers, width, columns = initial.shape
    raw, xa, xb = send_rows(initial, logk, direction, face_speed, face_flags)
    xa, xb = swaps(xa, xb, "gx")
    coef_in, c_in, t_in, jy_in, e, mask, hot, side_hot, rates, meta = cone(
        retard, decay, screen_cells.T, screen_count, raw, layers, width, species
    )
    e = all_edges(e, xa, xb)
    ea, eb = swaps(e, e, Y)
    partial, coef_out, c_out, jy_out = rim(rates, xa, xb, coef_in, c_in, t_in, mask, hot)
    partial, *side = side_steps(rates, e, ea, eb, partial, mask, side_hot)
    reach = -(-(screen_cells.shape[1] - 1 + HALO) // width)
    partials = [partial] + from_others(partial, "gx", reach)
    inner, outer = (coef_in, c_in, jy_in), (coef_out, c_out, jy_out)
    hessian = adjoint(rates, well_weight, meta, mask, inner, outer, side, partials)
    return hessian.reshape(layers, width, columns)


def solution(mesh):
    in_specs = (
        P("grp", None, "gx", Y),
        P("grp", "gx", Y),
        P("grp", "gx", Y),
        P("grp", None, "gx", Y),
        P("grp", None, "gx", Y),
        P(),
        P(),
        P("grp", None),
        P("grp"),
        P("grp", None),
    )
    return jax.shard_map(shards, mesh=mesh, in_specs=in_specs, out_specs=P("grp", "gx", Y), check_vma=False)
```

```python
import functools

import jax
import jax.numpy as jnp
from jax import lax
from jax.experimental import pallas as pl
from jax.experimental.pallas import tpu as pltpu
from jax.sharding import PartitionSpec as P

STEPS = 4
HALO = STEPS
RATE = 0.02
HALF_DT = 0.025
LANES = 128
TILE = 8
GROUP = 16
RIGHT = 64
Y = ("gy", "sa")
MIB = 1024 * 1024
PX, QX, BX, PY, QYM, QY, PYM, BY, BYM, D, K, KDIR = range(12)
KINDS = 12
VMEM = pl.BlockSpec(memory_space=pltpu.VMEM)
HBM = pl.BlockSpec(memory_space=pltpu.HBM)
F32, BF16, I32 = jnp.float32, jnp.bfloat16, jnp.int32


def in_hbm(*arrays):
    return [pltpu.with_memory_space_constraint(a, pltpu.HBM) for a in arrays]


def lane_of(shape):
    return lax.broadcasted_iota(I32, shape, len(shape) - 1)


def roll(value, shift, axis):
    return pltpu.roll(value, shift % value.shape[axis], axis)


def y_next(value):
    return roll(value, LANES - 1, 1)


def y_previous(value):
    return roll(value, 1, 1)


def pack_edges(fields):
    lane = lane_of(fields[0].shape)
    packed = jnp.zeros_like(fields[0])
    for f, field in enumerate(fields):
        packed = jnp.where(lane // GROUP == f, roll(field, 8 + GROUP * f, 1), packed)
    return packed


def z_pair(value):
    tiles = [value[i : i + TILE] for i in range(0, value.shape[0], TILE)]
    row = lax.broadcasted_iota(I32, tiles[0].shape, 0)
    ups = [roll(t, TILE - 1, 0) for t in tiles]
    downs = [roll(t, 1, 0) for t in tiles]
    pairs = []
    for i, tile in enumerate(tiles):
        above = jnp.where(row == TILE - 1, ups[i + 1] if i + 1 < len(tiles) else tile, ups[i])
        below = jnp.where(row == 0, downs[i - 1] if i else tile, downs[i])
        pairs.append(above + below)
    return jnp.concatenate(pairs, axis=0)


def state_row(m, width):
    low, high = HALO + m, HALO + width - 1 - m

    def find(r):
        if low <= r <= high:
            return 0, r - HALO
        return (1, r - m) if r < low else (1, HALO + r - high - 1)

    return find


def coef_row(kind, width):
    low, high = HALO, HALO + width - 1
    if kind in (PX, QX, BX, D):
        high -= 1
    if kind == D:
        low += 1

    def find(r):
        if low <= r <= high:
            return 0, r - HALO
        return (1, r) if r <= HALO else (1, HALO + 1 + r - (HALO + width - 1))

    return find


def read_state(refs, m, width, r, s):
    which, index = state_row(m, width)(r)
    return refs[which][m, index, s]


def read_coef(refs, kind, width, r):
    which, index = coef_row(kind, width)(r)
    return refs[which][index, kind]


def row_fields(raw, x, layers, width, species):
    initial_ref, logk_ref, direction_ref, speed_ref, flags_ref = raw
    plane = layers * width

    def take(ref, index):
        return ref[pl.ds(index * plane + x, layers, stride=width), :]

    fields = [take(initial_ref, s) for s in range(species)]
    conductance = jnp.exp(take(logk_ref, 0))
    fields += [conductance, conductance * take(direction_ref, 0)]
    for axis in range(2):
        speed = take(speed_ref, axis)
        fields.append(jnp.where(take(flags_ref, axis) == 1, speed, -speed))
    return fields


def y_coefs(k, kd, u, mask=None):
    half = HALF_DT * (k + y_next(k))
    p = half + jnp.maximum(u, 0.0)
    q = half - jnp.minimum(u, 0.0)
    b = HALF_DT * (kd + y_next(kd))
    if mask is not None:
        p, q, b = p * mask, q * mask, b * mask
    return {PY: p, QY: q, BY: b, PYM: y_previous(p), QYM: y_previous(q), BYM: y_previous(b), K: k, KDIR: kd}


def x_coefs(k, k_next, kd, kd_next, u, mask=None):
    half = HALF_DT * (k + k_next)
    p = half + jnp.maximum(u, 0.0)
    q = half - jnp.minimum(u, 0.0)
    b = HALF_DT * (kd + kd_next)
    return (p, q, b) if mask is None else (p * mask, q * mask, b * mask)


def step_cell(r, m, s, rate, coef, state, tangent, put_c, put_t, put_jy):
    kept = rate - coef(D, r)
    upper, lower = coef(QX, r), coef(PX, r - 1)
    after, before = coef(QY, r), coef(PYM, r)

    def moved(value, up, down, yp, ym):
        return kept * value + upper * up + lower * down + after * yp + before * ym + RATE * z_pair(value)

    c, up, down = state(r, s), state(r + 1, s), state(r - 1, s)
    yp, ym = y_next(c), y_previous(c)
    jump = yp - c
    source = (
        coef(BX, r) * (up - c) - coef(BX, r - 1) * (c - down) + coef(BY, r) * jump - coef(BYM, r) * (c - ym)
    )
    put_jy(s, jump)
    if m + 1 < STEPS:
        put_c(s, moved(c, up, down, yp, ym))
    if m > 0:
        t = tangent(r, s)
        source = source + moved(t, tangent(r + 1, s), tangent(r - 1, s), y_next(t), y_previous(t))
    put_t(s, source)


def put_at(ref, m, index):
    def store(s, value):
        ref[m, index, s] = value

    return store


def picked_sums(wide, hot, masks, layers):
    picked = jnp.zeros((wide.shape[0], hot.shape[1]), F32)
    for piece in range(3):
        coarse = wide.astype(BF16)
        picked = picked + jnp.dot(coarse, hot, preferred_element_type=F32)
        wide = wide - coarse.astype(F32)
    wells = masks.shape[1]
    totals = []
    for s in range(hot.shape[1] // wells):
        total = jnp.zeros((layers, wells), F32)
        for i in range(0, wide.shape[0], layers):
            total = total + picked[i : i + layers, s * wells : (s + 1) * wells] * masks[i : i + layers].astype(F32)
        totals.append(jnp.sum(total, axis=0, keepdims=True))
    return totals


def send_kernel(*refs, layers, width, species):
    sources, raw, (xa_ref, xb_ref, sem) = refs[:5], refs[5:10], refs[10:]
    copies = [pltpu.make_async_copy(a, b, sem.at[i]) for i, (a, b) in enumerate(zip(sources, raw))]
    for copy in copies:
        copy.start()
    for copy in copies:
        copy.wait()
    even = lax.rem(lax.axis_index("gx"), 2) == 0
    for r in range(HALO):
        bottom = row_fields(raw, r, layers, width, species)
        top = row_fields(raw, width - HALO + r, layers, width, species)
        for f in range(species + 4):
            xa_ref[r, f] = jnp.where(even, top[f], bottom[f])
            xb_ref[r, f] = jnp.where(even, bottom[f], top[f])


def send_rows(initial, logk, direction, face_speed, face_flags):
    species, layers, width, _ = initial.shape
    sources = [a.reshape(-1, LANES) for a in (initial, logk, direction, face_speed, face_flags)]
    rows = jax.ShapeDtypeStruct((HALO, species + 4, layers, LANES), F32)
    *raw, xa, xb = pl.pallas_call(
        functools.partial(send_kernel, layers=layers, width=width, species=species),
        out_shape=tuple(jax.ShapeDtypeStruct(a.shape, a.dtype) for a in sources) + (rows, rows),
        in_specs=[HBM] * 5,
        out_specs=[VMEM] * 7,
        scratch_shapes=[pltpu.SemaphoreType.DMA((5,))],
        compiler_params=pltpu.CompilerParams(vmem_limit_bytes=3 * MIB),
        name="send_rows",
    )(*in_hbm(*sources))
    return raw, xa, xb


def divide(value, by):
    return lax.shift_right_logical(value, by.bit_length() - 1) if by & (by - 1) == 0 else lax.div(value, by)


def well_table(cells, counts, width):
    total_x, total_y = width * lax.axis_size("gx"), LANES * lax.axis_size(Y)
    start, second = cells[0:1], cells[1:2]
    depth = divide(start, total_x * total_y)
    rest = start - depth * (total_x * total_y)
    x = divide(rest, total_y)
    y = rest - x * total_y
    end = x + jnp.where(second > start, counts - 1, 1 - counts)
    row_start, col_start = lax.axis_index("gx") * width, lax.axis_index(Y) * LANES
    return [depth, jnp.minimum(x, end) - row_start, jnp.maximum(x, end) - row_start, y - col_start, counts]


def strip_columns(wells):
    own = lax.broadcasted_iota(I32, (LANES, wells), 0)
    return own, own % RIGHT // GROUP, own % GROUP + jnp.where(own < RIGHT, -8, 120)


def cone_kernel(
    retard_hbm, decay_hbm, cells_hbm, count_hbm, initial_ref, logk_ref, direction_ref, speed_ref, flags_ref,
    coef_ref, c_ref, t_ref, jy_ref, e_ref, mask_ref, hot_ref, side_hot_ref, rate_ref, meta_ref,
    retard_ref, decay_ref, cells_ref, count_ref, sem, *, layers, width, species,
):
    copies = [
        pltpu.make_async_copy(a, b, sem.at[i])
        for i, (a, b) in enumerate(
            ((retard_hbm, retard_ref), (decay_hbm, decay_ref), (cells_hbm, cells_ref), (count_hbm, count_ref))
        )
    ]
    for copy in copies:
        copy.start()
    raw = initial_ref, logk_ref, direction_ref, speed_ref, flags_ref
    kept = None
    for x in range(width):
        fields = row_fields(raw, x, layers, width, species)
        k, kd, ux, uy = fields[species:]
        e_ref[x] = pack_edges(fields)
        for s in range(species):
            c_ref[0, x, s] = fields[s]
        found = y_coefs(k, kd, uy)
        for kind, value in found.items():
            coef_ref[x, kind] = value
        diagonal = found[PY] + found[QYM] + 2 * RATE
        if x:
            p, q, b = x_coefs(kept[0], k, kept[1], kd, kept[2])
            coef_ref[x - 1, PX], coef_ref[x - 1, QX], coef_ref[x - 1, BX] = p, q, b
            coef_ref[x - 1, D] = kept[3] + p
            diagonal = diagonal + q
        kept = (k, kd, ux, diagonal)
    coef_ref[width - 1, D] = kept[3]
    coef_ref[width - 1, PX] = kept[2]

    for copy in copies:
        copy.wait()
    lane = lane_of((1, LANES))
    strips = jnp.full((1, LANES), retard_ref[species - 1], F32)
    rates = []
    for s in range(species):
        rate = jnp.full((1, LANES), retard_ref[s], F32)
        strips = jnp.where(lane % RIGHT // GROUP == s, rate, strips)
        factor = jnp.exp(jnp.full((1, LANES), -decay_ref[s], F32)) / rate
        rate_ref[s : s + 1, :] = rate
        rate_ref[species + 1 + s : species + 2 + s, :] = factor**STEPS
        rates.append(rate)
    rate_ref[species : species + 1, :] = strips

    for m in range(STEPS):
        for r in range(HALO + 1 + m, HALO + width - 1 - m):
            x = r - HALO
            for s in range(species):
                step_cell(
                    r, m, s, rates[s],
                    lambda kind, r: coef_ref[r - HALO, kind],
                    lambda r, s: c_ref[m, r - HALO, s],
                    lambda r, s: t_ref[m - 1, r - HALO, s],
                    put_at(c_ref, m + 1, x), put_at(t_ref, m, x), put_at(jy_ref, m, x),
                )

    wells = meta_ref.shape[1]
    table = well_table(cells_ref, count_ref[...].reshape(1, wells), width)
    for i, row in enumerate(table):
        meta_ref[i : i + 1, :] = row
    depth, first, last, where_y = table[:4]
    in_layer = lax.broadcasted_iota(I32, (layers, wells), 0) == depth
    for r in range(width + 2 * HALO):
        inside = (first <= r - HALO) & (last >= r - HALO) & in_layer
        mask_ref[r * layers : (r + 1) * layers, :] = jnp.where(inside, 1.0, 0.0).astype(BF16)
    own, strip_species, strip_column = strip_columns(wells)
    hit = (own == where_y) & (own >= STEPS) & (own < LANES - STEPS)
    hot_ref[...] = jnp.where(hit, 1.0, 0.0).astype(BF16)
    reach = (strip_column < STEPS) & (strip_column >= -HALO)
    reach = reach | ((strip_column >= LANES - STEPS) & (strip_column < LANES + HALO))
    hit = reach & (strip_column == where_y)
    for s in range(species):
        side_hot_ref[:, s * wells : (s + 1) * wells] = jnp.where(hit & (strip_species == s), 1.0, 0.0).astype(BF16)


def cone(retard, decay, cells, counts, raw, layers, width, species):
    wells = counts.shape[0]
    state = jax.ShapeDtypeStruct((STEPS, width, species, layers, LANES), F32)
    return pl.pallas_call(
        functools.partial(cone_kernel, layers=layers, width=width, species=species),
        out_shape=(
            jax.ShapeDtypeStruct((width, KINDS, layers, LANES), F32),
            state,
            state,
            state,
            jax.ShapeDtypeStruct((width, layers, LANES), F32),
            jax.ShapeDtypeStruct(((width + 2 * HALO) * layers, wells), BF16),
            jax.ShapeDtypeStruct((LANES, wells), BF16),
            jax.ShapeDtypeStruct((LANES, species * wells), BF16),
            jax.ShapeDtypeStruct((2 * species + 2, LANES), F32),
            jax.ShapeDtypeStruct((TILE, wells), I32),
        ),
        in_specs=[HBM] * 4 + [VMEM] * 5,
        out_specs=[VMEM] * 10,
        scratch_shapes=[
            pltpu.SMEM(retard.shape, F32),
            pltpu.SMEM(decay.shape, F32),
            pltpu.VMEM(cells.shape, I32),
            pltpu.VMEM(counts.shape, I32),
            pltpu.SemaphoreType.DMA((4,)),
        ],
        compiler_params=pltpu.CompilerParams(vmem_limit_bytes=4 * MIB),
        cost_estimate=pl.CostEstimate(flops=10**7, bytes_accessed=10**7, transcendentals=0),
        name="cone_steps",
    )(*in_hbm(retard, decay, cells, counts), *raw)


def neighbour_row(r, a_ref, b_ref, width):
    even = lax.rem(lax.axis_index("gx"), 2) == 0
    from_a = even if r >= HALO else jnp.logical_not(even)
    index = r % (HALO + width)
    return [jnp.where(from_a, a_ref[index, f], b_ref[index, f]) for f in range(a_ref.shape[1])]


def edges_kernel(e_ref, xa_ref, xb_ref, all_ref, a_ref, b_ref, *, width):
    rows = width + 2 * HALO
    half = rows // 2
    even = lax.rem(lax.axis_index(Y), 2) == 0
    edges = {}
    for r in range(rows):
        inner = HALO <= r < HALO + width
        edges[r] = e_ref[r - HALO] if inner else pack_edges(neighbour_row(r, xa_ref, xb_ref, width))
        all_ref[r] = edges[r]
    near = lane_of(edges[0].shape) % GROUP < 8
    for r in range(half):
        one, two = edges[r], edges[r + half]
        to_right = jnp.where(near, one, roll(two, 8, 1))
        to_left = jnp.where(near, roll(two, -8, 1), one)
        a_ref[r] = jnp.where(even, to_right, to_left)
        b_ref[r] = jnp.where(even, to_left, to_right)


def outer_edges(r, a_ref, b_ref, near):
    half = a_ref.shape[0]
    even = lax.rem(lax.axis_index(Y), 2) == 0
    if r < half:
        return jnp.where(near == even, b_ref[r], a_ref[r])
    both = jnp.where(near == even, a_ref[r - half], b_ref[r - half])
    return jnp.where(near, roll(both, -8, 1), roll(both, 8, 1))


def all_edges(e, xa, xb):
    width, layers, _ = e.shape
    return pl.pallas_call(
        functools.partial(edges_kernel, width=width),
        out_shape=(
            jax.ShapeDtypeStruct((width + 2 * HALO, layers, LANES), F32),
            jax.ShapeDtypeStruct((width // 2 + HALO, layers, LANES), F32),
            jax.ShapeDtypeStruct((width // 2 + HALO, layers, LANES), F32),
        ),
        in_specs=[VMEM] * 3,
        out_specs=[VMEM] * 3,
        compiler_params=pltpu.CompilerParams(vmem_limit_bytes=1 * MIB),
        name="edge_columns",
    )(e, xa, xb)


def rim_kernel(
    rate_ref, xa_ref, xb_ref, coef_in, c_in, t_in, mask_ref, hot_ref,
    partial_ref, coef_out, c_out, jy_out, t_out, *, layers, width, species,
):
    gx = lax.axis_index("gx")
    rows = width + 2 * HALO
    coefs = (coef_in, coef_out)
    last = HALO + width - 1
    get = lambda kind, r: read_coef(coefs, kind, width, r)

    def put_coef(kind, r, value):
        which, index = coef_row(kind, width)(r)
        coefs[which][index, kind] = value

    speeds = {last: coef_in[width - 1, PX]}
    for r in list(range(HALO)) + list(range(HALO + width, rows)):
        fields = neighbour_row(r, xa_ref, xb_ref, width)
        k, kd, speeds[r], uy = fields[species:]
        index = state_row(0, width)(r)[1]
        for s in range(species):
            c_out[0, index, s] = fields[s]
        for kind, value in y_coefs(k, kd, uy).items():
            put_coef(kind, r, value)
    inside_low = jnp.where(gx > 0, 1.0, 0.0).astype(F32)
    inside_high = jnp.where(gx < lax.axis_size("gx") - 1, 1.0, 0.0).astype(F32)
    for r in list(range(HALO)) + list(range(last, rows - 1)):
        mask = inside_low if r < HALO else inside_high
        values = x_coefs(get(K, r), get(K, r + 1), get(KDIR, r), get(KDIR, r + 1), speeds[r], mask)
        for kind, value in zip((PX, QX, BX), values):
            put_coef(kind, r, value)
    for r in list(range(1, HALO + 1)) + list(range(last, rows - 1)):
        if r == HALO:
            value = coef_in[0, D] + get(QX, r - 1)
        elif r == last:
            value = coef_in[width - 1, D] + get(PX, r)
        else:
            value = get(PY, r) + get(QYM, r) + 2 * RATE + get(PX, r) + get(QX, r - 1)
        put_coef(D, r, value)

    for m in range(STEPS):
        for r in list(range(1 + m, HALO + 1 + m)) + list(range(last - m, rows - 1 - m)):
            index = state_row(m + 1, width)(r)[1]
            for s in range(species):
                step_cell(
                    r, m, s, rate_ref[s : s + 1, :], get,
                    lambda r, s: read_state((c_in, c_out), m, width, r, s),
                    lambda r, s: tangent_row(t_in, t_out, m, width, r)[s],
                    put_at(c_out, m + 1, index), put_at(t_out, m, index), put_at(jy_out, m, index),
                )

    masks = mask_ref[HALO * layers : (HALO + width) * layers, :]
    for s in range(species):
        block = [tangent_row(t_in, t_out, STEPS, width, r)[s] for r in range(HALO, HALO + width)]
        partial_ref[s : s + 1, :] = picked_sums(jnp.concatenate(block, axis=0), hot_ref[...], masks, layers)[0]


def tangent_row(t_in, t_out, m, width, r):
    which, index = state_row(m, width)(r)
    return (t_in, t_out)[which].at[m - 1, index]


def rim(rates, xa, xb, coef, c, t, mask, hot):
    _, width, species, layers, _ = c.shape
    wells = mask.shape[1]
    state = (STEPS, 2 * HALO, species, layers, LANES)
    return pl.pallas_call(
        functools.partial(rim_kernel, layers=layers, width=width, species=species),
        out_shape=(
            jax.ShapeDtypeStruct((species, wells), F32),
            jax.ShapeDtypeStruct((2 * HALO + 2, KINDS, layers, LANES), F32),
            jax.ShapeDtypeStruct(state, F32),
            jax.ShapeDtypeStruct(state, F32),
        ),
        in_specs=[VMEM] * 8,
        out_specs=[VMEM] * 4,
        scratch_shapes=[pltpu.VMEM(state, F32)],
        compiler_params=pltpu.CompilerParams(vmem_limit_bytes=6 * MIB),
        cost_estimate=pl.CostEstimate(flops=10**7, bytes_accessed=10**7, transcendentals=0),
        name="rim_steps",
    )(rates, xa, xb, coef, c, t, mask, hot)


def strips_kernel(
    rate_ref, e_ref, ea_ref, eb_ref, partial_in, mask_ref, hot_ref,
    partial_ref, coef_ref, c_ref, jy_ref, t_ref, *, layers, width, species,
):
    shape = (layers, LANES)
    rows = width + 2 * HALO
    lane = lane_of(shape)
    column = lane % GROUP
    near, left = column < 8, lane < RIGHT
    gx, gy = lax.axis_index("gx"), lax.axis_index(Y)
    first_y, last_y = gy == 0, gy == lax.axis_size(Y) - 1
    mask = jnp.where(
        left, jnp.where(first_y & near, 0.0, 1.0), jnp.where(last_y & (column >= 7), 0.0, 1.0)
    ).astype(F32)
    inside_low = jnp.where(gx > 0, 1.0, 0.0).astype(F32)
    inside_high = jnp.where(gx < lax.axis_size("gx") - 1, 1.0, 0.0).astype(F32)
    group = lane % RIGHT // GROUP

    def spread(first, second, third):
        return jnp.where(group == 0, first, jnp.where(group == 1, second, third))

    kept = None
    for r in range(rows):
        own = e_ref[r]
        outer = outer_edges(r, ea_ref, eb_ref, near)
        left_strip = jnp.where(near, outer, own)
        right_strip = jnp.where(near, own, outer)
        low = jnp.where(left, left_strip, roll(right_strip, RIGHT, 1))
        high = jnp.where(left, roll(left_strip, RIGHT, 1), right_strip)
        c_ref[0, r] = low
        by_one, by_two = roll(high, GROUP, 1), roll(high, 2 * GROUP, 1)
        back_one, back_two = roll(high, -GROUP, 1), roll(high, -2 * GROUP, 1)
        k = spread(roll(low, -3 * GROUP, 1), roll(low, -2 * GROUP, 1), roll(low, -GROUP, 1))
        kd, ux, uy = spread(high, by_one, by_two), spread(back_one, high, by_one), spread(back_two, back_one, high)
        found = y_coefs(k, kd, uy, mask)
        for kind, value in found.items():
            coef_ref[r, kind] = value
        diagonal = found[PY] + found[QYM] + 2 * RATE
        if r:
            inside = inside_low if r <= HALO else inside_high if r >= HALO + width else None
            p, q, b = x_coefs(kept[0], k, kept[1], kd, kept[2], inside)
            coef_ref[r - 1, PX], coef_ref[r - 1, QX], coef_ref[r - 1, BX] = p, q, b
            coef_ref[r - 1, D] = kept[3] + p
            diagonal = diagonal + q
        kept = (k, kd, ux, diagonal)

    rate = rate_ref[species : species + 1, :]
    for m in range(STEPS):
        for r in range(1 + m, rows - 1 - m):

            def put(ref, slot):
                def store(s, value):
                    ref[slot, r] = value

                return store

            step_cell(
                r, m, 0, rate,
                lambda kind, r: coef_ref[r, kind],
                lambda r, s: c_ref[m, r],
                lambda r, s: t_ref[m - 1, r],
                put(c_ref, m + 1), put(t_ref, m), put(jy_ref, m),
            )

    masks = mask_ref[HALO * layers : (HALO + width) * layers, :]
    block = jnp.concatenate([t_ref[STEPS - 1, r] for r in range(HALO, HALO + width)], axis=0)
    for s, total in enumerate(picked_sums(block, hot_ref[...], masks, layers)):
        partial_ref[s : s + 1, :] = partial_in[s : s + 1, :] + total


def side_steps(rates, e, ea, eb, partial, mask, hot):
    rows, layers, _ = e.shape
    species, wells = partial.shape
    state = (STEPS, rows, layers, LANES)
    return pl.pallas_call(
        functools.partial(strips_kernel, layers=layers, width=rows - 2 * HALO, species=species),
        out_shape=(
            jax.ShapeDtypeStruct((species, wells), F32),
            jax.ShapeDtypeStruct((rows, KINDS, layers, LANES), F32),
            jax.ShapeDtypeStruct(state, F32),
            jax.ShapeDtypeStruct(state, F32),
        ),
        in_specs=[VMEM] * 7,
        out_specs=[VMEM] * 4,
        scratch_shapes=[pltpu.VMEM(state, F32)],
        compiler_params=pltpu.CompilerParams(vmem_limit_bytes=6 * MIB),
        name="strip_steps",
    )(rates, e, ea, eb, partial, mask, hot)


def adjoint_kernel(
    rate_ref, weight_ref, meta_ref, mask_ref, coef_in, coef_out, c_in, c_out, jy_in, jy_out,
    coef_side, c_side, jy_side, partial_ref, *rest, layers, width, species, parts,
):
    others, out_ref, lam_ref = rest[:parts], *rest[parts:]
    rows = width + 2 * HALO
    shape = (layers, LANES)
    lane = lane_of(shape)
    gx, gy = lax.axis_index("gx"), lax.axis_index(Y)
    where_y = meta_ref[3:4, :]
    counts = meta_ref[4:5, :].astype(F32)
    wells = meta_ref.shape[1]

    own, strip_species, strip_column = strip_columns(wells)
    strip_hit, own_hit = strip_column == where_y, own == where_y
    residuals = []
    for s in range(species):
        total = partial_ref[s : s + 1, :]
        for other in others:
            total = total + other[s : s + 1, :]
        factor = rate_ref[species + 1 + s, 0:1][:, None]
        residual = weight_ref[s : s + 1, :] * (total * factor) / counts
        residuals.append(residual / counts * factor)
    lam = jnp.zeros((rows * layers, (species + 1) * LANES), F32)
    for piece in range(3):
        coarse = [r.astype(BF16).astype(F32) for r in residuals]
        residuals = [r - q for r, q in zip(residuals, coarse)]
        blocks = [jnp.where(own_hit, q, 0.0).astype(BF16) for q in coarse]
        side = jnp.zeros((LANES, wells), F32)
        for s in range(species):
            side = jnp.where(strip_hit & (strip_species == s), coarse[s], side)
        spread = jnp.concatenate(blocks + [side.astype(BF16)], axis=0)
        lam = lam + lax.dot_general(mask_ref[...], spread, (((1,), (1,)), ((), ())), preferred_element_type=F32)
    for s in range(species + 1):
        lam_ref[0, :, s] = lam[:, s * LANES : (s + 1) * LANES].reshape(rows, layers, LANES)

    def main_coef(kind, r):
        return read_coef((coef_in, coef_out), kind, width, r)

    def side_coef(kind, r):
        return coef_side[r, kind]

    first_row, last_row = HALO - 1, HALO + width - 1
    sums = {}

    def add(key, term):
        sums[key] = sums[key] + term if key in sums else term

    for m in reversed(range(STEPS)):
        now = STEPS - 1 - m
        low, high = STEPS - m, rows - 1 - (STEPS - m)
        for r in range(min(low, first_row), max(high, last_row) + 1):
            sense, retreat = first_row <= r <= last_row, m > 0 and low <= r <= high
            for s in range(species + 1):
                is_side = s == species
                coef = side_coef if is_side else main_coef
                value, up = lam_ref[now, r, s], lam_ref[now, r + 1, s]
                after = y_next(value)
                if sense:
                    if is_side:
                        jump = c_side[m, r + 1] - c_side[m, r]
                    else:
                        states = (c_in, c_out)
                        jump = read_state(states, m, width, r + 1, s) - read_state(states, m, width, r, s)
                    add(("x", is_side, r), jump * (up - value))
                    if r >= HALO:
                        if is_side:
                            jump = jy_side[m, r]
                        else:
                            which, index = state_row(m + 1, width)(r)
                            jump = (jy_in, jy_out)[which][m, index, s]
                        add(("y", is_side, r), jump * (after - value))
                if retreat:
                    lam_ref[now + 1, r, s] = (
                        (rate_ref[s : s + 1, :] - coef(D, r)) * value
                        + coef(PX, r) * up
                        + coef(QX, r - 1) * lam_ref[now, r - 1, s]
                        + coef(PY, r) * after
                        + coef(QYM, r) * y_previous(value)
                        + RATE * z_pair(value)
                    )

    column, left = lane % GROUP, lane < RIGHT
    first_y, last_y = gy == 0, gy == lax.axis_size(Y) - 1
    side_mask = jnp.where(
        left, jnp.where(first_y & (column < 8), 0.0, 1.0), jnp.where(last_y & (column >= 7), 0.0, 1.0)
    ).astype(F32)
    inside_low = jnp.where(gx > 0, 1.0, 0.0).astype(F32)
    inside_high = jnp.where(gx < lax.axis_size("gx") - 1, 1.0, 0.0).astype(F32)
    for x in range(width):
        r = x + HALO
        totals = []
        for is_side in (False, True):
            upper, lower = sums["x", is_side, r], sums["x", is_side, r - 1]
            if x == 0:
                lower = lower * inside_low
            if x == width - 1:
                upper = upper * inside_high
            along_y = sums["y", is_side, r]
            if is_side:
                along_y = along_y * side_mask
            totals.append(upper + lower + along_y + y_previous(along_y))
        total, side = totals
        all_species = side
        for s in range(1, species):
            all_species = all_species + roll(side, -GROUP * s, 1)
        total = jnp.where(lane < STEPS, roll(all_species, -8, 1), total)
        total = jnp.where(lane >= LANES - STEPS, roll(all_species, 120 - RIGHT, 1), total)
        out_ref[pl.ds(x, layers, stride=width), :] = -HALF_DT * main_coef(K, r) * total


def adjoint(rates, weight, meta, mask, inner, outer, side, partials):
    (coef_in, c_in, jy_in), (coef_out, c_out, jy_out) = inner, outer
    _, width, species, layers, _ = c_in.shape
    parts = len(partials) - 1
    operands = (rates, weight, meta, mask, coef_in, coef_out, c_in, c_out, jy_in, jy_out, *side, *partials)
    return pl.pallas_call(
        functools.partial(adjoint_kernel, layers=layers, width=width, species=species, parts=parts),
        out_shape=jax.ShapeDtypeStruct((layers * width, LANES), F32),
        in_specs=[VMEM] * len(operands),
        out_specs=VMEM,
        scratch_shapes=[pltpu.VMEM((STEPS, width + 2 * HALO, species + 1, layers, LANES), F32)],
        compiler_params=pltpu.CompilerParams(vmem_limit_bytes=12 * MIB),
        name="adjoint_steps",
    )(*operands)


def pairs(count, start):
    return [p for i in range(start, count - 1, 2) for p in ((i, i + 1), (i + 1, i))]


def swap_x(first, second):
    count, side = lax.axis_size("gx"), lax.axis_size(Y)
    partner = dict(pairs(count, 1))
    odd = [
        (i * side + j, partner[i] * side + j if i in partner else i * side + (j ^ 1))
        for i in range(count)
        for j in range(side)
    ]
    return lax.ppermute(first, "gx", pairs(count, 0)), lax.ppermute(second, ("gx",) + Y, odd)


def swap_y(first, second):
    count = lax.axis_size(Y)
    odd = pairs(count, 1) + [(0, count - 1), (count - 1, 0)]
    return lax.ppermute(first, Y, pairs(count, 0)), lax.ppermute(second, Y, odd)


def from_others(value, axis, reach):
    count = lax.axis_size(axis)
    if count in (2, 4):
        return [lax.ppermute(value, axis, [(i, i ^ d) for i in range(count)]) for d in range(1, count)]
    return [
        lax.ppermute(value, axis, [(i, i + d) for i in range(count) if 0 <= i + d < count])
        for distance in range(1, min(reach, count - 1) + 1)
        for d in (distance, -distance)
    ]


def shards(
    initial, logk, direction, face_speed, face_flags, retard, decay, screen_cells, screen_count, well_weight
):
    species, layers, width, columns = initial.shape
    raw, xa, xb = send_rows(initial, logk, direction, face_speed, face_flags)
    xa, xb = swap_x(xa, xb)
    coef_in, c_in, t_in, jy_in, e, mask, hot, side_hot, rates, meta = cone(
        retard, decay, screen_cells.T, screen_count, raw, layers, width, species
    )
    e, ea, eb = all_edges(e, xa, xb)
    ea, eb = swap_y(ea, eb)
    partial, coef_out, c_out, jy_out = rim(rates, xa, xb, coef_in, c_in, t_in, mask, hot)
    partial, *side = side_steps(rates, e, ea, eb, partial, mask, side_hot)
    reach = -(-(screen_cells.shape[1] - 1 + HALO) // width)
    partials = [partial] + from_others(partial, "gx", reach)
    inner, outer = (coef_in, c_in, jy_in), (coef_out, c_out, jy_out)
    hessian = adjoint(rates, well_weight, meta, mask, inner, outer, side, partials)
    return hessian.reshape(layers, width, columns)


def solution(mesh):
    in_specs = (
        P("grp", None, "gx", Y),
        P("grp", "gx", Y),
        P("grp", "gx", Y),
        P("grp", None, "gx", Y),
        P("grp", None, "gx", Y),
        P(),
        P(),
        P("grp", None),
        P("grp"),
        P("grp", None),
    )
    return jax.shard_map(shards, mesh=mesh, in_specs=in_specs, out_specs=P("grp", "gx", Y), check_vma=False)
```

```python
import functools

import jax
import jax.numpy as jnp
from jax import lax
from jax.experimental import pallas as pl
from jax.experimental.pallas import tpu as pltpu
from jax.sharding import PartitionSpec as P

STEPS = 4
HALO = STEPS
RATE = 0.02
HALF_DT = 0.025
LANES = 128
TILE = 8
GROUP = 16
RIGHT = 64
Y = ("gy", "sa")
MIB = 1024 * 1024
PX, QX, BX, PY, QYM, QY, PYM, BY, BYM, D, K, KDIR = range(12)
KINDS = 12
VMEM = pl.BlockSpec(memory_space=pltpu.VMEM)
HBM = pl.BlockSpec(memory_space=pltpu.HBM)
F32, BF16, I32 = jnp.float32, jnp.bfloat16, jnp.int32


def in_hbm(*arrays):
    return [pltpu.with_memory_space_constraint(a, pltpu.HBM) for a in arrays]


def lane_of(shape):
    return lax.broadcasted_iota(I32, shape, len(shape) - 1)


def roll(value, shift, axis):
    return pltpu.roll(value, shift % value.shape[axis], axis)


def y_next(value):
    return roll(value, LANES - 1, 1)


def y_previous(value):
    return roll(value, 1, 1)


def pack_edges(fields):
    lane = lane_of(fields[0].shape)
    packed = jnp.zeros_like(fields[0])
    for f, field in enumerate(fields):
        packed = jnp.where(lane // GROUP == f, roll(field, 8 + GROUP * f, 1), packed)
    return packed


def z_pair(value):
    tiles = [value[i : i + TILE] for i in range(0, value.shape[0], TILE)]
    row = lax.broadcasted_iota(I32, tiles[0].shape, 0)
    ups = [roll(t, TILE - 1, 0) for t in tiles]
    downs = [roll(t, 1, 0) for t in tiles]
    pairs = []
    for i, tile in enumerate(tiles):
        above = jnp.where(row == TILE - 1, ups[i + 1] if i + 1 < len(tiles) else tile, ups[i])
        below = jnp.where(row == 0, downs[i - 1] if i else tile, downs[i])
        pairs.append(above + below)
    return jnp.concatenate(pairs, axis=0)


def state_row(m, width):
    low, high = HALO + m, HALO + width - 1 - m

    def find(r):
        if low <= r <= high:
            return 0, r - HALO
        return (1, r - m) if r < low else (1, HALO + r - high - 1)

    return find


def coef_row(kind, width):
    low, high = HALO, HALO + width - 1
    if kind in (PX, QX, BX, D):
        high -= 1
    if kind == D:
        low += 1

    def find(r):
        if low <= r <= high:
            return 0, r - HALO
        return (1, r) if r <= HALO else (1, HALO + 1 + r - (HALO + width - 1))

    return find


def read_state(refs, m, width, r, s):
    which, index = state_row(m, width)(r)
    return refs[which][m, index, s]


def read_coef(refs, kind, width, r):
    which, index = coef_row(kind, width)(r)
    return refs[which][index, kind]


def row_fields(raw, x, layers, width, species):
    initial_ref, logk_ref, direction_ref, speed_ref, flags_ref = raw
    plane = layers * width

    def take(ref, index):
        return ref[pl.ds(index * plane + x, layers, stride=width), :]

    fields = [take(initial_ref, s) for s in range(species)]
    conductance = jnp.exp(take(logk_ref, 0))
    fields += [conductance, conductance * take(direction_ref, 0)]
    for axis in range(2):
        speed = take(speed_ref, axis)
        fields.append(jnp.where(take(flags_ref, axis) == 1, speed, -speed))
    return fields


def y_coefs(k, kd, u, mask=None):
    half = HALF_DT * (k + y_next(k))
    p = half + jnp.maximum(u, 0.0)
    q = half - jnp.minimum(u, 0.0)
    b = HALF_DT * (kd + y_next(kd))
    if mask is not None:
        p, q, b = p * mask, q * mask, b * mask
    return {PY: p, QY: q, BY: b, PYM: y_previous(p), QYM: y_previous(q), BYM: y_previous(b), K: k, KDIR: kd}


def x_coefs(k, k_next, kd, kd_next, u, mask=None):
    half = HALF_DT * (k + k_next)
    p = half + jnp.maximum(u, 0.0)
    q = half - jnp.minimum(u, 0.0)
    b = HALF_DT * (kd + kd_next)
    return (p, q, b) if mask is None else (p * mask, q * mask, b * mask)


def step_cell(r, m, s, rate, coef, state, tangent, put_c, put_t, put_jy):
    kept = rate - coef(D, r)
    upper, lower = coef(QX, r), coef(PX, r - 1)
    after, before = coef(QY, r), coef(PYM, r)

    def moved(value, up, down, yp, ym):
        return kept * value + upper * up + lower * down + after * yp + before * ym + RATE * z_pair(value)

    c, up, down = state(r, s), state(r + 1, s), state(r - 1, s)
    yp, ym = y_next(c), y_previous(c)
    jump = yp - c
    source = (
        coef(BX, r) * (up - c) - coef(BX, r - 1) * (c - down) + coef(BY, r) * jump - coef(BYM, r) * (c - ym)
    )
    put_jy(s, jump)
    if m + 1 < STEPS:
        put_c(s, moved(c, up, down, yp, ym))
    if m > 0:
        t = tangent(r, s)
        source = source + moved(t, tangent(r + 1, s), tangent(r - 1, s), y_next(t), y_previous(t))
    put_t(s, source)


def put_at(ref, m, index):
    def store(s, value):
        ref[m, index, s] = value

    return store


def picked_sums(wide, hot, masks, layers):
    picked = jnp.zeros((wide.shape[0], hot.shape[1]), F32)
    for piece in range(3):
        coarse = wide.astype(BF16)
        picked = picked + jnp.dot(coarse, hot, preferred_element_type=F32)
        wide = wide - coarse.astype(F32)
    wells = masks.shape[1]
    totals = []
    for s in range(hot.shape[1] // wells):
        total = jnp.zeros((layers, wells), F32)
        for i in range(0, wide.shape[0], layers):
            total = total + picked[i : i + layers, s * wells : (s + 1) * wells] * masks[i : i + layers].astype(F32)
        totals.append(jnp.sum(total, axis=0, keepdims=True))
    return totals


def send_kernel(*refs, layers, width, species):
    sources, raw, (xa_ref, xb_ref, sem) = refs[:5], refs[5:10], refs[10:]
    copies = [pltpu.make_async_copy(a, b, sem.at[i]) for i, (a, b) in enumerate(zip(sources, raw))]
    for copy in copies:
        copy.start()
    for copy in copies:
        copy.wait()
    even = lax.rem(lax.axis_index("gx"), 2) == 0
    for r in range(HALO):
        bottom = row_fields(raw, r, layers, width, species)
        top = row_fields(raw, width - HALO + r, layers, width, species)
        for f in range(species + 4):
            xa_ref[r, f] = jnp.where(even, top[f], bottom[f])
            xb_ref[r, f] = jnp.where(even, bottom[f], top[f])


def send_rows(initial, logk, direction, face_speed, face_flags):
    species, layers, width, _ = initial.shape
    sources = [a.reshape(-1, LANES) for a in (initial, logk, direction, face_speed, face_flags)]
    rows = jax.ShapeDtypeStruct((HALO, species + 4, layers, LANES), F32)
    *raw, xa, xb = pl.pallas_call(
        functools.partial(send_kernel, layers=layers, width=width, species=species),
        out_shape=tuple(jax.ShapeDtypeStruct(a.shape, a.dtype) for a in sources) + (rows, rows),
        in_specs=[HBM] * 5,
        out_specs=[VMEM] * 7,
        scratch_shapes=[pltpu.SemaphoreType.DMA((5,))],
        compiler_params=pltpu.CompilerParams(vmem_limit_bytes=3 * MIB),
        name="send_rows",
    )(*in_hbm(*sources))
    return raw, xa, xb


def divide(value, by):
    return lax.shift_right_logical(value, by.bit_length() - 1) if by & (by - 1) == 0 else lax.div(value, by)


def well_table(cells, counts, width):
    total_x, total_y = width * lax.axis_size("gx"), LANES * lax.axis_size(Y)
    start, second = cells[0:1], cells[1:2]
    depth = divide(start, total_x * total_y)
    rest = start - depth * (total_x * total_y)
    x = divide(rest, total_y)
    y = rest - x * total_y
    end = x + jnp.where(second > start, counts - 1, 1 - counts)
    row_start, col_start = lax.axis_index("gx") * width, lax.axis_index(Y) * LANES
    return [depth, jnp.minimum(x, end) - row_start, jnp.maximum(x, end) - row_start, y - col_start, counts]


def strip_columns(wells):
    own = lax.broadcasted_iota(I32, (LANES, wells), 0)
    return own, own % RIGHT // GROUP, own % GROUP + jnp.where(own < RIGHT, -8, 120)


def cone_kernel(
    retard_hbm, decay_hbm, cells_hbm, count_hbm, initial_ref, logk_ref, direction_ref, speed_ref, flags_ref,
    coef_ref, c_ref, t_ref, jy_ref, e_ref, mask_ref, hot_ref, side_hot_ref, spread_ref, rate_ref, meta_ref,
    retard_ref, decay_ref, cells_ref, count_ref, sem, *, layers, width, species,
):
    copies = [
        pltpu.make_async_copy(a, b, sem.at[i])
        for i, (a, b) in enumerate(
            ((retard_hbm, retard_ref), (decay_hbm, decay_ref), (cells_hbm, cells_ref), (count_hbm, count_ref))
        )
    ]
    for copy in copies:
        copy.start()
    raw = initial_ref, logk_ref, direction_ref, speed_ref, flags_ref
    kept = None
    for x in range(width):
        fields = row_fields(raw, x, layers, width, species)
        k, kd, ux, uy = fields[species:]
        e_ref[x] = pack_edges(fields)
        for s in range(species):
            c_ref[0, x, s] = fields[s]
        found = y_coefs(k, kd, uy)
        for kind, value in found.items():
            coef_ref[x, kind] = value
        diagonal = found[PY] + found[QYM] + 2 * RATE
        if x:
            p, q, b = x_coefs(kept[0], k, kept[1], kd, kept[2])
            coef_ref[x - 1, PX], coef_ref[x - 1, QX], coef_ref[x - 1, BX] = p, q, b
            coef_ref[x - 1, D] = kept[3] + p
            diagonal = diagonal + q
        kept = (k, kd, ux, diagonal)
    coef_ref[width - 1, D] = kept[3]
    coef_ref[width - 1, PX] = kept[2]

    for copy in copies:
        copy.wait()
    lane = lane_of((1, LANES))
    strips = jnp.full((1, LANES), retard_ref[species - 1], F32)
    rates = []
    for s in range(species):
        rate = jnp.full((1, LANES), retard_ref[s], F32)
        strips = jnp.where(lane % RIGHT // GROUP == s, rate, strips)
        factor = jnp.exp(jnp.full((1, LANES), -decay_ref[s], F32)) / rate
        rate_ref[s : s + 1, :] = rate
        rate_ref[species + 1 + s : species + 2 + s, :] = factor**STEPS
        rates.append(rate)
    rate_ref[species : species + 1, :] = strips

    for m in range(STEPS):
        for r in range(HALO + 1 + m, HALO + width - 1 - m):
            x = r - HALO
            for s in range(species):
                step_cell(
                    r, m, s, rates[s],
                    lambda kind, r: coef_ref[r - HALO, kind],
                    lambda r, s: c_ref[m, r - HALO, s],
                    lambda r, s: t_ref[m - 1, r - HALO, s],
                    put_at(c_ref, m + 1, x), put_at(t_ref, m, x), put_at(jy_ref, m, x),
                )

    wells = meta_ref.shape[1]
    table = well_table(cells_ref, count_ref[...].reshape(1, wells), width)
    for i, row in enumerate(table):
        meta_ref[i : i + 1, :] = row
    depth, first, last, where_y = table[:4]
    in_layer = lax.broadcasted_iota(I32, (layers, wells), 0) == depth
    for r in range(width + 2 * HALO):
        inside = (first <= r - HALO) & (last >= r - HALO) & in_layer
        mask_ref[r * layers : (r + 1) * layers, :] = jnp.where(inside, 1.0, 0.0).astype(BF16)
    own, strip_species, strip_column = strip_columns(wells)
    hit = (own == where_y) & (own >= STEPS) & (own < LANES - STEPS)
    hot_ref[...] = jnp.where(hit, 1.0, 0.0).astype(BF16)
    reach = (strip_column < STEPS) & (strip_column >= -HALO)
    reach = reach | ((strip_column >= LANES - STEPS) & (strip_column < LANES + HALO))
    hit = reach & (strip_column == where_y)
    for s in range(species):
        side_hot_ref[:, s * wells : (s + 1) * wells] = jnp.where(hit & (strip_species == s), 1.0, 0.0).astype(BF16)


    source = lax.broadcasted_iota(I32, (2 * LANES, LANES), 0)
    target = lax.broadcasted_iota(I32, (2 * LANES, LANES), 1)
    target = jnp.where(target < RIGHT, 0, LANES) + target % GROUP
    for f in range(4):
        hit = source == target + (species + f) * GROUP
        spread_ref[:, f * LANES : (f + 1) * LANES] = jnp.where(hit, 1.0, 0.0).astype(BF16)


def cone(retard, decay, cells, counts, raw, layers, width, species):
    wells = counts.shape[0]
    state = jax.ShapeDtypeStruct((STEPS, width, species, layers, LANES), F32)
    return pl.pallas_call(
        functools.partial(cone_kernel, layers=layers, width=width, species=species),
        out_shape=(
            jax.ShapeDtypeStruct((width, KINDS, layers, LANES), F32),
            state,
            state,
            state,
            jax.ShapeDtypeStruct((width, layers, LANES), F32),
            jax.ShapeDtypeStruct(((width + 2 * HALO) * layers, wells), BF16),
            jax.ShapeDtypeStruct((LANES, wells), BF16),
            jax.ShapeDtypeStruct((LANES, species * wells), BF16),
            jax.ShapeDtypeStruct((2 * LANES, 4 * LANES), BF16),
            jax.ShapeDtypeStruct((2 * species + 2, LANES), F32),
            jax.ShapeDtypeStruct((TILE, wells), I32),
        ),
        in_specs=[HBM] * 4 + [VMEM] * 5,
        out_specs=[VMEM] * 11,
        scratch_shapes=[
            pltpu.SMEM(retard.shape, F32),
            pltpu.SMEM(decay.shape, F32),
            pltpu.VMEM(cells.shape, I32),
            pltpu.VMEM(counts.shape, I32),
            pltpu.SemaphoreType.DMA((4,)),
        ],
        compiler_params=pltpu.CompilerParams(vmem_limit_bytes=4 * MIB),
        cost_estimate=pl.CostEstimate(flops=10**7, bytes_accessed=10**7, transcendentals=0),
        name="cone_steps",
    )(*in_hbm(retard, decay, cells, counts), *raw)


def neighbour_row(r, a_ref, b_ref, width):
    even = lax.rem(lax.axis_index("gx"), 2) == 0
    from_a = even if r >= HALO else jnp.logical_not(even)
    index = r % (HALO + width)
    return [jnp.where(from_a, a_ref[index, f], b_ref[index, f]) for f in range(a_ref.shape[1])]


def edges_kernel(e_ref, xa_ref, xb_ref, all_ref, a_ref, b_ref, *, width):
    rows = width + 2 * HALO
    half = rows // 2
    even = lax.rem(lax.axis_index(Y), 2) == 0
    edges = {}
    for r in range(rows):
        inner = HALO <= r < HALO + width
        edges[r] = e_ref[r - HALO] if inner else pack_edges(neighbour_row(r, xa_ref, xb_ref, width))
        all_ref[r] = edges[r]
    near = lane_of(edges[0].shape) % GROUP < 8
    for r in range(half):
        one, two = edges[r], edges[r + half]
        to_right = jnp.where(near, one, roll(two, 8, 1))
        to_left = jnp.where(near, roll(two, -8, 1), one)
        a_ref[r] = jnp.where(even, to_right, to_left)
        b_ref[r] = jnp.where(even, to_left, to_right)


def outer_edges(r, a_ref, b_ref, near):
    half = a_ref.shape[0]
    even = lax.rem(lax.axis_index(Y), 2) == 0
    if r < half:
        return jnp.where(near == even, b_ref[r], a_ref[r])
    both = jnp.where(near == even, a_ref[r - half], b_ref[r - half])
    return jnp.where(near, roll(both, -8, 1), roll(both, 8, 1))


def all_edges(e, xa, xb):
    width, layers, _ = e.shape
    return pl.pallas_call(
        functools.partial(edges_kernel, width=width),
        out_shape=(
            jax.ShapeDtypeStruct((width + 2 * HALO, layers, LANES), F32),
            jax.ShapeDtypeStruct((width // 2 + HALO, layers, LANES), F32),
            jax.ShapeDtypeStruct((width // 2 + HALO, layers, LANES), F32),
        ),
        in_specs=[VMEM] * 3,
        out_specs=[VMEM] * 3,
        compiler_params=pltpu.CompilerParams(vmem_limit_bytes=1 * MIB),
        name="edge_columns",
    )(e, xa, xb)


def rim_kernel(
    rate_ref, xa_ref, xb_ref, coef_in, c_in, t_in, mask_ref, hot_ref,
    partial_ref, coef_out, c_out, jy_out, t_out, *, layers, width, species,
):
    gx = lax.axis_index("gx")
    rows = width + 2 * HALO
    coefs = (coef_in, coef_out)
    last = HALO + width - 1
    get = lambda kind, r: read_coef(coefs, kind, width, r)

    def put_coef(kind, r, value):
        which, index = coef_row(kind, width)(r)
        coefs[which][index, kind] = value

    speeds = {last: coef_in[width - 1, PX]}
    for r in list(range(HALO)) + list(range(HALO + width, rows)):
        fields = neighbour_row(r, xa_ref, xb_ref, width)
        k, kd, speeds[r], uy = fields[species:]
        index = state_row(0, width)(r)[1]
        for s in range(species):
            c_out[0, index, s] = fields[s]
        for kind, value in y_coefs(k, kd, uy).items():
            put_coef(kind, r, value)
    inside_low = jnp.where(gx > 0, 1.0, 0.0).astype(F32)
    inside_high = jnp.where(gx < lax.axis_size("gx") - 1, 1.0, 0.0).astype(F32)
    for r in list(range(HALO)) + list(range(last, rows - 1)):
        mask = inside_low if r < HALO else inside_high
        values = x_coefs(get(K, r), get(K, r + 1), get(KDIR, r), get(KDIR, r + 1), speeds[r], mask)
        for kind, value in zip((PX, QX, BX), values):
            put_coef(kind, r, value)
    for r in list(range(1, HALO + 1)) + list(range(last, rows - 1)):
        if r == HALO:
            value = coef_in[0, D] + get(QX, r - 1)
        elif r == last:
            value = coef_in[width - 1, D] + get(PX, r)
        else:
            value = get(PY, r) + get(QYM, r) + 2 * RATE + get(PX, r) + get(QX, r - 1)
        put_coef(D, r, value)

    for m in range(STEPS):
        for r in list(range(1 + m, HALO + 1 + m)) + list(range(last - m, rows - 1 - m)):
            index = state_row(m + 1, width)(r)[1]
            for s in range(species):
                step_cell(
                    r, m, s, rate_ref[s : s + 1, :], get,
                    lambda r, s: read_state((c_in, c_out), m, width, r, s),
                    lambda r, s: tangent_row(t_in, t_out, m, width, r)[s],
                    put_at(c_out, m + 1, index), put_at(t_out, m, index), put_at(jy_out, m, index),
                )

    masks = mask_ref[HALO * layers : (HALO + width) * layers, :]
    for s in range(species):
        block = [tangent_row(t_in, t_out, STEPS, width, r)[s] for r in range(HALO, HALO + width)]
        partial_ref[s : s + 1, :] = picked_sums(jnp.concatenate(block, axis=0), hot_ref[...], masks, layers)[0]


def tangent_row(t_in, t_out, m, width, r):
    which, index = state_row(m, width)(r)
    return (t_in, t_out)[which].at[m - 1, index]


def rim(rates, xa, xb, coef, c, t, mask, hot):
    _, width, species, layers, _ = c.shape
    wells = mask.shape[1]
    state = (STEPS, 2 * HALO, species, layers, LANES)
    return pl.pallas_call(
        functools.partial(rim_kernel, layers=layers, width=width, species=species),
        out_shape=(
            jax.ShapeDtypeStruct((species, wells), F32),
            jax.ShapeDtypeStruct((2 * HALO + 2, KINDS, layers, LANES), F32),
            jax.ShapeDtypeStruct(state, F32),
            jax.ShapeDtypeStruct(state, F32),
        ),
        in_specs=[VMEM] * 8,
        out_specs=[VMEM] * 4,
        scratch_shapes=[pltpu.VMEM(state, F32)],
        compiler_params=pltpu.CompilerParams(vmem_limit_bytes=6 * MIB),
        cost_estimate=pl.CostEstimate(flops=10**7, bytes_accessed=10**7, transcendentals=0),
        name="rim_steps",
    )(rates, xa, xb, coef, c, t, mask, hot)


def strips_kernel(
    rate_ref, e_ref, ea_ref, eb_ref, partial_in, mask_ref, hot_ref, spread_ref,
    partial_ref, coef_ref, c_ref, jy_ref, t_ref, *, layers, width, species,
):
    shape = (layers, LANES)
    rows = width + 2 * HALO
    lane = lane_of(shape)
    column = lane % GROUP
    near, left = column < 8, lane < RIGHT
    gx, gy = lax.axis_index("gx"), lax.axis_index(Y)
    first_y, last_y = gy == 0, gy == lax.axis_size(Y) - 1
    mask = jnp.where(
        left, jnp.where(first_y & near, 0.0, 1.0), jnp.where(last_y & (column >= 7), 0.0, 1.0)
    ).astype(F32)
    inside_low = jnp.where(gx > 0, 1.0, 0.0).astype(F32)
    inside_high = jnp.where(gx < lax.axis_size("gx") - 1, 1.0, 0.0).astype(F32)
    both = []
    for r in range(rows):
        own, outer = e_ref[r], outer_edges(r, ea_ref, eb_ref, near)
        left_strip, right_strip = jnp.where(near, outer, own), jnp.where(near, own, outer)
        c_ref[0, r] = jnp.where(left, left_strip, roll(right_strip, RIGHT, 1))
        both.append(jnp.concatenate([left_strip, right_strip], axis=1))
    rest = jnp.concatenate(both, axis=0)
    fields = jnp.zeros((rows * layers, 4 * LANES), F32)
    for piece in range(3):
        coarse = rest.astype(BF16)
        fields = fields + jnp.dot(coarse, spread_ref[...], preferred_element_type=F32)
        rest = rest - coarse.astype(F32)

    kept = None
    for r in range(rows):
        k, kd, ux, uy = [fields[r * layers : (r + 1) * layers, f * LANES : (f + 1) * LANES] for f in range(4)]
        found = y_coefs(k, kd, uy, mask)
        for kind, value in found.items():
            coef_ref[r, kind] = value
        diagonal = found[PY] + found[QYM] + 2 * RATE
        if r:
            inside = inside_low if r <= HALO else inside_high if r >= HALO + width else None
            p, q, b = x_coefs(kept[0], k, kept[1], kd, kept[2], inside)
            coef_ref[r - 1, PX], coef_ref[r - 1, QX], coef_ref[r - 1, BX] = p, q, b
            coef_ref[r - 1, D] = kept[3] + p
            diagonal = diagonal + q
        kept = (k, kd, ux, diagonal)

    rate = rate_ref[species : species + 1, :]
    for m in range(STEPS):
        for r in range(1 + m, rows - 1 - m):

            def put(ref, slot):
                def store(s, value):
                    ref[slot, r] = value

                return store

            step_cell(
                r, m, 0, rate,
                lambda kind, r: coef_ref[r, kind],
                lambda r, s: c_ref[m, r],
                lambda r, s: t_ref[m - 1, r],
                put(c_ref, m + 1), put(t_ref, m), put(jy_ref, m),
            )

    masks = mask_ref[HALO * layers : (HALO + width) * layers, :]
    block = jnp.concatenate([t_ref[STEPS - 1, r] for r in range(HALO, HALO + width)], axis=0)
    for s, total in enumerate(picked_sums(block, hot_ref[...], masks, layers)):
        partial_ref[s : s + 1, :] = partial_in[s : s + 1, :] + total


def side_steps(rates, e, ea, eb, partial, mask, hot, spread):
    rows, layers, _ = e.shape
    species, wells = partial.shape
    state = (STEPS, rows, layers, LANES)
    return pl.pallas_call(
        functools.partial(strips_kernel, layers=layers, width=rows - 2 * HALO, species=species),
        out_shape=(
            jax.ShapeDtypeStruct((species, wells), F32),
            jax.ShapeDtypeStruct((rows, KINDS, layers, LANES), F32),
            jax.ShapeDtypeStruct(state, F32),
            jax.ShapeDtypeStruct(state, F32),
        ),
        in_specs=[VMEM] * 8,
        out_specs=[VMEM] * 4,
        scratch_shapes=[pltpu.VMEM(state, F32)],
        compiler_params=pltpu.CompilerParams(vmem_limit_bytes=6 * MIB),
        name="strip_steps",
    )(rates, e, ea, eb, partial, mask, hot, spread)


def adjoint_kernel(
    rate_ref, weight_ref, meta_ref, mask_ref, coef_in, coef_out, c_in, c_out, jy_in, jy_out,
    coef_side, c_side, jy_side, partial_ref, *rest, layers, width, species, parts,
):
    others, out_ref, lam_ref = rest[:parts], *rest[parts:]
    rows = width + 2 * HALO
    shape = (layers, LANES)
    lane = lane_of(shape)
    gx, gy = lax.axis_index("gx"), lax.axis_index(Y)
    where_y = meta_ref[3:4, :]
    counts = meta_ref[4:5, :].astype(F32)
    wells = meta_ref.shape[1]

    own, strip_species, strip_column = strip_columns(wells)
    strip_hit, own_hit = strip_column == where_y, own == where_y
    residuals = []
    for s in range(species):
        total = partial_ref[s : s + 1, :]
        for other in others:
            total = total + other[s : s + 1, :]
        factor = rate_ref[species + 1 + s, 0:1][:, None]
        residual = weight_ref[s : s + 1, :] * (total * factor) / counts
        residuals.append(residual / counts * factor)
    lam = jnp.zeros((rows * layers, (species + 1) * LANES), F32)
    for piece in range(3):
        coarse = [r.astype(BF16).astype(F32) for r in residuals]
        residuals = [r - q for r, q in zip(residuals, coarse)]
        blocks = [jnp.where(own_hit, q, 0.0).astype(BF16) for q in coarse]
        side = jnp.zeros((LANES, wells), F32)
        for s in range(species):
            side = jnp.where(strip_hit & (strip_species == s), coarse[s], side)
        spread = jnp.concatenate(blocks + [side.astype(BF16)], axis=0)
        lam = lam + lax.dot_general(mask_ref[...], spread, (((1,), (1,)), ((), ())), preferred_element_type=F32)
    for s in range(species + 1):
        lam_ref[0, :, s] = lam[:, s * LANES : (s + 1) * LANES].reshape(rows, layers, LANES)

    def main_coef(kind, r):
        return read_coef((coef_in, coef_out), kind, width, r)

    def side_coef(kind, r):
        return coef_side[r, kind]

    first_row, last_row = HALO - 1, HALO + width - 1
    sums = {}

    def add(key, term):
        sums[key] = sums[key] + term if key in sums else term

    for m in reversed(range(STEPS)):
        now = STEPS - 1 - m
        low, high = STEPS - m, rows - 1 - (STEPS - m)
        for r in range(min(low, first_row), max(high, last_row) + 1):
            sense, retreat = first_row <= r <= last_row, m > 0 and low <= r <= high
            for s in range(species + 1):
                is_side = s == species
                coef = side_coef if is_side else main_coef
                value, up = lam_ref[now, r, s], lam_ref[now, r + 1, s]
                after = y_next(value)
                if sense:
                    if is_side:
                        jump = c_side[m, r + 1] - c_side[m, r]
                    else:
                        states = (c_in, c_out)
                        jump = read_state(states, m, width, r + 1, s) - read_state(states, m, width, r, s)
                    add(("x", is_side, r), jump * (up - value))
                    if r >= HALO:
                        if is_side:
                            jump = jy_side[m, r]
                        else:
                            which, index = state_row(m + 1, width)(r)
                            jump = (jy_in, jy_out)[which][m, index, s]
                        add(("y", is_side, r), jump * (after - value))
                if retreat:
                    lam_ref[now + 1, r, s] = (
                        (rate_ref[s : s + 1, :] - coef(D, r)) * value
                        + coef(PX, r) * up
                        + coef(QX, r - 1) * lam_ref[now, r - 1, s]
                        + coef(PY, r) * after
                        + coef(QYM, r) * y_previous(value)
                        + RATE * z_pair(value)
                    )

    column, left = lane % GROUP, lane < RIGHT
    first_y, last_y = gy == 0, gy == lax.axis_size(Y) - 1
    side_mask = jnp.where(
        left, jnp.where(first_y & (column < 8), 0.0, 1.0), jnp.where(last_y & (column >= 7), 0.0, 1.0)
    ).astype(F32)
    inside_low = jnp.where(gx > 0, 1.0, 0.0).astype(F32)
    inside_high = jnp.where(gx < lax.axis_size("gx") - 1, 1.0, 0.0).astype(F32)
    for x in range(width):
        r = x + HALO
        totals = []
        for is_side in (False, True):
            upper, lower = sums["x", is_side, r], sums["x", is_side, r - 1]
            if x == 0:
                lower = lower * inside_low
            if x == width - 1:
                upper = upper * inside_high
            along_y = sums["y", is_side, r]
            if is_side:
                along_y = along_y * side_mask
            totals.append(upper + lower + along_y + y_previous(along_y))
        total, side = totals
        all_species = side
        for s in range(1, species):
            all_species = all_species + roll(side, -GROUP * s, 1)
        total = jnp.where(lane < STEPS, roll(all_species, -8, 1), total)
        total = jnp.where(lane >= LANES - STEPS, roll(all_species, 120 - RIGHT, 1), total)
        out_ref[pl.ds(x, layers, stride=width), :] = -HALF_DT * main_coef(K, r) * total


def adjoint(rates, weight, meta, mask, inner, outer, side, partials):
    (coef_in, c_in, jy_in), (coef_out, c_out, jy_out) = inner, outer
    _, width, species, layers, _ = c_in.shape
    parts = len(partials) - 1
    operands = (rates, weight, meta, mask, coef_in, coef_out, c_in, c_out, jy_in, jy_out, *side, *partials)
    return pl.pallas_call(
        functools.partial(adjoint_kernel, layers=layers, width=width, species=species, parts=parts),
        out_shape=jax.ShapeDtypeStruct((layers * width, LANES), F32),
        in_specs=[VMEM] * len(operands),
        out_specs=VMEM,
        scratch_shapes=[pltpu.VMEM((STEPS, width + 2 * HALO, species + 1, layers, LANES), F32)],
        compiler_params=pltpu.CompilerParams(vmem_limit_bytes=12 * MIB),
        name="adjoint_steps",
    )(*operands)


def pairs(count, start):
    return [p for i in range(start, count - 1, 2) for p in ((i, i + 1), (i + 1, i))]


def swap_x(first, second):
    count, side = lax.axis_size("gx"), lax.axis_size(Y)
    partner = dict(pairs(count, 1))
    odd = [
        (i * side + j, partner[i] * side + j if i in partner else i * side + (j ^ 1))
        for i in range(count)
        for j in range(side)
    ]
    return lax.ppermute(first, "gx", pairs(count, 0)), lax.ppermute(second, ("gx",) + Y, odd)


def swap_y(first, second):
    count = lax.axis_size(Y)
    odd = pairs(count, 1) + [(0, count - 1), (count - 1, 0)]
    return lax.ppermute(first, Y, pairs(count, 0)), lax.ppermute(second, Y, odd)


def from_others(value, axis, reach):
    count = lax.axis_size(axis)
    if count in (2, 4):
        return [lax.ppermute(value, axis, [(i, i ^ d) for i in range(count)]) for d in range(1, count)]
    return [
        lax.ppermute(value, axis, [(i, i + d) for i in range(count) if 0 <= i + d < count])
        for distance in range(1, min(reach, count - 1) + 1)
        for d in (distance, -distance)
    ]


def shards(
    initial, logk, direction, face_speed, face_flags, retard, decay, screen_cells, screen_count, well_weight
):
    species, layers, width, columns = initial.shape
    raw, xa, xb = send_rows(initial, logk, direction, face_speed, face_flags)
    xa, xb = swap_x(xa, xb)
    coef_in, c_in, t_in, jy_in, e, mask, hot, side_hot, spread, rates, meta = cone(
        retard, decay, screen_cells.T, screen_count, raw, layers, width, species
    )
    e, ea, eb = all_edges(e, xa, xb)
    ea, eb = swap_y(ea, eb)
    partial, coef_out, c_out, jy_out = rim(rates, xa, xb, coef_in, c_in, t_in, mask, hot)
    partial, *side = side_steps(rates, e, ea, eb, partial, mask, side_hot, spread)
    reach = -(-(screen_cells.shape[1] - 1 + HALO) // width)
    partials = [partial] + from_others(partial, "gx", reach)
    inner, outer = (coef_in, c_in, jy_in), (coef_out, c_out, jy_out)
    hessian = adjoint(rates, well_weight, meta, mask, inner, outer, side, partials)
    return hessian.reshape(layers, width, columns)


def solution(mesh):
    in_specs = (
        P("grp", None, "gx", Y),
        P("grp", "gx", Y),
        P("grp", "gx", Y),
        P("grp", None, "gx", Y),
        P("grp", None, "gx", Y),
        P(),
        P(),
        P("grp", None),
        P("grp"),
        P("grp", None),
    )
    return jax.shard_map(shards, mesh=mesh, in_specs=in_specs, out_specs=P("grp", "gx", Y), check_vma=False)
```

```python
import functools

import jax
import jax.numpy as jnp
from jax import lax
from jax.experimental import pallas as pl
from jax.experimental.pallas import tpu as pltpu
from jax.sharding import PartitionSpec as P

STEPS = 4
HALO = STEPS
RATE = 0.02
HALF_DT = 0.025
LANES = 128
TILE = 8
GROUP = 16
RIGHT = 64
Y = ("gy", "sa")
MIB = 1024 * 1024
PX, QX, BX, PY, QYM, QY, PYM, BY, BYM, D, K, KDIR = range(12)
KINDS = 12
VMEM = pl.BlockSpec(memory_space=pltpu.VMEM)
HBM = pl.BlockSpec(memory_space=pltpu.HBM)
F32, BF16, I32 = jnp.float32, jnp.bfloat16, jnp.int32


def in_hbm(*arrays):
    return [pltpu.with_memory_space_constraint(a, pltpu.HBM) for a in arrays]


def lane_of(shape):
    return lax.broadcasted_iota(I32, shape, len(shape) - 1)


def roll(value, shift, axis):
    return pltpu.roll(value, shift % value.shape[axis], axis)


def y_next(value):
    return roll(value, LANES - 1, 1)


def y_previous(value):
    return roll(value, 1, 1)


def pack_edges(fields):
    lane = lane_of(fields[0].shape)
    packed = jnp.zeros_like(fields[0])
    for f, field in enumerate(fields):
        packed = jnp.where(lane // GROUP == f, roll(field, 8 + GROUP * f, 1), packed)
    return packed


def z_pair(value):
    tiles = [value[i : i + TILE] for i in range(0, value.shape[0], TILE)]
    row = lax.broadcasted_iota(I32, tiles[0].shape, 0)
    ups = [roll(t, TILE - 1, 0) for t in tiles]
    downs = [roll(t, 1, 0) for t in tiles]
    pairs = []
    for i, tile in enumerate(tiles):
        above = jnp.where(row == TILE - 1, ups[i + 1] if i + 1 < len(tiles) else tile, ups[i])
        below = jnp.where(row == 0, downs[i - 1] if i else tile, downs[i])
        pairs.append(above + below)
    return jnp.concatenate(pairs, axis=0)


def state_row(m, width):
    low, high = HALO + m, HALO + width - 1 - m

    def find(r):
        if low <= r <= high:
            return 0, r - HALO
        return (1, r - m) if r < low else (1, HALO + r - high - 1)

    return find


def coef_row(kind, width):
    low, high = HALO, HALO + width - 1
    if kind in (PX, QX, BX, D):
        high -= 1
    if kind == D:
        low += 1

    def find(r):
        if low <= r <= high:
            return 0, r - HALO
        return (1, r) if r <= HALO else (1, HALO + 1 + r - (HALO + width - 1))

    return find


def read_state(refs, m, width, r, s):
    which, index = state_row(m, width)(r)
    return refs[which][m, index, s]


def read_coef(refs, kind, width, r):
    which, index = coef_row(kind, width)(r)
    return refs[which][index, kind]


def row_fields(raw, x, layers, width, species):
    initial_ref, logk_ref, direction_ref, speed_ref, flags_ref = raw
    plane = layers * width

    def take(ref, index):
        return ref[pl.ds(index * plane + x, layers, stride=width), :]

    fields = [take(initial_ref, s) for s in range(species)]
    conductance = jnp.exp(take(logk_ref, 0))
    fields += [conductance, conductance * take(direction_ref, 0)]
    for axis in range(2):
        speed = take(speed_ref, axis)
        fields.append(jnp.where(take(flags_ref, axis) == 1, speed, -speed))
    return fields


def y_coefs(k, kd, u, mask=None):
    half = HALF_DT * (k + y_next(k))
    p = half + jnp.maximum(u, 0.0)
    q = half - jnp.minimum(u, 0.0)
    b = HALF_DT * (kd + y_next(kd))
    if mask is not None:
        p, q, b = p * mask, q * mask, b * mask
    return {PY: p, QY: q, BY: b, PYM: y_previous(p), QYM: y_previous(q), BYM: y_previous(b), K: k, KDIR: kd}


def x_coefs(k, k_next, kd, kd_next, u, mask=None):
    half = HALF_DT * (k + k_next)
    p = half + jnp.maximum(u, 0.0)
    q = half - jnp.minimum(u, 0.0)
    b = HALF_DT * (kd + kd_next)
    return (p, q, b) if mask is None else (p * mask, q * mask, b * mask)


def step_cell(r, m, s, rate, coef, state, tangent, put_c, put_t, put_jy):
    kept = rate - coef(D, r)
    upper, lower = coef(QX, r), coef(PX, r - 1)
    after, before = coef(QY, r), coef(PYM, r)

    def moved(value, up, down, yp, ym):
        return kept * value + upper * up + lower * down + after * yp + before * ym + RATE * z_pair(value)

    c, up, down = state(r, s), state(r + 1, s), state(r - 1, s)
    yp, ym = y_next(c), y_previous(c)
    jump = yp - c
    source = (
        coef(BX, r) * (up - c) - coef(BX, r - 1) * (c - down) + coef(BY, r) * jump - coef(BYM, r) * (c - ym)
    )
    put_jy(s, jump)
    if m + 1 < STEPS:
        put_c(s, moved(c, up, down, yp, ym))
    if m > 0:
        t = tangent(r, s)
        source = source + moved(t, tangent(r + 1, s), tangent(r - 1, s), y_next(t), y_previous(t))
    put_t(s, source)


def once(load):
    return functools.cache(load)


def put_at(ref, m, index):
    def store(s, value):
        ref[m, index, s] = value

    return store


def picked_sums(wide, hot, masks, layers):
    picked = jnp.zeros((wide.shape[0], hot.shape[1]), F32)
    for piece in range(3):
        coarse = wide.astype(BF16)
        picked = picked + jnp.dot(coarse, hot, preferred_element_type=F32)
        wide = wide - coarse.astype(F32)
    wells = masks.shape[1]
    totals = []
    for s in range(hot.shape[1] // wells):
        total = jnp.zeros((layers, wells), F32)
        for i in range(0, wide.shape[0], layers):
            total = total + picked[i : i + layers, s * wells : (s + 1) * wells] * masks[i : i + layers].astype(F32)
        totals.append(jnp.sum(total, axis=0, keepdims=True))
    return totals


def send_kernel(*refs, layers, width, species):
    sources, raw, (xa_ref, xb_ref, sem) = refs[:5], refs[5:10], refs[10:]
    copies = [pltpu.make_async_copy(a, b, sem.at[i]) for i, (a, b) in enumerate(zip(sources, raw))]
    for copy in copies:
        copy.start()
    for copy in copies:
        copy.wait()
    even = lax.rem(lax.axis_index("gx"), 2) == 0
    for r in range(HALO):
        bottom = row_fields(raw, r, layers, width, species)
        top = row_fields(raw, width - HALO + r, layers, width, species)
        for f in range(species + 4):
            xa_ref[r, f] = jnp.where(even, top[f], bottom[f])
            xb_ref[r, f] = jnp.where(even, bottom[f], top[f])


def send_rows(initial, logk, direction, face_speed, face_flags):
    species, layers, width, _ = initial.shape
    sources = [a.reshape(-1, LANES) for a in (initial, logk, direction, face_speed, face_flags)]
    rows = jax.ShapeDtypeStruct((HALO, species + 4, layers, LANES), F32)
    *raw, xa, xb = pl.pallas_call(
        functools.partial(send_kernel, layers=layers, width=width, species=species),
        out_shape=tuple(jax.ShapeDtypeStruct(a.shape, a.dtype) for a in sources) + (rows, rows),
        in_specs=[HBM] * 5,
        out_specs=[VMEM] * 7,
        scratch_shapes=[pltpu.SemaphoreType.DMA((5,))],
        compiler_params=pltpu.CompilerParams(vmem_limit_bytes=3 * MIB),
        name="send_rows",
    )(*in_hbm(*sources))
    return raw, xa, xb


def divide(value, by):
    return lax.shift_right_logical(value, by.bit_length() - 1) if by & (by - 1) == 0 else lax.div(value, by)


def well_table(cells, counts, width):
    total_x, total_y = width * lax.axis_size("gx"), LANES * lax.axis_size(Y)
    start, second = cells[0:1], cells[1:2]
    depth = divide(start, total_x * total_y)
    rest = start - depth * (total_x * total_y)
    x = divide(rest, total_y)
    y = rest - x * total_y
    end = x + jnp.where(second > start, counts - 1, 1 - counts)
    row_start, col_start = lax.axis_index("gx") * width, lax.axis_index(Y) * LANES
    return [depth, jnp.minimum(x, end) - row_start, jnp.maximum(x, end) - row_start, y - col_start, counts]


def strip_columns(wells):
    own = lax.broadcasted_iota(I32, (LANES, wells), 0)
    return own, own % RIGHT // GROUP, own % GROUP + jnp.where(own < RIGHT, -8, 120)


def cone_kernel(
    retard_hbm, decay_hbm, cells_hbm, count_hbm, initial_ref, logk_ref, direction_ref, speed_ref, flags_ref,
    coef_ref, c_ref, t_ref, jy_ref, e_ref, mask_ref, hot_ref, side_hot_ref, spread_ref, patch_ref, rate_ref, meta_ref,
    retard_ref, decay_ref, cells_ref, count_ref, sem, *, layers, width, species,
):
    copies = [
        pltpu.make_async_copy(a, b, sem.at[i])
        for i, (a, b) in enumerate(
            ((retard_hbm, retard_ref), (decay_hbm, decay_ref), (cells_hbm, cells_ref), (count_hbm, count_ref))
        )
    ]
    for copy in copies:
        copy.start()
    raw = initial_ref, logk_ref, direction_ref, speed_ref, flags_ref
    kept = None
    for x in range(width):
        fields = row_fields(raw, x, layers, width, species)
        k, kd, ux, uy = fields[species:]
        e_ref[x] = pack_edges(fields)
        for s in range(species):
            c_ref[0, x, s] = fields[s]
        found = y_coefs(k, kd, uy)
        for kind, value in found.items():
            coef_ref[x, kind] = value
        diagonal = found[PY] + found[QYM] + 2 * RATE
        if x:
            p, q, b = x_coefs(kept[0], k, kept[1], kd, kept[2])
            coef_ref[x - 1, PX], coef_ref[x - 1, QX], coef_ref[x - 1, BX] = p, q, b
            coef_ref[x - 1, D] = kept[3] + p
            diagonal = diagonal + q
        kept = (k, kd, ux, diagonal)
    coef_ref[width - 1, D] = kept[3]
    coef_ref[width - 1, PX] = kept[2]

    for copy in copies:
        copy.wait()
    lane = lane_of((1, LANES))
    strips = jnp.full((1, LANES), retard_ref[species - 1], F32)
    rates = []
    for s in range(species):
        rate = jnp.full((1, LANES), retard_ref[s], F32)
        strips = jnp.where(lane % RIGHT // GROUP == s, rate, strips)
        factor = jnp.exp(jnp.full((1, LANES), -decay_ref[s], F32)) / rate
        rate_ref[s : s + 1, :] = rate
        rate_ref[species + 1 + s : species + 2 + s, :] = factor**STEPS
        rates.append(rate)
    rate_ref[species : species + 1, :] = strips

    for m in range(STEPS):
        coef = once(lambda kind, r: coef_ref[r - HALO, kind])
        state = once(lambda r, s: c_ref[m, r - HALO, s])
        tangent = once(lambda r, s: t_ref[m - 1, r - HALO, s])
        for r in range(HALO + 1 + m, HALO + width - 1 - m):
            x = r - HALO
            puts = put_at(c_ref, m + 1, x), put_at(t_ref, m, x), put_at(jy_ref, m, x)
            for s in range(species):
                step_cell(r, m, s, rates[s], coef, state, tangent, *puts)

    wells = meta_ref.shape[1]
    table = well_table(cells_ref, count_ref[...].reshape(1, wells), width)
    for i, row in enumerate(table):
        meta_ref[i : i + 1, :] = row
    depth, first, last, where_y = table[:4]
    in_layer = lax.broadcasted_iota(I32, (layers, wells), 0) == depth
    for r in range(width + 2 * HALO):
        inside = (first <= r - HALO) & (last >= r - HALO) & in_layer
        mask_ref[r * layers : (r + 1) * layers, :] = jnp.where(inside, 1.0, 0.0).astype(BF16)
    own, strip_species, strip_column = strip_columns(wells)
    hit = (own == where_y) & (own >= STEPS) & (own < LANES - STEPS)
    hot_ref[...] = jnp.where(hit, 1.0, 0.0).astype(BF16)
    reach = (strip_column < STEPS) & (strip_column >= -HALO)
    reach = reach | ((strip_column >= LANES - STEPS) & (strip_column < LANES + HALO))
    hit = reach & (strip_column == where_y)
    for s in range(species):
        side_hot_ref[:, s * wells : (s + 1) * wells] = jnp.where(hit & (strip_species == s), 1.0, 0.0).astype(BF16)


    source = lax.broadcasted_iota(I32, (2 * LANES, LANES), 0)
    target = lax.broadcasted_iota(I32, (2 * LANES, LANES), 1)
    target = jnp.where(target < RIGHT, 0, LANES) + target % GROUP
    for f in range(4):
        hit = source == target + (species + f) * GROUP
        spread_ref[:, f * LANES : (f + 1) * LANES] = jnp.where(hit, 1.0, 0.0).astype(BF16)
    source, target = source[:LANES], lax.broadcasted_iota(I32, (LANES, LANES), 1)
    used = (target < STEPS) | (target >= LANES - STEPS)
    same = (source < RIGHT) == (target < STEPS)
    hit = used & same & (source % RIGHT < species * GROUP) & (source % GROUP == (target + 8) % GROUP)
    patch_ref[...] = jnp.where(hit, 1.0, 0.0).astype(BF16)


def cone(retard, decay, cells, counts, raw, layers, width, species):
    wells = counts.shape[0]
    state = jax.ShapeDtypeStruct((STEPS, width, species, layers, LANES), F32)
    return pl.pallas_call(
        functools.partial(cone_kernel, layers=layers, width=width, species=species),
        out_shape=(
            jax.ShapeDtypeStruct((width, KINDS, layers, LANES), F32),
            state,
            state,
            state,
            jax.ShapeDtypeStruct((width, layers, LANES), F32),
            jax.ShapeDtypeStruct(((width + 2 * HALO) * layers, wells), BF16),
            jax.ShapeDtypeStruct((LANES, wells), BF16),
            jax.ShapeDtypeStruct((LANES, species * wells), BF16),
            jax.ShapeDtypeStruct((2 * LANES, 4 * LANES), BF16),
            jax.ShapeDtypeStruct((LANES, LANES), BF16),
            jax.ShapeDtypeStruct((2 * species + 2, LANES), F32),
            jax.ShapeDtypeStruct((TILE, wells), I32),
        ),
        in_specs=[HBM] * 4 + [VMEM] * 5,
        out_specs=[VMEM] * 12,
        scratch_shapes=[
            pltpu.SMEM(retard.shape, F32),
            pltpu.SMEM(decay.shape, F32),
            pltpu.VMEM(cells.shape, I32),
            pltpu.VMEM(counts.shape, I32),
            pltpu.SemaphoreType.DMA((4,)),
        ],
        compiler_params=pltpu.CompilerParams(vmem_limit_bytes=4 * MIB),
        cost_estimate=pl.CostEstimate(flops=10**7, bytes_accessed=10**7, transcendentals=0),
        name="cone_steps",
    )(*in_hbm(retard, decay, cells, counts), *raw)


def neighbour_row(r, a_ref, b_ref, width):
    even = lax.rem(lax.axis_index("gx"), 2) == 0
    from_a = even if r >= HALO else jnp.logical_not(even)
    index = r % (HALO + width)
    return [jnp.where(from_a, a_ref[index, f], b_ref[index, f]) for f in range(a_ref.shape[1])]


def edges_kernel(e_ref, xa_ref, xb_ref, all_ref, a_ref, b_ref, *, width):
    rows = width + 2 * HALO
    half = rows // 2
    even = lax.rem(lax.axis_index(Y), 2) == 0
    edges = {}
    for r in range(rows):
        inner = HALO <= r < HALO + width
        edges[r] = e_ref[r - HALO] if inner else pack_edges(neighbour_row(r, xa_ref, xb_ref, width))
        all_ref[r] = edges[r]
    near = lane_of(edges[0].shape) % GROUP < 8
    for r in range(half):
        one, two = edges[r], edges[r + half]
        to_right = jnp.where(near, one, roll(two, 8, 1))
        to_left = jnp.where(near, roll(two, -8, 1), one)
        a_ref[r] = jnp.where(even, to_right, to_left)
        b_ref[r] = jnp.where(even, to_left, to_right)


def outer_edges(r, a_ref, b_ref, near):
    half = a_ref.shape[0]
    even = lax.rem(lax.axis_index(Y), 2) == 0
    if r < half:
        return jnp.where(near == even, b_ref[r], a_ref[r])
    both = jnp.where(near == even, a_ref[r - half], b_ref[r - half])
    return jnp.where(near, roll(both, -8, 1), roll(both, 8, 1))


def all_edges(e, xa, xb):
    width, layers, _ = e.shape
    return pl.pallas_call(
        functools.partial(edges_kernel, width=width),
        out_shape=(
            jax.ShapeDtypeStruct((width + 2 * HALO, layers, LANES), F32),
            jax.ShapeDtypeStruct((width // 2 + HALO, layers, LANES), F32),
            jax.ShapeDtypeStruct((width // 2 + HALO, layers, LANES), F32),
        ),
        in_specs=[VMEM] * 3,
        out_specs=[VMEM] * 3,
        compiler_params=pltpu.CompilerParams(vmem_limit_bytes=1 * MIB),
        name="edge_columns",
    )(e, xa, xb)


def rim_kernel(
    rate_ref, xa_ref, xb_ref, coef_in, c_in, t_in, mask_ref, hot_ref,
    partial_ref, coef_out, c_out, jy_out, t_out, *, layers, width, species,
):
    gx = lax.axis_index("gx")
    rows = width + 2 * HALO
    coefs = (coef_in, coef_out)
    last = HALO + width - 1
    get = lambda kind, r: read_coef(coefs, kind, width, r)

    def put_coef(kind, r, value):
        which, index = coef_row(kind, width)(r)
        coefs[which][index, kind] = value

    speeds = {last: coef_in[width - 1, PX]}
    for r in list(range(HALO)) + list(range(HALO + width, rows)):
        fields = neighbour_row(r, xa_ref, xb_ref, width)
        k, kd, speeds[r], uy = fields[species:]
        index = state_row(0, width)(r)[1]
        for s in range(species):
            c_out[0, index, s] = fields[s]
        for kind, value in y_coefs(k, kd, uy).items():
            put_coef(kind, r, value)
    inside_low = jnp.where(gx > 0, 1.0, 0.0).astype(F32)
    inside_high = jnp.where(gx < lax.axis_size("gx") - 1, 1.0, 0.0).astype(F32)
    for r in list(range(HALO)) + list(range(last, rows - 1)):
        mask = inside_low if r < HALO else inside_high
        values = x_coefs(get(K, r), get(K, r + 1), get(KDIR, r), get(KDIR, r + 1), speeds[r], mask)
        for kind, value in zip((PX, QX, BX), values):
            put_coef(kind, r, value)
    for r in list(range(1, HALO + 1)) + list(range(last, rows - 1)):
        if r == HALO:
            value = coef_in[0, D] + get(QX, r - 1)
        elif r == last:
            value = coef_in[width - 1, D] + get(PX, r)
        else:
            value = get(PY, r) + get(QYM, r) + 2 * RATE + get(PX, r) + get(QX, r - 1)
        put_coef(D, r, value)

    for m in range(STEPS):
        coef = once(get)
        state = once(lambda r, s: read_state((c_in, c_out), m, width, r, s))
        tangent = once(lambda r, s: tangent_row(t_in, t_out, m, width, r)[s])
        for r in list(range(1 + m, HALO + 1 + m)) + list(range(last - m, rows - 1 - m)):
            index = state_row(m + 1, width)(r)[1]
            puts = put_at(c_out, m + 1, index), put_at(t_out, m, index), put_at(jy_out, m, index)
            for s in range(species):
                step_cell(r, m, s, rate_ref[s : s + 1, :], coef, state, tangent, *puts)

    masks = mask_ref[HALO * layers : (HALO + width) * layers, :]
    for s in range(species):
        block = [tangent_row(t_in, t_out, STEPS, width, r)[s] for r in range(HALO, HALO + width)]
        partial_ref[s : s + 1, :] = picked_sums(jnp.concatenate(block, axis=0), hot_ref[...], masks, layers)[0]


def tangent_row(t_in, t_out, m, width, r):
    which, index = state_row(m, width)(r)
    return (t_in, t_out)[which].at[m - 1, index]


def rim(rates, xa, xb, coef, c, t, mask, hot):
    _, width, species, layers, _ = c.shape
    wells = mask.shape[1]
    state = (STEPS, 2 * HALO, species, layers, LANES)
    return pl.pallas_call(
        functools.partial(rim_kernel, layers=layers, width=width, species=species),
        out_shape=(
            jax.ShapeDtypeStruct((species, wells), F32),
            jax.ShapeDtypeStruct((2 * HALO + 2, KINDS, layers, LANES), F32),
            jax.ShapeDtypeStruct(state, F32),
            jax.ShapeDtypeStruct(state, F32),
        ),
        in_specs=[VMEM] * 8,
        out_specs=[VMEM] * 4,
        scratch_shapes=[pltpu.VMEM(state, F32)],
        compiler_params=pltpu.CompilerParams(vmem_limit_bytes=6 * MIB),
        cost_estimate=pl.CostEstimate(flops=10**7, bytes_accessed=10**7, transcendentals=0),
        name="rim_steps",
    )(rates, xa, xb, coef, c, t, mask, hot)


def strips_kernel(
    rate_ref, e_ref, ea_ref, eb_ref, partial_in, mask_ref, hot_ref, spread_ref,
    partial_ref, coef_ref, c_ref, jy_ref, t_ref, *, layers, width, species,
):
    shape = (layers, LANES)
    rows = width + 2 * HALO
    lane = lane_of(shape)
    column = lane % GROUP
    near, left = column < 8, lane < RIGHT
    gx, gy = lax.axis_index("gx"), lax.axis_index(Y)
    first_y, last_y = gy == 0, gy == lax.axis_size(Y) - 1
    mask = jnp.where(
        left, jnp.where(first_y & near, 0.0, 1.0), jnp.where(last_y & (column >= 7), 0.0, 1.0)
    ).astype(F32)
    inside_low = jnp.where(gx > 0, 1.0, 0.0).astype(F32)
    inside_high = jnp.where(gx < lax.axis_size("gx") - 1, 1.0, 0.0).astype(F32)
    both = []
    for r in range(rows):
        own, outer = e_ref[r], outer_edges(r, ea_ref, eb_ref, near)
        left_strip, right_strip = jnp.where(near, outer, own), jnp.where(near, own, outer)
        c_ref[0, r] = jnp.where(left, left_strip, roll(right_strip, RIGHT, 1))
        both.append(jnp.concatenate([left_strip, right_strip], axis=1))
    rest = jnp.concatenate(both, axis=0)
    fields = jnp.zeros((rows * layers, 4 * LANES), F32)
    for piece in range(3):
        coarse = rest.astype(BF16)
        fields = fields + jnp.dot(coarse, spread_ref[...], preferred_element_type=F32)
        rest = rest - coarse.astype(F32)

    kept = None
    for r in range(rows):
        k, kd, ux, uy = [fields[r * layers : (r + 1) * layers, f * LANES : (f + 1) * LANES] for f in range(4)]
        found = y_coefs(k, kd, uy, mask)
        for kind, value in found.items():
            coef_ref[r, kind] = value
        diagonal = found[PY] + found[QYM] + 2 * RATE
        if r:
            inside = inside_low if r <= HALO else inside_high if r >= HALO + width else None
            p, q, b = x_coefs(kept[0], k, kept[1], kd, kept[2], inside)
            coef_ref[r - 1, PX], coef_ref[r - 1, QX], coef_ref[r - 1, BX] = p, q, b
            coef_ref[r - 1, D] = kept[3] + p
            diagonal = diagonal + q
        kept = (k, kd, ux, diagonal)

    def put(ref, m, r):
        def store(s, value):
            ref[m, r] = value

        return store

    rate = rate_ref[species : species + 1, :]
    for m in range(STEPS):
        coef = once(lambda kind, r: coef_ref[r, kind])
        state = once(lambda r, s: c_ref[m, r])
        tangent = once(lambda r, s: t_ref[m - 1, r])
        for r in range(1 + m, rows - 1 - m):
            step_cell(r, m, 0, rate, coef, state, tangent, put(c_ref, m + 1, r), put(t_ref, m, r), put(jy_ref, m, r))

    masks = mask_ref[HALO * layers : (HALO + width) * layers, :]
    block = jnp.concatenate([t_ref[STEPS - 1, r] for r in range(HALO, HALO + width)], axis=0)
    for s, total in enumerate(picked_sums(block, hot_ref[...], masks, layers)):
        partial_ref[s : s + 1, :] = partial_in[s : s + 1, :] + total


def side_steps(rates, e, ea, eb, partial, mask, hot, spread):
    rows, layers, _ = e.shape
    species, wells = partial.shape
    state = (STEPS, rows, layers, LANES)
    return pl.pallas_call(
        functools.partial(strips_kernel, layers=layers, width=rows - 2 * HALO, species=species),
        out_shape=(
            jax.ShapeDtypeStruct((species, wells), F32),
            jax.ShapeDtypeStruct((rows, KINDS, layers, LANES), F32),
            jax.ShapeDtypeStruct(state, F32),
            jax.ShapeDtypeStruct(state, F32),
        ),
        in_specs=[VMEM] * 8,
        out_specs=[VMEM] * 4,
        scratch_shapes=[pltpu.VMEM(state, F32)],
        compiler_params=pltpu.CompilerParams(vmem_limit_bytes=6 * MIB),
        name="strip_steps",
    )(rates, e, ea, eb, partial, mask, hot, spread)


def adjoint_kernel(
    rate_ref, weight_ref, meta_ref, mask_ref, coef_in, coef_out, c_in, c_out, jy_in, jy_out,
    coef_side, c_side, jy_side, patch_ref, partial_ref, *rest, layers, width, species, parts,
):
    others, out_ref, lam_ref = rest[:parts], *rest[parts:]
    rows = width + 2 * HALO
    shape = (layers, LANES)
    lane = lane_of(shape)
    gx, gy = lax.axis_index("gx"), lax.axis_index(Y)
    where_y = meta_ref[3:4, :]
    counts = meta_ref[4:5, :].astype(F32)
    wells = meta_ref.shape[1]

    own, strip_species, strip_column = strip_columns(wells)
    strip_hit, own_hit = strip_column == where_y, own == where_y
    residuals = []
    for s in range(species):
        total = partial_ref[s : s + 1, :]
        for other in others:
            total = total + other[s : s + 1, :]
        factor = rate_ref[species + 1 + s, 0:1][:, None]
        residual = weight_ref[s : s + 1, :] * (total * factor) / counts
        residuals.append(residual / counts * factor)
    lam = jnp.zeros((rows * layers, (species + 1) * LANES), F32)
    for piece in range(3):
        coarse = [r.astype(BF16).astype(F32) for r in residuals]
        residuals = [r - q for r, q in zip(residuals, coarse)]
        blocks = [jnp.where(own_hit, q, 0.0).astype(BF16) for q in coarse]
        side = jnp.zeros((LANES, wells), F32)
        for s in range(species):
            side = jnp.where(strip_hit & (strip_species == s), coarse[s], side)
        spread = jnp.concatenate(blocks + [side.astype(BF16)], axis=0)
        lam = lam + lax.dot_general(mask_ref[...], spread, (((1,), (1,)), ((), ())), preferred_element_type=F32)
    for s in range(species + 1):
        lam_ref[0, :, s] = lam[:, s * LANES : (s + 1) * LANES].reshape(rows, layers, LANES)

    def main_coef(kind, r):
        return read_coef((coef_in, coef_out), kind, width, r)

    def side_coef(kind, r):
        return coef_side[r, kind]

    first_row, last_row = HALO - 1, HALO + width - 1
    sums = {}

    def add(key, term):
        sums[key] = sums[key] + term if key in sums else term

    rates = [rate_ref[s : s + 1, :] for s in range(species + 1)]
    for m in reversed(range(STEPS)):
        now = STEPS - 1 - m
        low, high = STEPS - m, rows - 1 - (STEPS - m)
        lam_row = once(lambda r, s: lam_ref[now, r, s])
        main, side = once(main_coef), once(side_coef)
        state = once(lambda r, s: c_side[m, r] if s == species else read_state((c_in, c_out), m, width, r, s))
        for r in range(min(low, first_row), max(high, last_row) + 1):
            sense, retreat = first_row <= r <= last_row, m > 0 and low <= r <= high
            results = []
            for s in range(species + 1):
                is_side = s == species
                coef = side if is_side else main
                value, up = lam_row(r, s), lam_row(r + 1, s)
                after = y_next(value)
                if sense:
                    add(("x", is_side, r), (state(r + 1, s) - state(r, s)) * (up - value))
                    if r >= HALO:
                        if is_side:
                            jump = jy_side[m, r]
                        else:
                            which, index = state_row(m + 1, width)(r)
                            jump = (jy_in, jy_out)[which][m, index, s]
                        add(("y", is_side, r), jump * (after - value))
                if retreat:
                    results.append(
                        (rates[s] - coef(D, r)) * value
                        + coef(PX, r) * up
                        + coef(QX, r - 1) * lam_row(r - 1, s)
                        + coef(PY, r) * after
                        + coef(QYM, r) * y_previous(value)
                        + RATE * z_pair(value)
                    )
            for s, result in enumerate(results):
                lam_ref[now + 1, r, s] = result

    column, left = lane % GROUP, lane < RIGHT
    first_y, last_y = gy == 0, gy == lax.axis_size(Y) - 1
    side_mask = jnp.where(
        left, jnp.where(first_y & (column < 8), 0.0, 1.0), jnp.where(last_y & (column >= 7), 0.0, 1.0)
    ).astype(F32)
    inside_low = jnp.where(gx > 0, 1.0, 0.0).astype(F32)
    inside_high = jnp.where(gx < lax.axis_size("gx") - 1, 1.0, 0.0).astype(F32)

    sides, results = [], []
    for is_side in (True, False):
        lower = None
        for r in range(HALO - 1, HALO + width):
            upper, along_y = sums["x", is_side, r], sums.get(("y", is_side, r))
            if r < HALO:
                lower = upper * inside_low
                continue
            if r == HALO + width - 1:
                upper = upper * inside_high
            if is_side:
                along_y = along_y * side_mask
            total = upper + lower + along_y + y_previous(along_y)
            lower = upper
            if is_side:
                sides.append(total)
                if len(sides) == width:
                    rest = jnp.concatenate(sides, axis=0)
                    patch = jnp.zeros_like(rest)
                    for piece in range(3):
                        coarse = rest.astype(BF16)
                        patch = patch + jnp.dot(coarse, patch_ref[...], preferred_element_type=F32)
                        rest = rest - coarse.astype(F32)
            else:
                x = r - HALO
                total = jnp.where(
                    (lane < STEPS) | (lane >= LANES - STEPS), patch[x * layers : (x + 1) * layers], total
                )
                results.append(-HALF_DT * main_coef(K, r) * total)
    for x, result in enumerate(results):
        out_ref[pl.ds(x, layers, stride=width), :] = result


def adjoint(rates, weight, meta, mask, inner, outer, side, patch, partials):
    (coef_in, c_in, jy_in), (coef_out, c_out, jy_out) = inner, outer
    _, width, species, layers, _ = c_in.shape
    parts = len(partials) - 1
    operands = (rates, weight, meta, mask, coef_in, coef_out, c_in, c_out, jy_in, jy_out, *side, patch, *partials)
    return pl.pallas_call(
        functools.partial(adjoint_kernel, layers=layers, width=width, species=species, parts=parts),
        out_shape=jax.ShapeDtypeStruct((layers * width, LANES), F32),
        in_specs=[VMEM] * len(operands),
        out_specs=VMEM,
        scratch_shapes=[pltpu.VMEM((STEPS, width + 2 * HALO, species + 1, layers, LANES), F32)],
        compiler_params=pltpu.CompilerParams(vmem_limit_bytes=12 * MIB),
        name="adjoint_steps",
    )(*operands)


def pairs(count, start):
    return [p for i in range(start, count - 1, 2) for p in ((i, i + 1), (i + 1, i))]


def swap_x(first, second):
    count, side = lax.axis_size("gx"), lax.axis_size(Y)
    partner = dict(pairs(count, 1))
    odd = [
        (i * side + j, partner[i] * side + j if i in partner else i * side + (j ^ 1))
        for i in range(count)
        for j in range(side)
    ]
    return lax.ppermute(first, "gx", pairs(count, 0)), lax.ppermute(second, ("gx",) + Y, odd)


def swap_y(first, second):
    count = lax.axis_size(Y)
    odd = pairs(count, 1) + [(0, count - 1), (count - 1, 0)]
    return lax.ppermute(first, Y, pairs(count, 0)), lax.ppermute(second, Y, odd)


def from_others(value, axis, reach):
    count = lax.axis_size(axis)
    if count in (2, 4):
        return [lax.ppermute(value, axis, [(i, i ^ d) for i in range(count)]) for d in range(1, count)]
    return [
        lax.ppermute(value, axis, [(i, i + d) for i in range(count) if 0 <= i + d < count])
        for distance in range(1, min(reach, count - 1) + 1)
        for d in (distance, -distance)
    ]


def shards(
    initial, logk, direction, face_speed, face_flags, retard, decay, screen_cells, screen_count, well_weight
):
    species, layers, width, columns = initial.shape
    raw, xa, xb = send_rows(initial, logk, direction, face_speed, face_flags)
    xa, xb = swap_x(xa, xb)
    coef_in, c_in, t_in, jy_in, e, mask, hot, side_hot, spread, patch, rates, meta = cone(
        retard, decay, screen_cells.T, screen_count, raw, layers, width, species
    )
    e, ea, eb = all_edges(e, xa, xb)
    ea, eb = swap_y(ea, eb)
    partial, coef_out, c_out, jy_out = rim(rates, xa, xb, coef_in, c_in, t_in, mask, hot)
    partial, *side = side_steps(rates, e, ea, eb, partial, mask, side_hot, spread)
    reach = -(-(screen_cells.shape[1] - 1 + HALO) // width)
    partials = [partial] + from_others(partial, "gx", reach)
    inner, outer = (coef_in, c_in, jy_in), (coef_out, c_out, jy_out)
    hessian = adjoint(rates, well_weight, meta, mask, inner, outer, side, patch, partials)
    return hessian.reshape(layers, width, columns)


def solution(mesh):
    in_specs = (
        P("grp", None, "gx", Y),
        P("grp", "gx", Y),
        P("grp", "gx", Y),
        P("grp", None, "gx", Y),
        P("grp", None, "gx", Y),
        P(),
        P(),
        P("grp", None),
        P("grp"),
        P("grp", None),
    )
    return jax.shard_map(shards, mesh=mesh, in_specs=in_specs, out_specs=P("grp", "gx", Y), check_vma=False)
```

```python
import functools

import jax
import jax.numpy as jnp
from jax import lax
from jax.experimental import pallas as pl
from jax.experimental.pallas import tpu as pltpu
from jax.sharding import PartitionSpec as P

STEPS = 4
HALO = STEPS
RATE = 0.02
HALF_DT = 0.025
LANES = 128
TILE = 8
GROUP = 16
RIGHT = 64
Y = ("gy", "sa")
MIB = 1024 * 1024
PX, QX, BX, PY, QYM, QY, PYM, BY, BYM, D, K, KDIR = range(12)
KINDS = 12
VMEM = pl.BlockSpec(memory_space=pltpu.VMEM)
HBM = pl.BlockSpec(memory_space=pltpu.HBM)
F32, BF16, I32 = jnp.float32, jnp.bfloat16, jnp.int32


def in_hbm(*arrays):
    return [pltpu.with_memory_space_constraint(a, pltpu.HBM) for a in arrays]


def lane_of(shape):
    return lax.broadcasted_iota(I32, shape, len(shape) - 1)


def roll(value, shift, axis):
    return pltpu.roll(value, shift % value.shape[axis], axis)


def y_next(value):
    return roll(value, LANES - 1, 1)


def y_previous(value):
    return roll(value, 1, 1)


def pack_edges(fields):
    lane = lane_of(fields[0].shape)
    packed = jnp.zeros_like(fields[0])
    for f, field in enumerate(fields):
        packed = jnp.where(lane // GROUP == f, roll(field, 8 + GROUP * f, 1), packed)
    return packed


def z_pair(value):
    tiles = [value[i : i + TILE] for i in range(0, value.shape[0], TILE)]
    row = lax.broadcasted_iota(I32, tiles[0].shape, 0)
    ups = [roll(t, TILE - 1, 0) for t in tiles]
    downs = [roll(t, 1, 0) for t in tiles]
    pairs = []
    for i, tile in enumerate(tiles):
        above = jnp.where(row == TILE - 1, ups[i + 1] if i + 1 < len(tiles) else tile, ups[i])
        below = jnp.where(row == 0, downs[i - 1] if i else tile, downs[i])
        pairs.append(above + below)
    return jnp.concatenate(pairs, axis=0)


def state_row(m, width):
    low, high = HALO + m, HALO + width - 1 - m

    def find(r):
        if low <= r <= high:
            return 0, r - HALO
        return (1, r - m) if r < low else (1, HALO + r - high - 1)

    return find


def coef_row(kind, width):
    low, high = HALO, HALO + width - 1
    if kind in (PX, QX, BX, D):
        high -= 1
    if kind == D:
        low += 1

    def find(r):
        if low <= r <= high:
            return 0, r - HALO
        return (1, r) if r <= HALO else (1, HALO + 1 + r - (HALO + width - 1))

    return find


def read_state(refs, m, width, r, s):
    which, index = state_row(m, width)(r)
    return refs[which][m, index, s]


def read_coef(refs, kind, width, r):
    which, index = coef_row(kind, width)(r)
    return refs[which][index, kind]


def row_fields(raw, x, layers, width, species):
    initial_ref, logk_ref, direction_ref, speed_ref, flags_ref = raw
    plane = layers * width

    def take(ref, index):
        return ref[pl.ds(index * plane + x, layers, stride=width), :]

    fields = [take(initial_ref, s) for s in range(species)]
    conductance = jnp.exp(take(logk_ref, 0))
    fields += [conductance, conductance * take(direction_ref, 0)]
    for axis in range(2):
        speed = take(speed_ref, axis)
        fields.append(jnp.where(take(flags_ref, axis) == 1, speed, -speed))
    return fields


def y_coefs(k, kd, u, mask=None):
    half = HALF_DT * (k + y_next(k))
    p = half + jnp.maximum(u, 0.0)
    q = half - jnp.minimum(u, 0.0)
    b = HALF_DT * (kd + y_next(kd))
    if mask is not None:
        p, q, b = p * mask, q * mask, b * mask
    return {PY: p, QY: q, BY: b, PYM: y_previous(p), QYM: y_previous(q), BYM: y_previous(b), K: k, KDIR: kd}


def x_coefs(k, k_next, kd, kd_next, u, mask=None):
    half = HALF_DT * (k + k_next)
    p = half + jnp.maximum(u, 0.0)
    q = half - jnp.minimum(u, 0.0)
    b = HALF_DT * (kd + kd_next)
    return (p, q, b) if mask is None else (p * mask, q * mask, b * mask)


def step_cell(r, m, s, rate, coef, state, tangent, put_c, put_t, put_jy):
    kept = rate - coef(D, r)
    upper, lower = coef(QX, r), coef(PX, r - 1)
    after, before = coef(QY, r), coef(PYM, r)

    def moved(value, up, down, yp, ym):
        return kept * value + upper * up + lower * down + after * yp + before * ym + RATE * z_pair(value)

    c, up, down = state(r, s), state(r + 1, s), state(r - 1, s)
    yp, ym = y_next(c), y_previous(c)
    jump = yp - c
    source = (
        coef(BX, r) * (up - c) - coef(BX, r - 1) * (c - down) + coef(BY, r) * jump - coef(BYM, r) * (c - ym)
    )
    put_jy(s, jump)
    if m + 1 < STEPS:
        put_c(s, moved(c, up, down, yp, ym))
    if m > 0:
        t = tangent(r, s)
        source = source + moved(t, tangent(r + 1, s), tangent(r - 1, s), y_next(t), y_previous(t))
    put_t(s, source)


def pieces_of(value, axis):
    parts = []
    for _ in range(3):
        parts.append(value.astype(BF16))
        value = value - parts[-1].astype(F32)
    return jnp.concatenate(parts, axis=axis)


def once(load):
    return functools.cache(load)


def put_at(ref, m, index):
    def store(s, value):
        ref[m, index, s] = value

    return store


def picked_sums(wide, hot, masks, layers):
    picked = jnp.dot(pieces_of(wide, 1), jnp.concatenate([hot] * 3, axis=0), preferred_element_type=F32)
    wells = masks.shape[1]
    totals = []
    for s in range(hot.shape[1] // wells):
        total = jnp.zeros((layers, wells), F32)
        for i in range(0, wide.shape[0], layers):
            total = total + picked[i : i + layers, s * wells : (s + 1) * wells] * masks[i : i + layers].astype(F32)
        totals.append(jnp.sum(total, axis=0, keepdims=True))
    return totals


def send_kernel(*refs, layers, width, species):
    sources, raw, (xa_ref, xb_ref, sem) = refs[:5], refs[5:10], refs[10:]
    copies = [pltpu.make_async_copy(a, b, sem.at[i]) for i, (a, b) in enumerate(zip(sources, raw))]
    for copy in copies:
        copy.start()
    for copy in copies:
        copy.wait()
    even = lax.rem(lax.axis_index("gx"), 2) == 0
    for r in range(HALO):
        bottom = row_fields(raw, r, layers, width, species)
        top = row_fields(raw, width - HALO + r, layers, width, species)
        for f in range(species + 4):
            xa_ref[r, f] = jnp.where(even, top[f], bottom[f])
            xb_ref[r, f] = jnp.where(even, bottom[f], top[f])


def send_rows(initial, logk, direction, face_speed, face_flags):
    species, layers, width, _ = initial.shape
    sources = [a.reshape(-1, LANES) for a in (initial, logk, direction, face_speed, face_flags)]
    rows = jax.ShapeDtypeStruct((HALO, species + 4, layers, LANES), F32)
    *raw, xa, xb = pl.pallas_call(
        functools.partial(send_kernel, layers=layers, width=width, species=species),
        out_shape=tuple(jax.ShapeDtypeStruct(a.shape, a.dtype) for a in sources) + (rows, rows),
        in_specs=[HBM] * 5,
        out_specs=[VMEM] * 7,
        scratch_shapes=[pltpu.SemaphoreType.DMA((5,))],
        compiler_params=pltpu.CompilerParams(vmem_limit_bytes=3 * MIB),
        name="send_rows",
    )(*in_hbm(*sources))
    return raw, xa, xb


def divide(value, by):
    return lax.shift_right_logical(value, by.bit_length() - 1) if by & (by - 1) == 0 else lax.div(value, by)


def well_table(cells, counts, width):
    total_x, total_y = width * lax.axis_size("gx"), LANES * lax.axis_size(Y)
    start, second = cells[0:1], cells[1:2]
    depth = divide(start, total_x * total_y)
    rest = start - depth * (total_x * total_y)
    x = divide(rest, total_y)
    y = rest - x * total_y
    end = x + jnp.where(second > start, counts - 1, 1 - counts)
    row_start, col_start = lax.axis_index("gx") * width, lax.axis_index(Y) * LANES
    return [depth, jnp.minimum(x, end) - row_start, jnp.maximum(x, end) - row_start, y - col_start, counts]


def strip_columns(wells):
    own = lax.broadcasted_iota(I32, (LANES, wells), 0)
    return own, own % RIGHT // GROUP, own % GROUP + jnp.where(own < RIGHT, -8, 120)


def cone_kernel(
    retard_hbm, decay_hbm, cells_hbm, count_hbm, initial_ref, logk_ref, direction_ref, speed_ref, flags_ref,
    coef_ref, c_ref, t_ref, jy_ref, e_ref, mask_ref, hot_ref, side_hot_ref, spread_ref, patch_ref, rate_ref, meta_ref,
    retard_ref, decay_ref, cells_ref, count_ref, sem, *, layers, width, species,
):
    copies = [
        pltpu.make_async_copy(a, b, sem.at[i])
        for i, (a, b) in enumerate(
            ((retard_hbm, retard_ref), (decay_hbm, decay_ref), (cells_hbm, cells_ref), (count_hbm, count_ref))
        )
    ]
    for copy in copies:
        copy.start()
    raw = initial_ref, logk_ref, direction_ref, speed_ref, flags_ref
    kept = None
    for x in range(width):
        fields = row_fields(raw, x, layers, width, species)
        k, kd, ux, uy = fields[species:]
        e_ref[x] = pack_edges(fields)
        for s in range(species):
            c_ref[0, x, s] = fields[s]
        found = y_coefs(k, kd, uy)
        for kind, value in found.items():
            coef_ref[x, kind] = value
        diagonal = found[PY] + found[QYM] + 2 * RATE
        if x:
            p, q, b = x_coefs(kept[0], k, kept[1], kd, kept[2])
            coef_ref[x - 1, PX], coef_ref[x - 1, QX], coef_ref[x - 1, BX] = p, q, b
            coef_ref[x - 1, D] = kept[3] + p
            diagonal = diagonal + q
        kept = (k, kd, ux, diagonal)
    coef_ref[width - 1, D] = kept[3]
    coef_ref[width - 1, PX] = kept[2]

    for copy in copies:
        copy.wait()
    lane = lane_of((1, LANES))
    strips = jnp.full((1, LANES), retard_ref[species - 1], F32)
    rates = []
    for s in range(species):
        rate = jnp.full((1, LANES), retard_ref[s], F32)
        strips = jnp.where(lane % RIGHT // GROUP == s, rate, strips)
        factor = jnp.exp(jnp.full((1, LANES), -decay_ref[s], F32)) / rate
        rate_ref[s : s + 1, :] = rate
        rate_ref[species + 1 + s : species + 2 + s, :] = factor**STEPS
        rates.append(rate)
    rate_ref[species : species + 1, :] = strips

    for m in range(STEPS):
        coef = once(lambda kind, r: coef_ref[r - HALO, kind])
        state = once(lambda r, s: c_ref[m, r - HALO, s])
        tangent = once(lambda r, s: t_ref[m - 1, r - HALO, s])
        for r in range(HALO + 1 + m, HALO + width - 1 - m):
            x = r - HALO
            puts = put_at(c_ref, m + 1, x), put_at(t_ref, m, x), put_at(jy_ref, m, x)
            for s in range(species):
                step_cell(r, m, s, rates[s], coef, state, tangent, *puts)

    wells = meta_ref.shape[1]
    table = well_table(cells_ref, count_ref[...].reshape(1, wells), width)
    for i, row in enumerate(table):
        meta_ref[i : i + 1, :] = row
    depth, first, last, where_y = table[:4]
    in_layer = lax.broadcasted_iota(I32, (layers, wells), 0) == depth
    for r in range(width + 2 * HALO):
        inside = (first <= r - HALO) & (last >= r - HALO) & in_layer
        mask_ref[r * layers : (r + 1) * layers, :] = jnp.where(inside, 1.0, 0.0).astype(BF16)
    own, strip_species, strip_column = strip_columns(wells)
    hit = (own == where_y) & (own >= STEPS) & (own < LANES - STEPS)
    hot_ref[...] = jnp.where(hit, 1.0, 0.0).astype(BF16)
    reach = (strip_column < STEPS) & (strip_column >= -HALO)
    reach = reach | ((strip_column >= LANES - STEPS) & (strip_column < LANES + HALO))
    hit = reach & (strip_column == where_y)
    for s in range(species):
        side_hot_ref[:, s * wells : (s + 1) * wells] = jnp.where(hit & (strip_species == s), 1.0, 0.0).astype(BF16)


    source = lax.broadcasted_iota(I32, (2 * LANES, LANES), 0)
    target = lax.broadcasted_iota(I32, (2 * LANES, LANES), 1)
    target = jnp.where(target < RIGHT, 0, LANES) + target % GROUP
    for f in range(4):
        hit = source == target + (species + f) * GROUP
        spread_ref[:, f * LANES : (f + 1) * LANES] = jnp.where(hit, 1.0, 0.0).astype(BF16)
    source, target = source[:LANES], lax.broadcasted_iota(I32, (LANES, LANES), 1)
    used = (target < STEPS) | (target >= LANES - STEPS)
    same = (source < RIGHT) == (target < STEPS)
    hit = used & same & (source % RIGHT < species * GROUP) & (source % GROUP == (target + 8) % GROUP)
    patch_ref[...] = jnp.where(hit, 1.0, 0.0).astype(BF16)


def cone(retard, decay, cells, counts, raw, layers, width, species):
    wells = counts.shape[0]
    state = jax.ShapeDtypeStruct((STEPS, width, species, layers, LANES), F32)
    return pl.pallas_call(
        functools.partial(cone_kernel, layers=layers, width=width, species=species),
        out_shape=(
            jax.ShapeDtypeStruct((width, KINDS, layers, LANES), F32),
            state,
            state,
            state,
            jax.ShapeDtypeStruct((width, layers, LANES), F32),
            jax.ShapeDtypeStruct(((width + 2 * HALO) * layers, wells), BF16),
            jax.ShapeDtypeStruct((LANES, wells), BF16),
            jax.ShapeDtypeStruct((LANES, species * wells), BF16),
            jax.ShapeDtypeStruct((2 * LANES, 4 * LANES), BF16),
            jax.ShapeDtypeStruct((LANES, LANES), BF16),
            jax.ShapeDtypeStruct((2 * species + 2, LANES), F32),
            jax.ShapeDtypeStruct((TILE, wells), I32),
        ),
        in_specs=[HBM] * 4 + [VMEM] * 5,
        out_specs=[VMEM] * 12,
        scratch_shapes=[
            pltpu.SMEM(retard.shape, F32),
            pltpu.SMEM(decay.shape, F32),
            pltpu.VMEM(cells.shape, I32),
            pltpu.VMEM(counts.shape, I32),
            pltpu.SemaphoreType.DMA((4,)),
        ],
        compiler_params=pltpu.CompilerParams(vmem_limit_bytes=4 * MIB),
        cost_estimate=pl.CostEstimate(flops=10**7, bytes_accessed=10**7, transcendentals=0),
        name="cone_steps",
    )(*in_hbm(retard, decay, cells, counts), *raw)


def neighbour_row(r, a_ref, b_ref, width):
    even = lax.rem(lax.axis_index("gx"), 2) == 0
    from_a = even if r >= HALO else jnp.logical_not(even)
    index = r % (HALO + width)
    return [jnp.where(from_a, a_ref[index, f], b_ref[index, f]) for f in range(a_ref.shape[1])]


def edges_kernel(e_ref, xa_ref, xb_ref, all_ref, a_ref, b_ref, *, width):
    rows = width + 2 * HALO
    half = rows // 2
    even = lax.rem(lax.axis_index(Y), 2) == 0
    edges = {}
    for r in range(rows):
        inner = HALO <= r < HALO + width
        edges[r] = e_ref[r - HALO] if inner else pack_edges(neighbour_row(r, xa_ref, xb_ref, width))
        all_ref[r] = edges[r]
    near = lane_of(edges[0].shape) % GROUP < 8
    for r in range(half):
        one, two = edges[r], edges[r + half]
        to_right = jnp.where(near, one, roll(two, 8, 1))
        to_left = jnp.where(near, roll(two, -8, 1), one)
        a_ref[r] = jnp.where(even, to_right, to_left)
        b_ref[r] = jnp.where(even, to_left, to_right)


def outer_edges(r, a_ref, b_ref, near):
    half = a_ref.shape[0]
    even = lax.rem(lax.axis_index(Y), 2) == 0
    if r < half:
        return jnp.where(near == even, b_ref[r], a_ref[r])
    both = jnp.where(near == even, a_ref[r - half], b_ref[r - half])
    return jnp.where(near, roll(both, -8, 1), roll(both, 8, 1))


def all_edges(e, xa, xb):
    width, layers, _ = e.shape
    return pl.pallas_call(
        functools.partial(edges_kernel, width=width),
        out_shape=(
            jax.ShapeDtypeStruct((width + 2 * HALO, layers, LANES), F32),
            jax.ShapeDtypeStruct((width // 2 + HALO, layers, LANES), F32),
            jax.ShapeDtypeStruct((width // 2 + HALO, layers, LANES), F32),
        ),
        in_specs=[VMEM] * 3,
        out_specs=[VMEM] * 3,
        compiler_params=pltpu.CompilerParams(vmem_limit_bytes=1 * MIB),
        name="edge_columns",
    )(e, xa, xb)


def rim_kernel(
    rate_ref, xa_ref, xb_ref, coef_in, c_in, t_in, mask_ref, hot_ref,
    partial_ref, coef_out, c_out, jy_out, t_out, *, layers, width, species,
):
    gx = lax.axis_index("gx")
    rows = width + 2 * HALO
    coefs = (coef_in, coef_out)
    last = HALO + width - 1
    get = lambda kind, r: read_coef(coefs, kind, width, r)

    def put_coef(kind, r, value):
        which, index = coef_row(kind, width)(r)
        coefs[which][index, kind] = value

    speeds = {last: coef_in[width - 1, PX]}
    for r in list(range(HALO)) + list(range(HALO + width, rows)):
        fields = neighbour_row(r, xa_ref, xb_ref, width)
        k, kd, speeds[r], uy = fields[species:]
        index = state_row(0, width)(r)[1]
        for s in range(species):
            c_out[0, index, s] = fields[s]
        for kind, value in y_coefs(k, kd, uy).items():
            put_coef(kind, r, value)
    inside_low = jnp.where(gx > 0, 1.0, 0.0).astype(F32)
    inside_high = jnp.where(gx < lax.axis_size("gx") - 1, 1.0, 0.0).astype(F32)
    for r in list(range(HALO)) + list(range(last, rows - 1)):
        mask = inside_low if r < HALO else inside_high
        values = x_coefs(get(K, r), get(K, r + 1), get(KDIR, r), get(KDIR, r + 1), speeds[r], mask)
        for kind, value in zip((PX, QX, BX), values):
            put_coef(kind, r, value)
    for r in list(range(1, HALO + 1)) + list(range(last, rows - 1)):
        if r == HALO:
            value = coef_in[0, D] + get(QX, r - 1)
        elif r == last:
            value = coef_in[width - 1, D] + get(PX, r)
        else:
            value = get(PY, r) + get(QYM, r) + 2 * RATE + get(PX, r) + get(QX, r - 1)
        put_coef(D, r, value)

    for m in range(STEPS):
        coef = once(get)
        state = once(lambda r, s: read_state((c_in, c_out), m, width, r, s))
        tangent = once(lambda r, s: tangent_row(t_in, t_out, m, width, r)[s])
        for r in list(range(1 + m, HALO + 1 + m)) + list(range(last - m, rows - 1 - m)):
            index = state_row(m + 1, width)(r)[1]
            puts = put_at(c_out, m + 1, index), put_at(t_out, m, index), put_at(jy_out, m, index)
            for s in range(species):
                step_cell(r, m, s, rate_ref[s : s + 1, :], coef, state, tangent, *puts)

    masks = mask_ref[HALO * layers : (HALO + width) * layers, :]
    for s in range(species):
        block = [tangent_row(t_in, t_out, STEPS, width, r)[s] for r in range(HALO, HALO + width)]
        partial_ref[s : s + 1, :] = picked_sums(jnp.concatenate(block, axis=0), hot_ref[...], masks, layers)[0]


def tangent_row(t_in, t_out, m, width, r):
    which, index = state_row(m, width)(r)
    return (t_in, t_out)[which].at[m - 1, index]


def rim(rates, xa, xb, coef, c, t, mask, hot):
    _, width, species, layers, _ = c.shape
    wells = mask.shape[1]
    state = (STEPS, 2 * HALO, species, layers, LANES)
    return pl.pallas_call(
        functools.partial(rim_kernel, layers=layers, width=width, species=species),
        out_shape=(
            jax.ShapeDtypeStruct((species, wells), F32),
            jax.ShapeDtypeStruct((2 * HALO + 2, KINDS, layers, LANES), F32),
            jax.ShapeDtypeStruct(state, F32),
            jax.ShapeDtypeStruct(state, F32),
        ),
        in_specs=[VMEM] * 8,
        out_specs=[VMEM] * 4,
        scratch_shapes=[pltpu.VMEM(state, F32)],
        compiler_params=pltpu.CompilerParams(vmem_limit_bytes=6 * MIB),
        cost_estimate=pl.CostEstimate(flops=10**7, bytes_accessed=10**7, transcendentals=0),
        name="rim_steps",
    )(rates, xa, xb, coef, c, t, mask, hot)


def strips_kernel(
    rate_ref, e_ref, ea_ref, eb_ref, partial_in, mask_ref, hot_ref, spread_ref,
    partial_ref, coef_ref, c_ref, jy_ref, t_ref, *, layers, width, species,
):
    shape = (layers, LANES)
    rows = width + 2 * HALO
    lane = lane_of(shape)
    column = lane % GROUP
    near, left = column < 8, lane < RIGHT
    gx, gy = lax.axis_index("gx"), lax.axis_index(Y)
    first_y, last_y = gy == 0, gy == lax.axis_size(Y) - 1
    mask = jnp.where(
        left, jnp.where(first_y & near, 0.0, 1.0), jnp.where(last_y & (column >= 7), 0.0, 1.0)
    ).astype(F32)
    inside_low = jnp.where(gx > 0, 1.0, 0.0).astype(F32)
    inside_high = jnp.where(gx < lax.axis_size("gx") - 1, 1.0, 0.0).astype(F32)
    both = []
    for r in range(rows):
        own, outer = e_ref[r], outer_edges(r, ea_ref, eb_ref, near)
        left_strip, right_strip = jnp.where(near, outer, own), jnp.where(near, own, outer)
        c_ref[0, r] = jnp.where(left, left_strip, roll(right_strip, RIGHT, 1))
        both.append(jnp.concatenate([left_strip, right_strip], axis=1))
    fields = jnp.dot(
        pieces_of(jnp.concatenate(both, axis=0), 1),
        jnp.concatenate([spread_ref[...]] * 3, axis=0),
        preferred_element_type=F32,
    )

    kept = None
    for r in range(rows):
        k, kd, ux, uy = [fields[r * layers : (r + 1) * layers, f * LANES : (f + 1) * LANES] for f in range(4)]
        found = y_coefs(k, kd, uy, mask)
        for kind, value in found.items():
            coef_ref[r, kind] = value
        diagonal = found[PY] + found[QYM] + 2 * RATE
        if r:
            inside = inside_low if r <= HALO else inside_high if r >= HALO + width else None
            p, q, b = x_coefs(kept[0], k, kept[1], kd, kept[2], inside)
            coef_ref[r - 1, PX], coef_ref[r - 1, QX], coef_ref[r - 1, BX] = p, q, b
            coef_ref[r - 1, D] = kept[3] + p
            diagonal = diagonal + q
        kept = (k, kd, ux, diagonal)

    def put(ref, m, r):
        def store(s, value):
            ref[m, r] = value

        return store

    rate = rate_ref[species : species + 1, :]
    for m in range(STEPS):
        coef = once(lambda kind, r: coef_ref[r, kind])
        state = once(lambda r, s: c_ref[m, r])
        tangent = once(lambda r, s: t_ref[m - 1, r])
        for r in range(1 + m, rows - 1 - m):
            step_cell(r, m, 0, rate, coef, state, tangent, put(c_ref, m + 1, r), put(t_ref, m, r), put(jy_ref, m, r))

    masks = mask_ref[HALO * layers : (HALO + width) * layers, :]
    block = jnp.concatenate([t_ref[STEPS - 1, r] for r in range(HALO, HALO + width)], axis=0)
    for s, total in enumerate(picked_sums(block, hot_ref[...], masks, layers)):
        partial_ref[s : s + 1, :] = partial_in[s : s + 1, :] + total


def side_steps(rates, e, ea, eb, partial, mask, hot, spread):
    rows, layers, _ = e.shape
    species, wells = partial.shape
    state = (STEPS, rows, layers, LANES)
    return pl.pallas_call(
        functools.partial(strips_kernel, layers=layers, width=rows - 2 * HALO, species=species),
        out_shape=(
            jax.ShapeDtypeStruct((species, wells), F32),
            jax.ShapeDtypeStruct((rows, KINDS, layers, LANES), F32),
            jax.ShapeDtypeStruct(state, F32),
            jax.ShapeDtypeStruct(state, F32),
        ),
        in_specs=[VMEM] * 8,
        out_specs=[VMEM] * 4,
        scratch_shapes=[pltpu.VMEM(state, F32)],
        compiler_params=pltpu.CompilerParams(vmem_limit_bytes=6 * MIB),
        name="strip_steps",
    )(rates, e, ea, eb, partial, mask, hot, spread)


def adjoint_kernel(
    rate_ref, weight_ref, meta_ref, mask_ref, coef_in, coef_out, c_in, c_out, jy_in, jy_out,
    coef_side, c_side, jy_side, patch_ref, partial_ref, *rest, layers, width, species, parts,
):
    others, out_ref, lam_ref = rest[:parts], *rest[parts:]
    rows = width + 2 * HALO
    shape = (layers, LANES)
    lane = lane_of(shape)
    gx, gy = lax.axis_index("gx"), lax.axis_index(Y)
    where_y = meta_ref[3:4, :]
    counts = meta_ref[4:5, :].astype(F32)
    wells = meta_ref.shape[1]

    own, strip_species, strip_column = strip_columns(wells)
    strip_hit, own_hit = strip_column == where_y, own == where_y
    residuals = []
    for s in range(species):
        total = partial_ref[s : s + 1, :]
        for other in others:
            total = total + other[s : s + 1, :]
        factor = rate_ref[species + 1 + s, 0:1][:, None]
        residual = weight_ref[s : s + 1, :] * (total * factor) / counts
        residuals.append(residual / counts * factor)
    spreads = []
    for piece in range(3):
        coarse = [r.astype(BF16).astype(F32) for r in residuals]
        residuals = [r - q for r, q in zip(residuals, coarse)]
        blocks = [jnp.where(own_hit, q, 0.0).astype(BF16) for q in coarse]
        side = jnp.zeros((LANES, wells), F32)
        for s in range(species):
            side = jnp.where(strip_hit & (strip_species == s), coarse[s], side)
        spreads.append(jnp.concatenate(blocks + [side.astype(BF16)], axis=0))
    lam = lax.dot_general(
        jnp.concatenate([mask_ref[...]] * len(spreads), axis=1),
        jnp.concatenate(spreads, axis=1),
        (((1,), (1,)), ((), ())),
        preferred_element_type=F32,
    )
    for s in range(species + 1):
        lam_ref[0, :, s] = lam[:, s * LANES : (s + 1) * LANES].reshape(rows, layers, LANES)

    def main_coef(kind, r):
        return read_coef((coef_in, coef_out), kind, width, r)

    def side_coef(kind, r):
        return coef_side[r, kind]

    first_row, last_row = HALO - 1, HALO + width - 1
    sums = {}

    def add(key, term):
        sums[key] = sums[key] + term if key in sums else term

    rates = [rate_ref[s : s + 1, :] for s in range(species + 1)]
    for m in reversed(range(STEPS)):
        now = STEPS - 1 - m
        low, high = STEPS - m, rows - 1 - (STEPS - m)
        lam_row = once(lambda r, s: lam_ref[now, r, s])
        main, side = once(main_coef), once(side_coef)
        state = once(lambda r, s: c_side[m, r] if s == species else read_state((c_in, c_out), m, width, r, s))
        for r in range(min(low, first_row), max(high, last_row) + 1):
            sense, retreat = first_row <= r <= last_row, m > 0 and low <= r <= high
            results = []
            for s in range(species + 1):
                is_side = s == species
                coef = side if is_side else main
                value, up = lam_row(r, s), lam_row(r + 1, s)
                after = y_next(value)
                if sense:
                    add(("x", is_side, r), (state(r + 1, s) - state(r, s)) * (up - value))
                    if r >= HALO:
                        if is_side:
                            jump = jy_side[m, r]
                        else:
                            which, index = state_row(m + 1, width)(r)
                            jump = (jy_in, jy_out)[which][m, index, s]
                        add(("y", is_side, r), jump * (after - value))
                if retreat:
                    results.append(
                        (rates[s] - coef(D, r)) * value
                        + coef(PX, r) * up
                        + coef(QX, r - 1) * lam_row(r - 1, s)
                        + coef(PY, r) * after
                        + coef(QYM, r) * y_previous(value)
                        + RATE * z_pair(value)
                    )
            for s, result in enumerate(results):
                lam_ref[now + 1, r, s] = result

    column, left = lane % GROUP, lane < RIGHT
    first_y, last_y = gy == 0, gy == lax.axis_size(Y) - 1
    side_mask = jnp.where(
        left, jnp.where(first_y & (column < 8), 0.0, 1.0), jnp.where(last_y & (column >= 7), 0.0, 1.0)
    ).astype(F32)
    inside_low = jnp.where(gx > 0, 1.0, 0.0).astype(F32)
    inside_high = jnp.where(gx < lax.axis_size("gx") - 1, 1.0, 0.0).astype(F32)

    sides, results = [], []
    for is_side in (True, False):
        lower = None
        for r in range(HALO - 1, HALO + width):
            upper, along_y = sums["x", is_side, r], sums.get(("y", is_side, r))
            if r < HALO:
                lower = upper * inside_low
                continue
            if r == HALO + width - 1:
                upper = upper * inside_high
            if is_side:
                along_y = along_y * side_mask
            total = upper + lower + along_y + y_previous(along_y)
            lower = upper
            if is_side:
                sides.append(total)
                if len(sides) == width:
                    patch = jnp.dot(
                        pieces_of(jnp.concatenate(sides, axis=0), 1),
                        jnp.concatenate([patch_ref[...]] * 3, axis=0),
                        preferred_element_type=F32,
                    )
            else:
                x = r - HALO
                total = jnp.where(
                    (lane < STEPS) | (lane >= LANES - STEPS), patch[x * layers : (x + 1) * layers], total
                )
                results.append(-HALF_DT * main_coef(K, r) * total)
    for x, result in enumerate(results):
        out_ref[pl.ds(x, layers, stride=width), :] = result


def adjoint(rates, weight, meta, mask, inner, outer, side, patch, partials):
    (coef_in, c_in, jy_in), (coef_out, c_out, jy_out) = inner, outer
    _, width, species, layers, _ = c_in.shape
    parts = len(partials) - 1
    operands = (rates, weight, meta, mask, coef_in, coef_out, c_in, c_out, jy_in, jy_out, *side, patch, *partials)
    return pl.pallas_call(
        functools.partial(adjoint_kernel, layers=layers, width=width, species=species, parts=parts),
        out_shape=jax.ShapeDtypeStruct((layers * width, LANES), F32),
        in_specs=[VMEM] * len(operands),
        out_specs=VMEM,
        scratch_shapes=[pltpu.VMEM((STEPS, width + 2 * HALO, species + 1, layers, LANES), F32)],
        compiler_params=pltpu.CompilerParams(vmem_limit_bytes=12 * MIB),
        name="adjoint_steps",
    )(*operands)


def pairs(count, start):
    return [p for i in range(start, count - 1, 2) for p in ((i, i + 1), (i + 1, i))]


def swap_x(first, second):
    count, side = lax.axis_size("gx"), lax.axis_size(Y)
    partner = dict(pairs(count, 1))
    odd = [
        (i * side + j, partner[i] * side + j if i in partner else i * side + (j ^ 1))
        for i in range(count)
        for j in range(side)
    ]
    return lax.ppermute(first, "gx", pairs(count, 0)), lax.ppermute(second, ("gx",) + Y, odd)


def swap_y(first, second):
    count = lax.axis_size(Y)
    odd = pairs(count, 1) + [(0, count - 1), (count - 1, 0)]
    return lax.ppermute(first, Y, pairs(count, 0)), lax.ppermute(second, Y, odd)


def from_others(value, axis, reach):
    count = lax.axis_size(axis)
    if count in (2, 4):
        return [lax.ppermute(value, axis, [(i, i ^ d) for i in range(count)]) for d in range(1, count)]
    return [
        lax.ppermute(value, axis, [(i, i + d) for i in range(count) if 0 <= i + d < count])
        for distance in range(1, min(reach, count - 1) + 1)
        for d in (distance, -distance)
    ]


def shards(
    initial, logk, direction, face_speed, face_flags, retard, decay, screen_cells, screen_count, well_weight
):
    species, layers, width, columns = initial.shape
    raw, xa, xb = send_rows(initial, logk, direction, face_speed, face_flags)
    xa, xb = swap_x(xa, xb)
    coef_in, c_in, t_in, jy_in, e, mask, hot, side_hot, spread, patch, rates, meta = cone(
        retard, decay, screen_cells.T, screen_count, raw, layers, width, species
    )
    e, ea, eb = all_edges(e, xa, xb)
    ea, eb = swap_y(ea, eb)
    partial, coef_out, c_out, jy_out = rim(rates, xa, xb, coef_in, c_in, t_in, mask, hot)
    partial, *side = side_steps(rates, e, ea, eb, partial, mask, side_hot, spread)
    reach = -(-(screen_cells.shape[1] - 1 + HALO) // width)
    partials = [partial] + from_others(partial, "gx", reach)
    inner, outer = (coef_in, c_in, jy_in), (coef_out, c_out, jy_out)
    hessian = adjoint(rates, well_weight, meta, mask, inner, outer, side, patch, partials)
    return hessian.reshape(layers, width, columns)


def solution(mesh):
    in_specs = (
        P("grp", None, "gx", Y),
        P("grp", "gx", Y),
        P("grp", "gx", Y),
        P("grp", None, "gx", Y),
        P("grp", None, "gx", Y),
        P(),
        P(),
        P("grp", None),
        P("grp"),
        P("grp", None),
    )
    return jax.shard_map(shards, mesh=mesh, in_specs=in_specs, out_specs=P("grp", "gx", Y), check_vma=False)
```

```python
import functools

import jax
import jax.numpy as jnp
from jax import lax
from jax.experimental import pallas as pl
from jax.experimental.pallas import tpu as pltpu
from jax.sharding import PartitionSpec as P

STEPS = 4
HALO = STEPS
RATE = 0.02
HALF_DT = 0.025
LANES = 128
TILE = 8
GROUP = 16
RIGHT = 64
Y = ("gy", "sa")
MIB = 1024 * 1024
PX, QX, BX, PY, QYM, QY, PYM, BY, BYM, D, K, KDIR = range(12)
KINDS = 12
VMEM = pl.BlockSpec(memory_space=pltpu.VMEM)
HBM = pl.BlockSpec(memory_space=pltpu.HBM)
F32, BF16, I32 = jnp.float32, jnp.bfloat16, jnp.int32


def in_hbm(*arrays):
    return [pltpu.with_memory_space_constraint(a, pltpu.HBM) for a in arrays]


def lane_of(shape):
    return lax.broadcasted_iota(I32, shape, len(shape) - 1)


def roll(value, shift, axis):
    return pltpu.roll(value, shift % value.shape[axis], axis)


def y_next(value):
    return roll(value, LANES - 1, 1)


def y_previous(value):
    return roll(value, 1, 1)


def pack_edges(fields):
    lane = lane_of(fields[0].shape)
    packed = jnp.zeros_like(fields[0])
    for f, field in enumerate(fields):
        packed = jnp.where(lane // GROUP == f, roll(field, 8 + GROUP * f, 1), packed)
    return packed


def z_pair(value):
    tiles = [value[i : i + TILE] for i in range(0, value.shape[0], TILE)]
    row = lax.broadcasted_iota(I32, tiles[0].shape, 0)
    ups = [roll(t, TILE - 1, 0) for t in tiles]
    downs = [roll(t, 1, 0) for t in tiles]
    pairs = []
    for i, tile in enumerate(tiles):
        above = jnp.where(row == TILE - 1, ups[i + 1] if i + 1 < len(tiles) else tile, ups[i])
        below = jnp.where(row == 0, downs[i - 1] if i else tile, downs[i])
        pairs.append(above + below)
    return jnp.concatenate(pairs, axis=0)


def state_row(m, width):
    low, high = HALO + m, HALO + width - 1 - m

    def find(r):
        if low <= r <= high:
            return 0, r - HALO
        return (1, r - m) if r < low else (1, HALO + r - high - 1)

    return find


def coef_row(kind, width):
    low, high = HALO, HALO + width - 1
    if kind in (PX, QX, BX, D):
        high -= 1
    if kind == D:
        low += 1

    def find(r):
        if low <= r <= high:
            return 0, r - HALO
        return (1, r) if r <= HALO else (1, HALO + 1 + r - (HALO + width - 1))

    return find


def read_state(refs, m, width, r, s):
    which, index = state_row(m, width)(r)
    return refs[which][m, index, s]


def read_coef(refs, kind, width, r):
    which, index = coef_row(kind, width)(r)
    return refs[which][index, kind]


def row_fields(raw, x, layers, width, species, wanted=None):
    initial_ref, logk_ref, direction_ref, speed_ref, flags_ref = raw
    plane = layers * width

    def take(ref, index):
        return ref[pl.ds(index * plane + x, layers, stride=width), :]

    fields = []
    for f in range(species + 4) if wanted is None else wanted:
        if f < species:
            fields.append(take(initial_ref, f))
        elif f == species:
            fields.append(jnp.exp(take(logk_ref, 0)))
        elif f == species + 1:
            fields.append(jnp.exp(take(logk_ref, 0)) * take(direction_ref, 0))
        else:
            speed = take(speed_ref, f - species - 2)
            fields.append(jnp.where(take(flags_ref, f - species - 2) == 1, speed, -speed))
    return fields


def y_coefs(k, kd, u, mask=None):
    half = HALF_DT * (k + y_next(k))
    p = half + jnp.maximum(u, 0.0)
    q = half - jnp.minimum(u, 0.0)
    b = HALF_DT * (kd + y_next(kd))
    if mask is not None:
        p, q, b = p * mask, q * mask, b * mask
    return {PY: p, QY: q, BY: b, PYM: y_previous(p), QYM: y_previous(q), BYM: y_previous(b), K: k, KDIR: kd}


def x_coefs(k, k_next, kd, kd_next, u, mask=None):
    half = HALF_DT * (k + k_next)
    p = half + jnp.maximum(u, 0.0)
    q = half - jnp.minimum(u, 0.0)
    b = HALF_DT * (kd + kd_next)
    return (p, q, b) if mask is None else (p * mask, q * mask, b * mask)


def step_cell(r, m, s, rate, coef, state, tangent, put_c, put_t, put_jy, put_jx):
    kept = rate - coef(D, r)
    upper, lower = coef(QX, r), coef(PX, r - 1)
    after, before = coef(QY, r), coef(PYM, r)

    def moved(value, up, down, yp, ym):
        return kept * value + upper * up + lower * down + after * yp + before * ym + RATE * z_pair(value)

    c, up, down = state(r, s), state(r + 1, s), state(r - 1, s)
    yp, ym = y_next(c), y_previous(c)
    jump, jump_x = yp - c, up - c
    source = (
        coef(BX, r) * jump_x - coef(BX, r - 1) * (c - down) + coef(BY, r) * jump - coef(BYM, r) * (c - ym)
    )
    put_jy(s, jump)
    put_jx(s, jump_x)
    if m + 1 < STEPS:
        put_c(s, moved(c, up, down, yp, ym))
    if m > 0:
        t = tangent(r, s)
        source = source + moved(t, tangent(r + 1, s), tangent(r - 1, s), y_next(t), y_previous(t))
    put_t(s, source)


def pieces_of(value, axis):
    parts = []
    for _ in range(3):
        parts.append(value.astype(BF16))
        value = value - parts[-1].astype(F32)
    return jnp.concatenate(parts, axis=axis)


def once(load):
    return functools.cache(load)


def put_at(ref, m, index):
    def store(s, value):
        ref[m, index, s] = value

    return store


def picked_sums(wide, hot, masks, layers):
    picked = jnp.dot(pieces_of(wide, 1), jnp.concatenate([hot] * 3, axis=0), preferred_element_type=F32)
    wells = masks.shape[1]
    totals = []
    for s in range(hot.shape[1] // wells):
        total = jnp.zeros((layers, wells), F32)
        for i in range(0, wide.shape[0], layers):
            total = total + picked[i : i + layers, s * wells : (s + 1) * wells] * masks[i : i + layers].astype(F32)
        totals.append(jnp.sum(total, axis=0, keepdims=True))
    return totals


def send_kernel(*refs, layers, width, species):
    sources, raw, (xa_ref, xb_ref, sem) = refs[:5], refs[5:10], refs[10:]
    copies = [pltpu.make_async_copy(a, b, sem.at[i]) for i, (a, b) in enumerate(zip(sources, raw))]
    order = copies[1:] + copies[:1]
    for copy in order:
        copy.start()
    even = lax.rem(lax.axis_index("gx"), 2) == 0
    for waits, fields in ((order[:2], (species, species + 1)), (order[2:4], (species + 2, species + 3)), (order[4:], range(species))):
        for copy in waits:
            copy.wait()
        for r in range(HALO):
            bottom = row_fields(raw, r, layers, width, species, fields)
            top = row_fields(raw, width - HALO + r, layers, width, species, fields)
            for f, low, high in zip(fields, bottom, top):
                xa_ref[r, f] = jnp.where(even, high, low)
                xb_ref[r, f] = jnp.where(even, low, high)


def send_rows(initial, logk, direction, face_speed, face_flags):
    species, layers, width, _ = initial.shape
    sources = [a.reshape(-1, LANES) for a in (initial, logk, direction, face_speed, face_flags)]
    rows = jax.ShapeDtypeStruct((HALO, species + 4, layers, LANES), F32)
    *raw, xa, xb = pl.pallas_call(
        functools.partial(send_kernel, layers=layers, width=width, species=species),
        out_shape=tuple(jax.ShapeDtypeStruct(a.shape, a.dtype) for a in sources) + (rows, rows),
        in_specs=[HBM] * 5,
        out_specs=[VMEM] * 7,
        scratch_shapes=[pltpu.SemaphoreType.DMA((5,))],
        compiler_params=pltpu.CompilerParams(vmem_limit_bytes=3 * MIB),
        name="send_rows",
    )(*in_hbm(*sources))
    return raw, xa, xb


def divide(value, by):
    return lax.shift_right_logical(value, by.bit_length() - 1) if by & (by - 1) == 0 else lax.div(value, by)


def well_table(cells, counts, width):
    total_x, total_y = width * lax.axis_size("gx"), LANES * lax.axis_size(Y)
    start, second = cells[0:1], cells[1:2]
    depth = divide(start, total_x * total_y)
    rest = start - depth * (total_x * total_y)
    x = divide(rest, total_y)
    y = rest - x * total_y
    end = x + jnp.where(second > start, counts - 1, 1 - counts)
    row_start, col_start = lax.axis_index("gx") * width, lax.axis_index(Y) * LANES
    return [depth, jnp.minimum(x, end) - row_start, jnp.maximum(x, end) - row_start, y - col_start, counts]


def strip_columns(wells):
    own = lax.broadcasted_iota(I32, (LANES, wells), 0)
    return own, own % RIGHT // GROUP, own % GROUP + jnp.where(own < RIGHT, -8, 120)


def cone_kernel(
    retard_hbm, decay_hbm, cells_hbm, count_hbm, initial_ref, logk_ref, direction_ref, speed_ref, flags_ref,
    coef_ref, c_ref, t_ref, jy_ref, jx_ref, e_ref, mask_ref, hot_ref, side_hot_ref, spread_ref, patch_ref, rate_ref, meta_ref,
    retard_ref, decay_ref, cells_ref, count_ref, sem, *, layers, width, species,
):
    copies = [
        pltpu.make_async_copy(a, b, sem.at[i])
        for i, (a, b) in enumerate(
            ((retard_hbm, retard_ref), (decay_hbm, decay_ref), (cells_hbm, cells_ref), (count_hbm, count_ref))
        )
    ]
    for copy in copies:
        copy.start()
    raw = initial_ref, logk_ref, direction_ref, speed_ref, flags_ref
    kept = None
    for x in range(width):
        fields = row_fields(raw, x, layers, width, species)
        k, kd, ux, uy = fields[species:]
        e_ref[x] = pack_edges(fields)
        for s in range(species):
            c_ref[0, x, s] = fields[s]
        found = y_coefs(k, kd, uy)
        for kind, value in found.items():
            coef_ref[x, kind] = value
        diagonal = found[PY] + found[QYM] + 2 * RATE
        if x:
            p, q, b = x_coefs(kept[0], k, kept[1], kd, kept[2])
            coef_ref[x - 1, PX], coef_ref[x - 1, QX], coef_ref[x - 1, BX] = p, q, b
            coef_ref[x - 1, D] = kept[3] + p
            diagonal = diagonal + q
        kept = (k, kd, ux, diagonal)
    coef_ref[width - 1, D] = kept[3]
    coef_ref[width - 1, PX] = kept[2]

    for copy in copies:
        copy.wait()
    lane = lane_of((1, LANES))
    strips = jnp.full((1, LANES), retard_ref[species - 1], F32)
    rates = []
    for s in range(species):
        rate = jnp.full((1, LANES), retard_ref[s], F32)
        strips = jnp.where(lane % RIGHT // GROUP == s, rate, strips)
        factor = jnp.exp(jnp.full((1, LANES), -decay_ref[s], F32)) / rate
        rate_ref[s : s + 1, :] = rate
        rate_ref[species + 1 + s : species + 2 + s, :] = factor**STEPS
        rates.append(rate)
    rate_ref[species : species + 1, :] = strips

    for m in range(STEPS):
        coef = once(lambda kind, r: coef_ref[r - HALO, kind])
        state = once(lambda r, s: c_ref[m, r - HALO, s])
        tangent = once(lambda r, s: t_ref[m - 1, r - HALO, s])
        for r in range(HALO + 1 + m, HALO + width - 1 - m):
            x = r - HALO
            puts = put_at(c_ref, m + 1, x), put_at(t_ref, m, x), put_at(jy_ref, m, x), put_at(jx_ref, m, x)
            for s in range(species):
                step_cell(r, m, s, rates[s], coef, state, tangent, *puts)

    wells = meta_ref.shape[1]
    table = well_table(cells_ref, count_ref[...].reshape(1, wells), width)
    for i, row in enumerate(table):
        meta_ref[i : i + 1, :] = row
    depth, first, last, where_y = table[:4]
    in_layer = lax.broadcasted_iota(I32, (layers, wells), 0) == depth
    for r in range(width + 2 * HALO):
        inside = (first <= r - HALO) & (last >= r - HALO) & in_layer
        mask_ref[r * layers : (r + 1) * layers, :] = jnp.where(inside, 1.0, 0.0).astype(BF16)
    own, strip_species, strip_column = strip_columns(wells)
    hit = (own == where_y) & (own >= STEPS) & (own < LANES - STEPS)
    hot_ref[...] = jnp.where(hit, 1.0, 0.0).astype(BF16)
    reach = (strip_column < STEPS) & (strip_column >= -HALO)
    reach = reach | ((strip_column >= LANES - STEPS) & (strip_column < LANES + HALO))
    hit = reach & (strip_column == where_y)
    for s in range(species):
        side_hot_ref[:, s * wells : (s + 1) * wells] = jnp.where(hit & (strip_species == s), 1.0, 0.0).astype(BF16)


    source = lax.broadcasted_iota(I32, (2 * LANES, LANES), 0)
    target = lax.broadcasted_iota(I32, (2 * LANES, LANES), 1)
    target = jnp.where(target < RIGHT, 0, LANES) + target % GROUP
    for f in range(4):
        hit = source == target + (species + f) * GROUP
        spread_ref[:, f * LANES : (f + 1) * LANES] = jnp.where(hit, 1.0, 0.0).astype(BF16)
    source, target = source[:LANES], lax.broadcasted_iota(I32, (LANES, LANES), 1)
    used = (target < STEPS) | (target >= LANES - STEPS)
    same = (source < RIGHT) == (target < STEPS)
    hit = used & same & (source % RIGHT < species * GROUP) & (source % GROUP == (target + 8) % GROUP)
    patch_ref[...] = jnp.where(hit, 1.0, 0.0).astype(BF16)


def cone(retard, decay, cells, counts, raw, layers, width, species):
    wells = counts.shape[0]
    state = jax.ShapeDtypeStruct((STEPS, width, species, layers, LANES), F32)
    return pl.pallas_call(
        functools.partial(cone_kernel, layers=layers, width=width, species=species),
        out_shape=(
            jax.ShapeDtypeStruct((width, KINDS, layers, LANES), F32),
            state,
            state,
            state,
            state,
            jax.ShapeDtypeStruct((width, layers, LANES), F32),
            jax.ShapeDtypeStruct(((width + 2 * HALO) * layers, wells), BF16),
            jax.ShapeDtypeStruct((LANES, wells), BF16),
            jax.ShapeDtypeStruct((LANES, species * wells), BF16),
            jax.ShapeDtypeStruct((2 * LANES, 4 * LANES), BF16),
            jax.ShapeDtypeStruct((LANES, LANES), BF16),
            jax.ShapeDtypeStruct((2 * species + 2, LANES), F32),
            jax.ShapeDtypeStruct((TILE, wells), I32),
        ),
        in_specs=[HBM] * 4 + [VMEM] * 5,
        out_specs=[VMEM] * 13,
        scratch_shapes=[
            pltpu.SMEM(retard.shape, F32),
            pltpu.SMEM(decay.shape, F32),
            pltpu.VMEM(cells.shape, I32),
            pltpu.VMEM(counts.shape, I32),
            pltpu.SemaphoreType.DMA((4,)),
        ],
        compiler_params=pltpu.CompilerParams(vmem_limit_bytes=4 * MIB),
        cost_estimate=pl.CostEstimate(flops=10**7, bytes_accessed=10**7, transcendentals=0),
        name="cone_steps",
    )(*in_hbm(retard, decay, cells, counts), *raw)


def neighbour_row(r, a_ref, b_ref, width):
    even = lax.rem(lax.axis_index("gx"), 2) == 0
    from_a = even if r >= HALO else jnp.logical_not(even)
    index = r % (HALO + width)
    return [jnp.where(from_a, a_ref[index, f], b_ref[index, f]) for f in range(a_ref.shape[1])]


def edges_kernel(e_ref, xa_ref, xb_ref, all_ref, a_ref, b_ref, *, width):
    rows = width + 2 * HALO
    half = rows // 2
    even = lax.rem(lax.axis_index(Y), 2) == 0
    edges = {}
    for r in range(rows):
        inner = HALO <= r < HALO + width
        edges[r] = e_ref[r - HALO] if inner else pack_edges(neighbour_row(r, xa_ref, xb_ref, width))
        all_ref[r] = edges[r]
    near = lane_of(edges[0].shape) % GROUP < 8
    for r in range(half):
        one, two = edges[r], edges[r + half]
        to_right = jnp.where(near, one, roll(two, 8, 1))
        to_left = jnp.where(near, roll(two, -8, 1), one)
        a_ref[r] = jnp.where(even, to_right, to_left)
        b_ref[r] = jnp.where(even, to_left, to_right)


def outer_edges(r, a_ref, b_ref, near):
    half = a_ref.shape[0]
    even = lax.rem(lax.axis_index(Y), 2) == 0
    if r < half:
        return jnp.where(near == even, b_ref[r], a_ref[r])
    both = jnp.where(near == even, a_ref[r - half], b_ref[r - half])
    return jnp.where(near, roll(both, -8, 1), roll(both, 8, 1))


def all_edges(e, xa, xb):
    width, layers, _ = e.shape
    return pl.pallas_call(
        functools.partial(edges_kernel, width=width),
        out_shape=(
            jax.ShapeDtypeStruct((width + 2 * HALO, layers, LANES), F32),
            jax.ShapeDtypeStruct((width // 2 + HALO, layers, LANES), F32),
            jax.ShapeDtypeStruct((width // 2 + HALO, layers, LANES), F32),
        ),
        in_specs=[VMEM] * 3,
        out_specs=[VMEM] * 3,
        compiler_params=pltpu.CompilerParams(vmem_limit_bytes=1 * MIB),
        name="edge_columns",
    )(e, xa, xb)


def rim_kernel(
    rate_ref, xa_ref, xb_ref, coef_in, c_in, t_in, mask_ref, hot_ref,
    partial_ref, coef_out, c_out, jy_out, jx_out, t_out, *, layers, width, species,
):
    gx = lax.axis_index("gx")
    rows = width + 2 * HALO
    coefs = (coef_in, coef_out)
    last = HALO + width - 1
    get = lambda kind, r: read_coef(coefs, kind, width, r)

    def put_coef(kind, r, value):
        which, index = coef_row(kind, width)(r)
        coefs[which][index, kind] = value

    speeds = {last: coef_in[width - 1, PX]}
    for r in list(range(HALO)) + list(range(HALO + width, rows)):
        fields = neighbour_row(r, xa_ref, xb_ref, width)
        k, kd, speeds[r], uy = fields[species:]
        index = state_row(0, width)(r)[1]
        for s in range(species):
            c_out[0, index, s] = fields[s]
        for kind, value in y_coefs(k, kd, uy).items():
            put_coef(kind, r, value)
    inside_low = jnp.where(gx > 0, 1.0, 0.0).astype(F32)
    inside_high = jnp.where(gx < lax.axis_size("gx") - 1, 1.0, 0.0).astype(F32)
    for r in list(range(HALO)) + list(range(last, rows - 1)):
        mask = inside_low if r < HALO else inside_high
        values = x_coefs(get(K, r), get(K, r + 1), get(KDIR, r), get(KDIR, r + 1), speeds[r], mask)
        for kind, value in zip((PX, QX, BX), values):
            put_coef(kind, r, value)
    for r in list(range(1, HALO + 1)) + list(range(last, rows - 1)):
        if r == HALO:
            value = coef_in[0, D] + get(QX, r - 1)
        elif r == last:
            value = coef_in[width - 1, D] + get(PX, r)
        else:
            value = get(PY, r) + get(QYM, r) + 2 * RATE + get(PX, r) + get(QX, r - 1)
        put_coef(D, r, value)

    for m in range(STEPS):
        coef = once(get)
        state = once(lambda r, s: read_state((c_in, c_out), m, width, r, s))
        tangent = once(lambda r, s: tangent_row(t_in, t_out, m, width, r)[s])
        for r in list(range(1 + m, HALO + 1 + m)) + list(range(last - m, rows - 1 - m)):
            index = state_row(m + 1, width)(r)[1]
            puts = [put_at(ref, n, index) for ref, n in ((c_out, m + 1), (t_out, m), (jy_out, m), (jx_out, m))]
            for s in range(species):
                step_cell(r, m, s, rate_ref[s : s + 1, :], coef, state, tangent, *puts)

    masks = mask_ref[HALO * layers : (HALO + width) * layers, :]
    for s in range(species):
        block = [tangent_row(t_in, t_out, STEPS, width, r)[s] for r in range(HALO, HALO + width)]
        partial_ref[s : s + 1, :] = picked_sums(jnp.concatenate(block, axis=0), hot_ref[...], masks, layers)[0]


def tangent_row(t_in, t_out, m, width, r):
    which, index = state_row(m, width)(r)
    return (t_in, t_out)[which].at[m - 1, index]


def rim(rates, xa, xb, coef, c, t, mask, hot):
    _, width, species, layers, _ = c.shape
    wells = mask.shape[1]
    state = (STEPS, 2 * HALO, species, layers, LANES)
    return pl.pallas_call(
        functools.partial(rim_kernel, layers=layers, width=width, species=species),
        out_shape=(
            jax.ShapeDtypeStruct((species, wells), F32),
            jax.ShapeDtypeStruct((2 * HALO + 2, KINDS, layers, LANES), F32),
            jax.ShapeDtypeStruct(state, F32),
            jax.ShapeDtypeStruct(state, F32),
            jax.ShapeDtypeStruct(state, F32),
        ),
        in_specs=[VMEM] * 8,
        out_specs=[VMEM] * 5,
        scratch_shapes=[pltpu.VMEM(state, F32)],
        compiler_params=pltpu.CompilerParams(vmem_limit_bytes=6 * MIB),
        cost_estimate=pl.CostEstimate(flops=10**7, bytes_accessed=10**7, transcendentals=0),
        name="rim_steps",
    )(rates, xa, xb, coef, c, t, mask, hot)


def strips_kernel(
    rate_ref, e_ref, ea_ref, eb_ref, partial_in, mask_ref, hot_ref, spread_ref,
    partial_ref, coef_ref, c_ref, jy_ref, jx_ref, t_ref, *, layers, width, species,
):
    shape = (layers, LANES)
    rows = width + 2 * HALO
    lane = lane_of(shape)
    column = lane % GROUP
    near, left = column < 8, lane < RIGHT
    gx, gy = lax.axis_index("gx"), lax.axis_index(Y)
    first_y, last_y = gy == 0, gy == lax.axis_size(Y) - 1
    mask = jnp.where(
        left, jnp.where(first_y & near, 0.0, 1.0), jnp.where(last_y & (column >= 7), 0.0, 1.0)
    ).astype(F32)
    inside_low = jnp.where(gx > 0, 1.0, 0.0).astype(F32)
    inside_high = jnp.where(gx < lax.axis_size("gx") - 1, 1.0, 0.0).astype(F32)
    both = []
    for r in range(rows):
        own, outer = e_ref[r], outer_edges(r, ea_ref, eb_ref, near)
        left_strip, right_strip = jnp.where(near, outer, own), jnp.where(near, own, outer)
        c_ref[0, r] = jnp.where(left, left_strip, roll(right_strip, RIGHT, 1))
        both.append(jnp.concatenate([left_strip, right_strip], axis=1))
    fields = jnp.dot(
        pieces_of(jnp.concatenate(both, axis=0), 1),
        jnp.concatenate([spread_ref[...]] * 3, axis=0),
        preferred_element_type=F32,
    )

    kept = None
    for r in range(rows):
        k, kd, ux, uy = [fields[r * layers : (r + 1) * layers, f * LANES : (f + 1) * LANES] for f in range(4)]
        found = y_coefs(k, kd, uy, mask)
        for kind, value in found.items():
            coef_ref[r, kind] = value
        diagonal = found[PY] + found[QYM] + 2 * RATE
        if r:
            inside = inside_low if r <= HALO else inside_high if r >= HALO + width else None
            p, q, b = x_coefs(kept[0], k, kept[1], kd, kept[2], inside)
            coef_ref[r - 1, PX], coef_ref[r - 1, QX], coef_ref[r - 1, BX] = p, q, b
            coef_ref[r - 1, D] = kept[3] + p
            diagonal = diagonal + q
        kept = (k, kd, ux, diagonal)

    def put(ref, m, r):
        def store(s, value):
            ref[m, r] = value

        return store

    rate = rate_ref[species : species + 1, :]
    for m in range(STEPS):
        coef = once(lambda kind, r: coef_ref[r, kind])
        state = once(lambda r, s: c_ref[m, r])
        tangent = once(lambda r, s: t_ref[m - 1, r])
        for r in range(1 + m, rows - 1 - m):
            puts = put(c_ref, m + 1, r), put(t_ref, m, r), put(jy_ref, m, r), put(jx_ref, m, r)
            step_cell(r, m, 0, rate, coef, state, tangent, *puts)

    masks = mask_ref[HALO * layers : (HALO + width) * layers, :]
    block = jnp.concatenate([t_ref[STEPS - 1, r] for r in range(HALO, HALO + width)], axis=0)
    for s, total in enumerate(picked_sums(block, hot_ref[...], masks, layers)):
        partial_ref[s : s + 1, :] = partial_in[s : s + 1, :] + total


def side_steps(rates, e, ea, eb, partial, mask, hot, spread):
    rows, layers, _ = e.shape
    species, wells = partial.shape
    state = (STEPS, rows, layers, LANES)
    return pl.pallas_call(
        functools.partial(strips_kernel, layers=layers, width=rows - 2 * HALO, species=species),
        out_shape=(
            jax.ShapeDtypeStruct((species, wells), F32),
            jax.ShapeDtypeStruct((rows, KINDS, layers, LANES), F32),
            jax.ShapeDtypeStruct(state, F32),
            jax.ShapeDtypeStruct(state, F32),
            jax.ShapeDtypeStruct(state, F32),
        ),
        in_specs=[VMEM] * 8,
        out_specs=[VMEM] * 5,
        scratch_shapes=[pltpu.VMEM(state, F32)],
        compiler_params=pltpu.CompilerParams(vmem_limit_bytes=6 * MIB),
        name="strip_steps",
    )(rates, e, ea, eb, partial, mask, hot, spread)


def adjoint_kernel(
    rate_ref, weight_ref, meta_ref, mask_ref, coef_in, coef_out, c_in, c_out, jy_in, jy_out, jx_in, jx_out,
    coef_side, c_side, jy_side, jx_side, patch_ref, partial_ref, *rest, layers, width, species, parts,
):
    others, out_ref, lam_ref = rest[:parts], *rest[parts:]
    rows = width + 2 * HALO
    shape = (layers, LANES)
    lane = lane_of(shape)
    gx, gy = lax.axis_index("gx"), lax.axis_index(Y)
    where_y = meta_ref[3:4, :]
    counts = meta_ref[4:5, :].astype(F32)
    wells = meta_ref.shape[1]

    own, strip_species, strip_column = strip_columns(wells)
    strip_hit, own_hit = strip_column == where_y, own == where_y
    residuals = []
    for s in range(species):
        total = partial_ref[s : s + 1, :]
        for other in others:
            total = total + other[s : s + 1, :]
        factor = rate_ref[species + 1 + s, 0:1][:, None]
        residual = weight_ref[s : s + 1, :] * (total * factor) / counts
        residuals.append(residual / counts * factor)
    spreads = []
    for piece in range(3):
        coarse = [r.astype(BF16).astype(F32) for r in residuals]
        residuals = [r - q for r, q in zip(residuals, coarse)]
        blocks = [jnp.where(own_hit, q, 0.0).astype(BF16) for q in coarse]
        side = jnp.zeros((LANES, wells), F32)
        for s in range(species):
            side = jnp.where(strip_hit & (strip_species == s), coarse[s], side)
        spreads.append(jnp.concatenate(blocks + [side.astype(BF16)], axis=0))
    lam = lax.dot_general(
        jnp.concatenate([mask_ref[...]] * len(spreads), axis=1),
        jnp.concatenate(spreads, axis=1),
        (((1,), (1,)), ((), ())),
        preferred_element_type=F32,
    )
    for s in range(species + 1):
        lam_ref[0, :, s] = lam[:, s * LANES : (s + 1) * LANES].reshape(rows, layers, LANES)

    def main_coef(kind, r):
        return read_coef((coef_in, coef_out), kind, width, r)

    def side_coef(kind, r):
        return coef_side[r, kind]

    first_row, last_row = HALO - 1, HALO + width - 1
    sums = {}

    def add(key, term):
        sums[key] = sums[key] + term if key in sums else term

    rates = [rate_ref[s : s + 1, :] for s in range(species + 1)]
    for m in reversed(range(STEPS)):
        now = STEPS - 1 - m
        low, high = STEPS - m, rows - 1 - (STEPS - m)
        lam_row = once(lambda r, s: lam_ref[now, r, s])
        main, side = once(main_coef), once(side_coef)
        state = once(lambda r, s: c_side[m, r] if s == species else read_state((c_in, c_out), m, width, r, s))
        for r in range(min(low, first_row), max(high, last_row) + 1):
            sense, retreat = first_row <= r <= last_row, m > 0 and low <= r <= high
            results = []
            for s in range(species + 1):
                is_side = s == species
                coef = side if is_side else main
                value, up = lam_row(r, s), lam_row(r + 1, s)
                after = y_next(value)
                if sense:
                    which, index = state_row(m + 1, width)(r)
                    if r <= m:
                        jump = state(r + 1, s) - state(r, s)
                    else:
                        jump = jx_side[m, r] if is_side else (jx_in, jx_out)[which][m, index, s]
                    add(("x", is_side, r), jump * (up - value))
                    if r >= HALO:
                        jump = jy_side[m, r] if is_side else (jy_in, jy_out)[which][m, index, s]
                        add(("y", is_side, r), jump * (after - value))
                if retreat:
                    results.append(
                        (rates[s] - coef(D, r)) * value
                        + coef(PX, r) * up
                        + coef(QX, r - 1) * lam_row(r - 1, s)
                        + coef(PY, r) * after
                        + coef(QYM, r) * y_previous(value)
                        + RATE * z_pair(value)
                    )
            for s, result in enumerate(results):
                lam_ref[now + 1, r, s] = result

    column, left = lane % GROUP, lane < RIGHT
    first_y, last_y = gy == 0, gy == lax.axis_size(Y) - 1
    side_mask = jnp.where(
        left, jnp.where(first_y & (column < 8), 0.0, 1.0), jnp.where(last_y & (column >= 7), 0.0, 1.0)
    ).astype(F32)
    inside_low = jnp.where(gx > 0, 1.0, 0.0).astype(F32)
    inside_high = jnp.where(gx < lax.axis_size("gx") - 1, 1.0, 0.0).astype(F32)

    sides, results = [], []
    for is_side in (True, False):
        lower = None
        for r in range(HALO - 1, HALO + width):
            upper, along_y = sums["x", is_side, r], sums.get(("y", is_side, r))
            if r < HALO:
                lower = upper * inside_low
                continue
            if r == HALO + width - 1:
                upper = upper * inside_high
            if is_side:
                along_y = along_y * side_mask
            total = upper + lower + along_y + y_previous(along_y)
            lower = upper
            if is_side:
                sides.append(total)
                if len(sides) == width:
                    patch = jnp.dot(
                        pieces_of(jnp.concatenate(sides, axis=0), 1),
                        jnp.concatenate([patch_ref[...]] * 3, axis=0),
                        preferred_element_type=F32,
                    )
            else:
                x = r - HALO
                total = jnp.where(
                    (lane < STEPS) | (lane >= LANES - STEPS), patch[x * layers : (x + 1) * layers], total
                )
                results.append(-HALF_DT * main_coef(K, r) * total)
    for x, result in enumerate(results):
        out_ref[pl.ds(x, layers, stride=width), :] = result


def adjoint(rates, weight, meta, mask, inner, outer, side, patch, partials):
    (coef_in, c_in, jy_in, jx_in), (coef_out, c_out, jy_out, jx_out) = inner, outer
    _, width, species, layers, _ = c_in.shape
    parts = len(partials) - 1
    operands = (rates, weight, meta, mask, coef_in, coef_out, c_in, c_out, jy_in, jy_out, jx_in, jx_out, *side, patch, *partials)
    return pl.pallas_call(
        functools.partial(adjoint_kernel, layers=layers, width=width, species=species, parts=parts),
        out_shape=jax.ShapeDtypeStruct((layers * width, LANES), F32),
        in_specs=[VMEM] * len(operands),
        out_specs=VMEM,
        scratch_shapes=[pltpu.VMEM((STEPS, width + 2 * HALO, species + 1, layers, LANES), F32)],
        compiler_params=pltpu.CompilerParams(vmem_limit_bytes=12 * MIB),
        name="adjoint_steps",
    )(*operands)


def pairs(count, start):
    return [p for i in range(start, count - 1, 2) for p in ((i, i + 1), (i + 1, i))]


def swap_x(first, second):
    count, side = lax.axis_size("gx"), lax.axis_size(Y)
    partner = dict(pairs(count, 1))
    odd = [
        (i * side + j, partner[i] * side + j if i in partner else i * side + (j ^ 1))
        for i in range(count)
        for j in range(side)
    ]
    return lax.ppermute(first, "gx", pairs(count, 0)), lax.ppermute(second, ("gx",) + Y, odd)


def swap_y(first, second):
    count = lax.axis_size(Y)
    odd = pairs(count, 1) + [(0, count - 1), (count - 1, 0)]
    return lax.ppermute(first, Y, pairs(count, 0)), lax.ppermute(second, Y, odd)


def from_others(value, axis, reach):
    count = lax.axis_size(axis)
    if count in (2, 4):
        return [lax.ppermute(value, axis, [(i, i ^ d) for i in range(count)]) for d in range(1, count)]
    return [
        lax.ppermute(value, axis, [(i, i + d) for i in range(count) if 0 <= i + d < count])
        for distance in range(1, min(reach, count - 1) + 1)
        for d in (distance, -distance)
    ]


def shards(
    initial, logk, direction, face_speed, face_flags, retard, decay, screen_cells, screen_count, well_weight
):
    species, layers, width, columns = initial.shape
    raw, xa, xb = send_rows(initial, logk, direction, face_speed, face_flags)
    xa, xb = swap_x(xa, xb)
    coef_in, c_in, t_in, jy_in, jx_in, e, mask, hot, side_hot, spread, patch, rates, meta = cone(
        retard, decay, screen_cells.T, screen_count, raw, layers, width, species
    )
    e, ea, eb = all_edges(e, xa, xb)
    ea, eb = swap_y(ea, eb)
    partial, coef_out, c_out, jy_out, jx_out = rim(rates, xa, xb, coef_in, c_in, t_in, mask, hot)
    partial, *side = side_steps(rates, e, ea, eb, partial, mask, side_hot, spread)
    reach = -(-(screen_cells.shape[1] - 1 + HALO) // width)
    partials = [partial] + from_others(partial, "gx", reach)
    inner, outer = (coef_in, c_in, jy_in, jx_in), (coef_out, c_out, jy_out, jx_out)
    hessian = adjoint(rates, well_weight, meta, mask, inner, outer, side, patch, partials)
    return hessian.reshape(layers, width, columns)


def solution(mesh):
    in_specs = (
        P("grp", None, "gx", Y),
        P("grp", "gx", Y),
        P("grp", "gx", Y),
        P("grp", None, "gx", Y),
        P("grp", None, "gx", Y),
        P(),
        P(),
        P("grp", None),
        P("grp"),
        P("grp", None),
    )
    return jax.shard_map(shards, mesh=mesh, in_specs=in_specs, out_specs=P("grp", "gx", Y), check_vma=False)
```
